32 devices in a mesh: rep: 8 (over z, core), shard: 4 (over y, x).
Axes of the slice: x: 2, y: 2, z: 4, core: 2. Of those that a mesh axis runs over, the one named last changes fastest.
Arguments:
- tokens: bfloat16 [12288, 1024], P(('rep', 'shard')), may hold values from -6 to 6
- d_out: bfloat16 [12288, 1024], P(('rep', 'shard')), may hold values from -6 to 6
- routes: int32 [12288, 8], P(('rep', 'shard')), may hold values from 0 to 15, all different within a row; in each aligned block of 384 rows (0 to 383, 384 to 767, ...) at most 240 rows name the same one
- gates: float32 [12288, 8], P(('rep', 'shard')), may hold values from 0.25 to 1
- segment: int32 [8, 512], P('rep'), may hold values from 0 to 2, never falling along the last dimension, each value on 1 to 256 neighbouring positions
- gain_attn: bfloat16 [1024], P('shard'), may hold values from 0.099609375 to 1.8984375
- w_query: bfloat16 [1024, 1024], P('shard'), may hold values from -0.25 to 0.25
- key_weight: bfloat16 [1024, 512], P('shard'), may hold values from -0.25 to 0.25
- value_weight: bfloat16 [1024, 512], P('shard'), may hold values from -0.1875 to 0.1875
- w_out: bfloat16 [1024, 1024], P('shard'), may hold values from -0.75 to 0.75
- gain_ffn: bfloat16 [1024], P('shard'), may hold values from 0.099609375 to 1.8984375
- w_gate: bfloat16 [16, 1024, 512], P('shard'), may hold values from -0.1875 to 0.1875
- w_up: bfloat16 [16, 1024, 512], P('shard'), may hold values from -0.1875 to 0.1875
- w_down: bfloat16 [16, 512, 1024], P('shard'), may hold values from -0.5 to 0.5
Outputs:
- mixed: bfloat16 [12288, 1024], P(('rep', 'shard'))
- d_tokens: float32 [12288, 1024], P(('rep', 'shard'))
- grad_gain_attn: float32 [1024], P('shard')
- grad_w_query: float32 [1024, 1024], P('shard')
- grad_w_key: float32 [1024, 512], P('shard')
- grad_w_value: float32 [1024, 512], P('shard')
- grad_w_out: float32 [1024, 1024], P('shard')
- grad_gain_ffn: float32 [1024], P('shard')
- grad_w_gate: float32 [16, 1024, 512], P('shard')
- grad_w_up: float32 [16, 1024, 512], P('shard')
- grad_w_down: float32 [16, 512, 1024], P('shard')
The draws below stay inside these ranges and needn't reach their ends.
Inputs may be any that keep to these rules, and one draw needn't show every extreme that they name: `routes`: a token's 8 experts differ; among the 384 rows of one device no expert is named more than 240 times. `segment`: each group's row never falls and numbers its continuations from 0 in order; each continuation has 1 to 256 tokens, one exactly 256.
All inputs are finite; a program needn't handle non-finite values.
Results may differ from the reference program's by a relative error of at most 0.025.
Values may be sent and summed in bfloat16 or wider, within the bound.
No kernel may reach another device: no remote copies, remote signals or barrier semaphores. Data moves between devices by JAX's collectives and lax.ppermute only.
A program may use at most 256 MiB of HBM per device.

```python
import math
import jax
import jax.numpy as jnp
import numpy as np
from jax import lax

MODEL_WIDTH = 1024
QUERY_HEADS = 16
KEY_VALUE_HEADS = 8
HEAD_SIZE = 64
FF = 512
TOPK = 8
EXPERTS = 16
PROMPT = 1024
CLEN = 256
TOK_DEV = 384
CONT_TOK = 512
CONTS = 3
GROUPS = 8
GROUP_TOKENS = 1536
TOKENS = 12288
CAP = 240
N_SHARD = 4


def level_of(own_key, extent, shards, low, high):
    def one(axis_at, blocks):
        draws = jax.random.uniform(jax.random.fold_in(jax.random.fold_in(own_key, 6), axis_at), (blocks,), jnp.float32, low / len(shards), high / len(shards))
        return jnp.repeat(jnp.exp(draws), extent[axis_at] // blocks).reshape((-1,) + (1,) * (len(extent) - axis_at - 1))

    gain = one(*shards[0])
    for cut in shards[1:]:
        gain = gain * one(*cut)
    return gain


def profile(number_of, total, most, slope):
    weights = [(1 << 20) // math.isqrt(rank ** slope) + 1 for rank in range(2, number_of + 1)]
    rest, counts = total - most - (number_of - 1), [1] * (number_of - 1)
    while rest > 0:
        free = [i for i in range(number_of - 1) if counts[i] < most]
        whole, budget = sum([weights[i] for i in free]), rest
        for i in free:
            addition = min(most - counts[i], max(1, budget * weights[i] // whole), rest)
            counts[i] = counts[i] + addition
            rest = rest - addition
    return np.array([most] + counts)


def uneven(rng, number_of, total, reach, lean):
    if number_of == 2:
        one = jax.random.randint(rng, (), max(1, total - reach), min(reach, total - 1) + 1)
        return jnp.stack([one, total - one])
    lengths = jnp.asarray(profile(number_of, total, reach, lean), jnp.int32)
    twos = (number_of - 1) // 2
    source_of, taker = lengths[1:1 + 2 * twos:2], lengths[2:2 + 2 * twos:2]
    room = jnp.minimum(source_of - 1, reach - taker)
    shifted = jax.random.randint(jax.random.fold_in(rng, 1), (twos,), 0, 1 << 20) % (room + 1)
    lengths = lengths.at[1:1 + 2 * twos:2].set(source_of - shifted).at[2:2 + 2 * twos:2].set(taker + shifted)
    return lengths[jax.random.permutation(jax.random.fold_in(rng, 2), number_of)]


def deal_out(key, own, number, rows, amount, top, limit, skew):
    sequence = jax.random.permutation(key, amount)
    crowded, usual = portions_of(amount, rows * top, limit, skew, True), portions_of(amount, rows * top, limit, skew, False)
    places = jnp.arange(amount)

    def named(tallies, rotation):
        used = int((tallies > 0).sum())
        fixed = max(1, used // 4)
        moved = fixed + (places - fixed + rotation * (used - fixed)) % max(1, amount - fixed)
        return jnp.zeros((amount,), jnp.int32).at[sequence[jnp.where(places < fixed, places, moved)]].set(jnp.asarray(tallies, jnp.int32))

    tallies = jnp.where(number % 4 == 0, named(crowded, number // 4), named(usual, number - number // 4 - 1))
    mixed = jax.random.permutation(jax.random.fold_in(own, 3), amount)
    donor, sink = mixed[0:amount // 2 * 2:2], mixed[1:amount // 2 * 2:2]
    slack = jnp.minimum(tallies[donor] - 1, limit - tallies[sink]) // 2
    slack = jnp.where((donor == sequence[0]) | (sink == sequence[0]) | (tallies[sink] == 0), 0, jnp.maximum(slack, 0))
    moved = jax.random.randint(jax.random.fold_in(own, 4), (amount // 2,), 0, 1 << 20) % (slack + 1)
    tallies = tallies.at[donor].add(-moved).at[sink].add(moved)
    labels = jnp.searchsorted(jnp.cumsum(tallies), jnp.arange(rows * top), side="right").astype(jnp.int32)
    grid = labels.reshape(top, rows).T
    grid = grid[jax.random.permutation(jax.random.fold_in(own, 1), rows)]
    rotation = jax.random.randint(jax.random.fold_in(own, 2), (rows, 1), 0, top)
    return jnp.take_along_axis(grid, (jnp.arange(top)[None, :] + rotation) % top, axis=1)


def portions_of(number_of, total, bound, slope, full):
    weights = [(1 << 20) // math.isqrt(grade ** slope) + 1 for grade in range(1, number_of + 1)]
    largest = bound if full else min(bound, max(-(-total // number_of), total * weights[0] // sum(weights)))
    least = 1 if total - largest >= number_of - 1 else 0
    given, spare = [largest] + [least] * (number_of - 1), total - largest - least * (number_of - 1)
    while spare > 0:
        candidates = [i for i in range(1, number_of) if given[i] < largest] or [i for i in range(1, number_of) if given[i] < bound]
        pool, budget = sum([weights[i] for i in candidates]), spare
        for i in candidates:
            addition = min(bound - given[i], max(1, budget * weights[i] // pool), spare)
            given[i] = given[i] + addition
            spare = spare - addition
    return np.array(given)


def noise(rng, extent, spread, limit, cuts=(), held_as=jnp.bfloat16):
    level = level_of(rng, extent, cuts, -0.22, 0.18) if cuts else 1.0
    drawn = jax.random.normal(rng, extent, jnp.float32) * spread * level
    return jnp.minimum(jnp.maximum(drawn, -limit), limit).astype(held_as)


def setup_inputs(seed: int = 0) -> dict:
    streams_of = jax.random.split(jax.random.key(seed), 15)
    tokens = noise(streams_of[0], (TOKENS, MODEL_WIDTH), 1.0, 6.0, ((0, 32),))
    d_out = noise(streams_of[1], (TOKENS, MODEL_WIDTH), 1.0, 6.0, ((0, 32),))
    routes_keys = jax.random.split(jax.random.fold_in(streams_of[2], 1), TOKENS // TOK_DEV)
    routes_turns = jax.random.permutation(jax.random.fold_in(streams_of[2], 3), TOKENS // TOK_DEV)
    routes = jax.vmap(lambda own, number: deal_out(jax.random.fold_in(streams_of[2], 2), own, number, TOK_DEV, EXPERTS, TOPK, CAP, 1))(routes_keys, routes_turns).reshape((TOKENS, TOPK))
    gates = jnp.clip(jnp.exp(math.log(1.0) - 1.3862944 * jax.random.uniform(streams_of[3], (TOKENS, TOPK), jnp.float32) ** level_of(streams_of[3], (TOKENS, TOPK), ((0, 32),), -0.2, 0.2)), 0.25, 1.0)
    segment = jax.vmap(lambda own: jnp.searchsorted(jnp.cumsum(uneven(own, CONTS, CONT_TOK, CLEN, 1)), jnp.arange(CONT_TOK), side="right"))(jax.random.split(streams_of[4], GROUPS)).reshape((GROUPS, CONT_TOK)).astype(jnp.int32)
    gain_attn = jnp.clip(1.0 + 0.18 * jax.random.normal(streams_of[5], (MODEL_WIDTH,), jnp.float32), 0.099609375, 1.8984375).astype(jnp.bfloat16)
    w_query = noise(streams_of[6], (MODEL_WIDTH, QUERY_HEADS * HEAD_SIZE), (MODEL_WIDTH // 2) ** -0.5, 0.25, ((0, 4),))
    key_weight = noise(streams_of[7], (MODEL_WIDTH, KEY_VALUE_HEADS * HEAD_SIZE), (MODEL_WIDTH // 2) ** -0.5, 0.25, ((0, 4),))
    value_weight = noise(streams_of[8], (MODEL_WIDTH, KEY_VALUE_HEADS * HEAD_SIZE), MODEL_WIDTH ** -0.5, 0.1875, ((0, 4),))
    w_out = noise(streams_of[9], (QUERY_HEADS * HEAD_SIZE, MODEL_WIDTH), (QUERY_HEADS * HEAD_SIZE // 16) ** -0.5, 0.75, ((0, 4),))
    gain_ffn = jnp.clip(1.0 + 0.18 * jax.random.normal(streams_of[10], (MODEL_WIDTH,), jnp.float32), 0.099609375, 1.8984375).astype(jnp.bfloat16)
    w_gate = noise(streams_of[11], (EXPERTS, MODEL_WIDTH, FF), MODEL_WIDTH ** -0.5, 0.1875, ((0, 4),))
    w_up = noise(streams_of[12], (EXPERTS, MODEL_WIDTH, FF), MODEL_WIDTH ** -0.5, 0.1875, ((0, 4),))
    w_down = noise(streams_of[13], (EXPERTS, FF, MODEL_WIDTH), (FF // 4) ** -0.5, 0.5, ((0, 4),))
    return dict(tokens=tokens, d_out=d_out, routes=routes, gates=gates, segment=segment, gain_attn=gain_attn, w_query=w_query, key_weight=key_weight, value_weight=value_weight, w_out=w_out, gain_ffn=gain_ffn, w_gate=w_gate, w_up=w_up, w_down=w_down)


@jax.custom_vjp
def low(v):
    return lax.optimization_barrier(v.astype(jnp.bfloat16)).astype(jnp.float32)

@jax.custom_vjp
def low_back(v):
    return v

def low_keep(v):
    return (low(v), None)

def low_pass(kept, grad):
    return (grad,)

def back_keep(v):
    return (v, None)

def back_low(kept, grad):
    return (low(grad),)
low.defvjp(low_keep, low_pass)
low_back.defvjp(back_keep, back_low)
norm_eps = 1e-06
score_scale = 0.125
highest_precision = lax.Precision.HIGHEST

def norm_apply(value_matrix, gain_vec):
    return value_matrix * lax.rsqrt(lax.optimization_barrier(jnp.mean(value_matrix * value_matrix, axis=-1, keepdims=True)) + norm_eps) * gain_vec

def rotate(value_matrix, token_place, direction):
    count_of_rows = value_matrix.shape[0]
    by_head = value_matrix.reshape(count_of_rows, -1, HEAD_SIZE)
    half_size = HEAD_SIZE // 2
    frequency = jnp.exp(jnp.arange(half_size).astype(jnp.float32) * (-2.0 * math.log(10000.0) / HEAD_SIZE))
    angles = direction * token_place.astype(jnp.float32)[:, None] * frequency[None, :]
    cosine_part = jnp.cos(angles)[:, None, :]
    sine_part = jnp.sin(angles)[:, None, :]
    first_half = by_head[..., :half_size]
    second_half = by_head[..., half_size:]
    turned = jnp.concatenate([first_half * cosine_part - second_half * sine_part, second_half * cosine_part + first_half * sine_part], axis=-1)
    return turned.reshape(count_of_rows, -1)

def layout(cont_ids, rank_count):
    cont_total = cont_ids.shape[0]
    cont_share = cont_total // rank_count
    prompt_share = PROMPT // rank_count
    seg_start = lax.optimization_barrier(jnp.sum((cont_ids[None, :] < cont_ids[:, None]).astype(jnp.int32), axis=1))
    cont_place = PROMPT + jnp.arange(cont_total, dtype=jnp.int32) - seg_start
    device = jnp.arange(rank_count, dtype=jnp.int32)[:, None]
    local_index = jnp.arange(prompt_share + cont_share, dtype=jnp.int32)[None, :]
    prompt_side = local_index < prompt_share
    cont_entry = jnp.clip(device * cont_share + local_index - prompt_share, 0, cont_total - 1).astype(jnp.int32)
    token_order = jnp.where(prompt_side, device * prompt_share + local_index, PROMPT + cont_entry)
    token_group = jnp.where(prompt_side, 0, cont_ids[cont_entry] + 1)
    token_place = jnp.where(prompt_side, device * prompt_share + local_index, cont_place[cont_entry])
    return (token_order.reshape(-1).astype(jnp.int32), token_group.reshape(-1).astype(jnp.int32), token_place.reshape(-1).astype(jnp.int32))

def attention(query_rows, rows_of_keys, value_matrix, token_order, token_group):
    rows_per_block = TOK_DEV
    while rows_per_block * 2 <= 512 and GROUP_TOKENS // (rows_per_block * 2) * rows_per_block * 2 == GROUP_TOKENS:
        rows_per_block = rows_per_block * 2
    blocks = GROUP_TOKENS // rows_per_block
    group_length = QUERY_HEADS // KEY_VALUE_HEADS
    heads_of_keys = rows_of_keys.reshape(GROUP_TOKENS, KEY_VALUE_HEADS, HEAD_SIZE)
    heads_of_values = value_matrix.reshape(GROUP_TOKENS, KEY_VALUE_HEADS, HEAD_SIZE)

    def one_block(pieces):
        block_of_queries, order_block, group_block = pieces
        heads_of_queries = block_of_queries.reshape(rows_per_block, KEY_VALUE_HEADS, group_length, HEAD_SIZE)
        scores = low_back(jnp.einsum('qhgd,khd->hgqk', heads_of_queries, heads_of_keys, precision=highest_precision) * score_scale)
        allowed = (token_order[None, :] <= order_block[:, None]) & ((token_group[None, :] == 0) | (token_group[None, :] == group_block[:, None]))
        scores = jnp.where(allowed[None, None], scores, -1e+30)
        row_max = lax.optimization_barrier(jnp.max(scores, axis=-1, keepdims=True))
        exponent = jnp.exp(scores - row_max)
        softmax_weights = low(exponent / lax.optimization_barrier(jnp.sum(exponent, axis=-1, keepdims=True)))
        output = jnp.einsum('hgqk,khd->qhgd', softmax_weights, heads_of_values, precision=highest_precision)
        return low(low_back(output.reshape(rows_per_block, QUERY_HEADS * HEAD_SIZE)))
    outputs = lax.map(jax.checkpoint(one_block), (query_rows.reshape(blocks, rows_per_block, QUERY_HEADS * HEAD_SIZE), token_order.reshape(blocks, rows_per_block), token_group.reshape(blocks, rows_per_block)))
    return outputs.reshape(GROUP_TOKENS, QUERY_HEADS * HEAD_SIZE)

def experts(normed_ffn, route_ids, route_gates, w_gate, w_up, w_down):
    count_of_rows = normed_ffn.shape[0]
    capacity = N_SHARD * CAP
    route_flat = route_ids.reshape(-1).astype(jnp.int32)
    one_hot = (route_flat[:, None] == jnp.arange(EXPERTS, dtype=jnp.int32)[None, :]).astype(jnp.int32)
    position = lax.optimization_barrier(jnp.sum((jnp.cumsum(one_hot, axis=0) - one_hot) * one_hot, axis=1)).astype(jnp.int32)
    slot_index = route_flat * capacity + position
    rows_in = low_back(jnp.repeat(normed_ffn, TOPK, axis=0))
    buffer = jnp.zeros((EXPERTS * capacity, MODEL_WIDTH), jnp.float32).at[slot_index].set(rows_in).reshape(EXPERTS, capacity, MODEL_WIDTH)
    gate_part = low_back(jnp.einsum('erd,edf->erf', buffer, w_gate, precision=highest_precision))
    up_part = low_back(jnp.einsum('erd,edf->erf', buffer, w_up, precision=highest_precision))
    inner_act = low(jax.nn.silu(gate_part) * up_part)
    expert_out = low_back(low(jnp.einsum('erf,efd->erd', inner_act, w_down, precision=highest_precision)))
    gathered_back = expert_out.reshape(EXPERTS * capacity, MODEL_WIDTH)[slot_index].reshape(count_of_rows, TOPK, MODEL_WIDTH)
    return lax.optimization_barrier(jnp.sum(route_gates[:, :, None] * gathered_back, axis=1))

def group_forward(inputs, route_ids, route_gates, cont_ids, params):
    gain_attn, w_query, key_weight, value_weight, w_out, gain_ffn, w_gate, w_up, w_down = params
    token_order, token_group, token_place = layout(cont_ids, N_SHARD)
    normed = low(norm_apply(inputs, gain_attn))
    query_rows = low(rotate(low_back(jnp.dot(normed, w_query, precision=highest_precision)), token_place, 1.0))
    rows_of_keys = low(rotate(low_back(jnp.dot(normed, key_weight, precision=highest_precision)), token_place, 1.0))
    value_matrix = low(low_back(jnp.dot(normed, value_weight, precision=highest_precision)))
    attended = attention(query_rows, rows_of_keys, value_matrix, token_order, token_group)
    hidden = inputs + low_back(jnp.dot(attended, w_out, precision=highest_precision))
    normed_ffn = low(norm_apply(hidden, gain_ffn))
    return hidden + experts(normed_ffn, route_ids, route_gates, w_gate, w_up, w_down)

def reference(tokens, d_out, routes, gates, segment, gain_attn, w_query, key_weight, value_weight, w_out, gain_ffn, w_gate, w_up, w_down):
    params = tuple((weight_arg.astype(jnp.float32) for weight_arg in (gain_attn, w_query, key_weight, value_weight, w_out, gain_ffn, w_gate, w_up, w_down)))
    inputs = tokens.astype(jnp.float32).reshape(GROUPS, GROUP_TOKENS, MODEL_WIDTH)
    route_all = routes.reshape(GROUPS, GROUP_TOKENS, TOPK)
    gate_all = gates.astype(jnp.float32).reshape(GROUPS, GROUP_TOKENS, TOPK)

    def whole_layer(inputs_all, weight_set):

        def one_group(pieces):
            return group_forward(pieces[0], pieces[1], pieces[2], pieces[3], weight_set)
        return lax.map(jax.checkpoint(one_group), (inputs_all, route_all, gate_all, segment))
    mixed_out, pullback = jax.vjp(whole_layer, inputs, params)
    input_grad, weight_grads = pullback(d_out.astype(jnp.float32).reshape(GROUPS, GROUP_TOKENS, MODEL_WIDTH))
    return (mixed_out.reshape(TOKENS, MODEL_WIDTH).astype(jnp.bfloat16), input_grad.reshape(TOKENS, MODEL_WIDTH), weight_grads[0], weight_grads[1], weight_grads[2], weight_grads[3], weight_grads[4], weight_grads[5], weight_grads[6], weight_grads[7], weight_grads[8])
```

```python
import functools
import math

import jax
import jax.numpy as jnp
from jax import lax
from jax.experimental import pallas as pl
from jax.experimental.pallas import tpu as pltpu
from jax.sharding import PartitionSpec as P

QUERY_HEADS = 16
KEY_VALUE_HEADS = 8
HEAD = 64
EXPERTS = 16
PROMPT = 1024
EPS = 1e-06
F32 = jnp.float32
BF = jnp.bfloat16
TILE = 256
VMEM_LIMIT = 56 * 1024 * 1024


def nn(a, b):
    return lax.dot_general(a, b, (((1,), (0,)), ((), ())), preferred_element_type=F32)


def nt(a, b):
    return lax.dot_general(a, b, (((1,), (1,)), ((), ())), preferred_element_type=F32)


def call(kernel, out_shape, flops, nbytes, trans=0, **kw):
    return pl.pallas_call(
        kernel,
        out_shape=out_shape,
        compiler_params=pltpu.CompilerParams(vmem_limit_bytes=VMEM_LIMIT),
        cost_estimate=pl.CostEstimate(
            flops=int(flops), bytes_accessed=int(nbytes), transcendentals=int(trans)
        ),
        **kw,
    )


VM = pl.BlockSpec(memory_space=pltpu.VMEM)
SM = pl.BlockSpec(memory_space=pltpu.SMEM)


def shape(dims, dtype):
    return jax.ShapeDtypeStruct(dims, dtype)


class Geo:
    def __init__(self, n, rows, conts):
        self.n = n
        self.T = rows
        self.PS = PROMPT // n
        self.CT = conts
        self.CS = conts // n
        self.TG = PROMPT + conts
        self.G = KEY_VALUE_HEADS // n
        self.relay = n == 4

    def pieces(self):
        out = [(m, 0, self.T) for m in range(self.n)]
        if self.relay:
            half = self.T // 2
            out = out[:-1] + [(3, 0, half), (3, half, half)]
        return out

    def places(self, me, m, off, rows):
        j = me ^ m
        out = []
        lead = max(0, min(self.PS, off + rows) - off)
        if lead:
            out.append((0, lead, pl.multiple_of(j * self.PS + off, 32)))
        if rows > lead:
            start = off + lead - self.PS
            out.append((lead, rows - lead, pl.multiple_of(PROMPT + j * self.CS + start, 32)))
        return out

    def tiles(self):
        out = []
        for i in range(PROMPT // TILE):
            ks = [(0, i * TILE, 0)] if i else []
            out.append((i * TILE, ks + [(i * TILE, TILE, 1)]))
        for c in range(self.CT // TILE):
            ks = [(0, PROMPT, 0)]
            if c:
                ks.append((PROMPT + (c - 1) * TILE, TILE, 2))
            ks.append((PROMPT + c * TILE, TILE, 3))
            out.append((PROMPT + c * TILE, ks))
        return out

    def spread(self, me, start):
        out = []
        if start < PROMPT:
            step = min(self.PS, TILE)
            for a in range(0, TILE, step):
                j = (start + a) // self.PS
                off = (start + a) % self.PS
                out.append((a, step, pl.multiple_of((me ^ j) * self.T + off, 32)))
        else:
            step = min(self.CS, TILE)
            for a in range(0, TILE, step):
                j = (start - PROMPT + a) // self.CS
                off = (start - PROMPT + a) % self.CS
                out.append((a, step, pl.multiple_of((me ^ j) * self.T + self.PS + off, 32)))
        return out


def iota(dims, axis):
    return lax.broadcasted_iota(jnp.int32, dims, axis)


def swap_halves(v):
    lane = iota(v.shape, 1)
    first = (lane & 32) == 0
    return jnp.where(first, pltpu.roll(v, 96, 1), pltpu.roll(v, 32, 1))


def masked(s, kind, q0, k0, segc_ref, segr_ref):
    if kind == 0:
        return s
    ok = None
    if kind != 2:
        ok = iota(s.shape, 0) <= iota(s.shape, 1)
    if kind != 1:
        same = segc_ref[k0 - PROMPT : k0 - PROMPT + TILE, :] == segr_ref[:, q0 - PROMPT : q0 - PROMPT + TILE]
        ok = same if ok is None else ok & same
    return jnp.where(ok, s, -1e30)


def qkv_kernel(geo, me_ref, *refs):
    np_ = len(geo.pieces())
    toks = refs[:np_]
    w_ref, gain_ref, c_ref, s_ref = refs[np_ : np_ + 4]
    normed_ref, q_ref, kd_ref, vd_ref, kt_ref, vt_ref, raw = refs[np_ + 4 :]
    me = me_ref[0]
    G = geo.G
    gain = gain_ref[...].astype(F32)
    for (m, off, rows), tok in zip(geo.pieces(), toks):
        v = tok[...].astype(F32)
        r = lax.rsqrt(jnp.mean(v * v, axis=-1, keepdims=True) + EPS)
        x = (v * r * gain).astype(BF)
        normed_ref[m * geo.T + off : m * geo.T + off + rows, :] = x
        y = nn(x, w_ref[...])
        for a, cnt, dst in geo.places(me, m, off, rows):
            raw[pl.ds(dst, cnt), :] = y[a : a + cnt, :]
    for t in range(0, geo.TG, TILE):
        rows = slice(t, t + TILE)
        cos, sin = c_ref[rows, :], s_ref[rows, :]
        low = iota((TILE, 128), 1) < 64
        for g in range(G):
            v = raw[rows, g * 128 : g * 128 + 128]
            q = (v * cos + swap_halves(v) * sin).astype(BF).astype(F32) * 0.125
            q_ref[2 * g, rows, :] = jnp.where(low, q, 0.0).astype(BF)
            q_ref[2 * g + 1, rows, :] = jnp.where(low, 0.0, q).astype(BF)
        v = raw[rows, G * 128 : G * 128 + 128]
        k = (v * cos + swap_halves(v) * sin).astype(BF).astype(F32)
        v = raw[rows, G * 128 + 128 : G * 128 + 256].astype(BF).astype(F32)
        kt = k.T.astype(BF)
        vt = v.T.astype(BF)
        kr, vr = pltpu.roll(k, 64, 1), pltpu.roll(v, 64, 1)
        for g in range(G):
            kt_ref[g, :, rows] = kt[g * 64 : g * 64 + 64, :]
            vt_ref[g, :, rows] = vt[g * 64 : g * 64 + 64, :]
            pick = low if g == 0 else ~low
            if G == 1:
                kd_ref[g, rows, :] = k.astype(BF)
                vd_ref[g, rows, :] = v.astype(BF)
            else:
                kd_ref[g, rows, :] = jnp.where(pick, k, kr).astype(BF)
                vd_ref[g, rows, :] = jnp.where(pick, v, vr).astype(BF)


def att_kernel(geo, me_ref, q_ref, kd_ref, vt_ref, segc_ref, segr_ref, o_ref, lse_ref):
    me = me_ref[0]
    for q0, keys in geo.tiles():
        outs = []
        for h in range(2):
            q = q_ref[h, q0 : q0 + TILE, :]
            ss = [
                masked(nt(kd_ref[0, k0 : k0 + kn, :], q), kind, q0, k0, segc_ref, segr_ref)
                for k0, kn, kind in keys
            ]
            top = functools.reduce(
                jnp.maximum, [jnp.max(s, axis=0, keepdims=True) for s in ss]
            )
            ps = [jnp.exp(s - top) for s in ss]
            total = functools.reduce(
                jnp.add, [jnp.sum(p, axis=0, keepdims=True) for p in ps]
            )
            lse_ref[h, :, q0 : q0 + TILE] = top + jnp.log(total)
            inv = 1.0 / total
            acc = None
            for p, (k0, kn, kind) in zip(ps, keys):
                part = nn(vt_ref[0, :, k0 : k0 + kn], (p * inv).astype(BF))
                acc = part if acc is None else acc + part
            outs.append(acc)
        o = jnp.concatenate(outs, axis=0).T.astype(BF)
        for a, cnt, dst in geo.spread(me, q0):
            o_ref[pl.ds(dst, cnt), :] = o[a : a + cnt, :]


def hidden_kernel(geo, natt, *refs):
    pieces = geo.pieces()
    np_ = len(pieces)
    atts = refs[:natt]
    toks = refs[natt : natt + np_]
    w_ref, gain_ref = refs[natt + np_ : natt + np_ + 2]
    hid_ref, x_ref, xt_ref = refs[natt + np_ + 2 :]
    gain = gain_ref[...].astype(F32)
    index = {}
    k = 0
    for g in range(geo.G):
        for m, off, rows in att_pieces(geo):
            index[(m, g, off)] = (atts[k], off, rows)
            k += 1

    def att_rows(m, g, row, cnt):
        for (mm, gg, _), (ref, off, rows) in index.items():
            if mm == m and gg == g and off <= row and row + cnt <= off + rows:
                return ref[row - off : row - off + cnt, :]
        raise ValueError("piece")

    for (j, off, rows), tok in zip(pieces, toks):
        lhs = jnp.concatenate(
            [
                att_rows(m, g, (m ^ j) * geo.T + off, rows)
                for m in range(geo.n)
                for g in range(geo.G)
            ],
            axis=1,
        )
        h = tok[...].astype(F32) + nn(lhs, w_ref[...])
        if j == 0:
            hid_ref[...] = h
        r = lax.rsqrt(jnp.mean(h * h, axis=-1, keepdims=True) + EPS)
        x_ref[j * geo.T + off : j * geo.T + off + rows, :] = (h * r * gain).astype(BF)
        if off + rows == geo.T:
            blk = x_ref[j * geo.T : (j + 1) * geo.T, :].astype(F32)
            xt_ref[:, j * geo.T : (j + 1) * geo.T] = blk.T.astype(BF)


def att_pieces(geo):
    rows = geo.n * geo.T
    out = [(m, 0, rows) for m in range(geo.n)]
    if geo.relay:
        out = out[:-1] + [(3, 0, rows // 2), (3, rows // 2, rows // 2)]
    return out


def expert_rows(x, dout, wg, wu, wd, gate):
    g = nn(x, wg)
    u = nn(x, wu)
    back = nt(dout, wd) * gate
    s = 1.0 / (1.0 + jnp.exp(-g))
    sil = g * s
    act = (sil * u * gate).astype(BF)
    gg = (back * u * (s + sil * (1.0 - s))).astype(BF)
    ug = (back * sil).astype(BF)
    dx = nt(gg, wg) + nt(ug, wu)
    return act, gg, ug, dx


CH = 2


def put_grads(outs, xt_ref, dt_ref, gg_ref, ug_ref, ac_ref):
    rows = xt_ref.shape[0] // CH
    for k, out in enumerate(outs):
        xt = xt_ref[k * rows : (k + 1) * rows, :]
        out[0] = nn(xt, gg_ref[...]).astype(BF)
        out[1] = nn(xt, ug_ref[...]).astype(BF)
        out[2] = nn(dt_ref[k * rows : (k + 1) * rows, :], ac_ref[...]).astype(BF)


def expert_full_kernel(n, T, e, first, c_ref, *refs):
    x_ref, do_ref, gm_ref, wg_ref, wu_ref, wd_ref, xt_ref, dt_ref = refs[:8]
    rest = refs[8:]
    if not first:
        dx_in, rest = rest[0], rest[2:]
    act_ref, dx_ref = rest[:2]
    sends, keeps = rest[2 : 2 + CH], rest[2 + CH : 2 + 2 * CH]
    gg_s, ug_s, ac_s = rest[2 + 2 * CH :]
    r = pl.program_id(0)

    @pl.when(r < n)
    def _():
        act, gg, ug, dx = expert_rows(
            x_ref[...], do_ref[...], wg_ref[0], wu_ref[0], wd_ref[0], gm_ref[:, e : e + 1]
        )
        rows = pl.ds(pl.multiple_of(r * T, 128), T)
        gg_s[rows, :] = gg
        ug_s[rows, :] = ug
        ac_s[rows, :] = act
        act_ref[...] = act
        dx_ref[...] = dx if first else dx_in[...] + dx

    @pl.when(r == n)
    def _():
        put_grads(sends, xt_ref, dt_ref, gg_s, ug_s, ac_s)

    @pl.when(r == n + 1)
    def _():
        put_grads(keeps, xt_ref, dt_ref, gg_s, ug_s, ac_s)


def expert_full(n, T, E, e, core, x, dout, gm, wg, wu, wd, xt, dt, dx, act):
    first = dx is None
    D, M = wg.shape[1:]
    row = lambda r, c: (jnp.minimum(r, n - 1), 0)
    half = lambda r, c: (jnp.where(r == n + 1, c[0], 1 - c[0]), 0)
    fix = lambda r, c: (e, 0, 0)
    in_specs = [
        pl.BlockSpec((T, D), row),
        pl.BlockSpec((T, D), row),
        pl.BlockSpec((T, E), row),
        pl.BlockSpec((1, D, M), fix),
        pl.BlockSpec((1, D, M), fix),
        pl.BlockSpec((1, M, D), fix),
        pl.BlockSpec((D // 2, n * T), half),
        pl.BlockSpec((D // 2, n * T), half),
    ]
    args = [x, dout, gm, wg, wu, wd, xt, dt]
    alias = {}
    if not first:
        in_specs += [pl.BlockSpec((T, D), row), pl.BlockSpec(memory_space=pl.ANY)]
        args += [dx, act]
        alias = {9: 1, 10: 0}
    whole = lambda r, c: (0, 0, 0)
    return call(
        functools.partial(expert_full_kernel, n, T, e, first),
        (
            shape((n * T, E * M), BF),
            shape((n * T, D), F32),
        )
        + (shape((3, D // 2 // CH, M), BF),) * (2 * CH),
        16 * n * T * D * M,
        24e6,
        grid_spec=pltpu.PrefetchScalarGridSpec(
            num_scalar_prefetch=1,
            grid=(n + 2,),
            in_specs=in_specs,
            out_specs=(
                pl.BlockSpec((T, M), lambda r, c: (jnp.minimum(r, n - 1), e)),
                pl.BlockSpec((T, D), row),
            )
            + (pl.BlockSpec((3, D // 2 // CH, M), whole),) * (2 * CH),
            scratch_shapes=[pltpu.VMEM((n * T, M), BF)] * 3,
        ),
        input_output_aliases=alias,
        name=f"expert_full{e}",
    )(core, *args)


def expert_block_kernel(count, e0, fresh, *refs):
    x_ref, do_ref, gm_ref, wg_ref, wu_ref, wd_ref, dx_ref, _act = refs[:8]
    rest = refs[8:] if fresh else refs[10:]
    act_ref, gg_ref, ug_ref, out_ref, acc = rest
    i = pl.program_id(0)
    lane = iota(gm_ref.shape, 1)
    gate = jnp.sum(jnp.where(lane == e0 + i, gm_ref[...], 0.0), axis=1, keepdims=True)
    act, gg, ug, dx = expert_rows(
        x_ref[...], do_ref[...], wg_ref[0], wu_ref[0], wd_ref[0], gate
    )
    act_ref[...] = act
    gg_ref[...] = gg
    ug_ref[...] = ug

    @pl.when(i == 0)
    def _():
        acc[...] = dx_ref[...] + dx

    @pl.when(i > 0)
    def _():
        acc[...] += dx

    @pl.when(i == count - 1)
    def _():
        out_ref[...] = acc[...].astype(BF)


def expert_block(n, T, E, j, e0, count, x, dout, gm, wg, wu, wd, dx, act, gg, ug):
    D, M = wg.shape[1:]
    fresh = gg is None
    row = lambda i: (j, 0)
    ex = lambda i: (e0 + i, 0, 0)
    any_ = pl.BlockSpec(memory_space=pl.ANY)
    in_specs = [
        pl.BlockSpec((T, D), row),
        pl.BlockSpec((T, D), row),
        pl.BlockSpec((T, E), row),
        pl.BlockSpec((1, D, M), ex),
        pl.BlockSpec((1, D, M), ex),
        pl.BlockSpec((1, M, D), ex),
        pl.BlockSpec((T, D), row),
        any_,
    ]
    args = [x, dout, gm, wg, wu, wd, dx, act]
    alias = {7: 0}
    if not fresh:
        in_specs += [any_, any_]
        args += [gg, ug]
        alias = {7: 0, 8: 1, 9: 2}
    return call(
        functools.partial(expert_block_kernel, count, e0, fresh),
        (
            shape((n * T, E * M), BF),
            shape((n * T, count * M), BF),
            shape((n * T, count * M), BF),
            shape((T, D), BF),
        ),
        10 * count * T * D * M,
        count * 4e6,
        grid=(count,),
        in_specs=in_specs,
        out_specs=(
            pl.BlockSpec((T, M), lambda i: (j, e0 + i)),
            pl.BlockSpec((T, M), lambda i: (j, i)),
            pl.BlockSpec((T, M), lambda i: (j, i)),
            pl.BlockSpec((T, D), lambda i: (0, 0)),
        ),
        scratch_shapes=[pltpu.VMEM((T, D), F32)],
        input_output_aliases=alias,
        name=f"expert_block{j}",
    )(*args)


def weight_grad_kernel(c_ref, xt_ref, dt_ref, gg_ref, ug_ref, ac_ref, *outs):
    @pl.when(pl.program_id(0) == 0)
    def _():
        put_grads(outs[:CH], xt_ref, dt_ref, gg_ref, ug_ref, ac_ref)

    @pl.when(pl.program_id(0) == 1)
    def _():
        put_grads(outs[CH:], xt_ref, dt_ref, gg_ref, ug_ref, ac_ref)


def weight_grad(R, M, e, i, core, xt, dt, gg, ug, act):
    D = xt.shape[0]
    half = lambda s, c: (jnp.where(s == 1, c[0], 1 - c[0]), 0)
    whole = lambda s, c: (0, 0, 0)
    return call(
        weight_grad_kernel,
        (shape((3, D // 2 // CH, M), BF),) * (2 * CH),
        6 * R * D * M,
        14e6,
        grid_spec=pltpu.PrefetchScalarGridSpec(
            num_scalar_prefetch=1,
            grid=(2,),
            in_specs=[
                pl.BlockSpec((D // 2, R), half),
                pl.BlockSpec((D // 2, R), half),
                pl.BlockSpec((R, M), lambda s, c: (0, i)),
                pl.BlockSpec((R, M), lambda s, c: (0, i)),
                pl.BlockSpec((R, M), lambda s, c: (0, e)),
            ],
            out_specs=(pl.BlockSpec((3, D // 2 // CH, M), whole),) * (2 * CH),
        ),
        name=f"weight_grad{e}",
    )(core, xt, dt, gg, ug, act)


def norm_back_kernel(count, low, *refs):
    parts = refs[:count]
    base_ref, v_ref, gain_ref = refs[count : count + 3]
    outs = refs[count + 3 :]
    grad = parts[0][...].astype(F32)
    for p in parts[1:]:
        grad = grad + p[...].astype(F32)
    v = v_ref[...].astype(F32)
    r = lax.rsqrt(jnp.mean(v * v, axis=-1, keepdims=True) + EPS)
    gv = gain_ref[...].astype(F32) * grad
    res = (
        base_ref[...].astype(F32)
        + r * gv
        - v * (r * r * r * jnp.mean(gv * v, axis=-1, keepdims=True))
    )
    outs[0][...] = res
    if low:
        outs[1][...] = res.astype(BF)
        part = jnp.sum(grad * v * r, axis=0, keepdims=True)

        @pl.when(pl.program_id(0) == 0)
        def _():
            outs[2][...] = part

        @pl.when(pl.program_id(0) > 0)
        def _():
            outs[2][...] += part


def norm_back(parts, base, v, gain, low):
    T, D = v.shape
    B = 128
    row = pl.BlockSpec((B, D), lambda i: (i, 0))
    one = pl.BlockSpec((1, D), lambda i: (0, 0))
    out = [shape((T, D), F32)]
    specs = [row]
    if low:
        out += [shape((T, D), BF), shape((1, D), F32)]
        specs += [row, one]
    return call(
        functools.partial(norm_back_kernel, len(parts), low),
        tuple(out),
        20 * T * D,
        T * D * 16,
        grid=(T // B,),
        in_specs=[row] * len(parts) + [row, row, one],
        out_specs=tuple(specs),
        name="norm_back",
    )(*parts, base, v, gain)


def att_back_kernel(geo, me_ref, *refs):
    pieces = geo.pieces()
    np_ = len(pieces)
    brs = refs[:np_]
    (w_ref, q_ref, kd_ref, kt_ref, vd_ref, lse_ref, segc_ref, segr_ref, c_ref, s_ref) = refs[
        np_ : np_ + 10
    ]
    out_ref, do_s, dk_s, dv_s, dq_s = refs[np_ + 10 :]
    me = me_ref[0]
    G = geo.G
    for (m, off, rows), br in zip(pieces, brs):
        y = nt(br[...], w_ref[...])
        low = iota((rows, 128), 1) < 64
        for g in range(G):
            part = y[:, g * 128 : g * 128 + 128]
            lo = jnp.where(low, part, 0.0).astype(BF)
            hi = jnp.where(low, 0.0, part).astype(BF)
            for a, cnt, dst in geo.places(me, m, off, rows):
                do_s[2 * g, pl.ds(dst, cnt), :] = lo[a : a + cnt, :]
                do_s[2 * g + 1, pl.ds(dst, cnt), :] = hi[a : a + cnt, :]
    dk_s[...] = jnp.zeros_like(dk_s)
    dv_s[...] = jnp.zeros_like(dv_s)

    def head(i, carry):
        g = i // 2
        for q0, keys in geo.tiles():
            q = q_ref[i, q0 : q0 + TILE, :]
            do = do_s[i, q0 : q0 + TILE, :]
            lse = lse_ref[i, :, q0 : q0 + TILE]
            ps, dps = [], []
            delta = None
            for k0, kn, kind in keys:
                s = masked(nt(kd_ref[g, k0 : k0 + kn, :], q), kind, q0, k0, segc_ref, segr_ref)
                p = jnp.exp(s - lse)
                dp = nt(vd_ref[g, k0 : k0 + kn, :], do)
                dv_s[g, k0 : k0 + kn, :] += nn(p.astype(BF), do)
                d = jnp.sum(p * dp, axis=0, keepdims=True)
                delta = d if delta is None else delta + d
                ps.append(p)
                dps.append(dp)
            acc = None
            for p, dp, (k0, kn, kind) in zip(ps, dps, keys):
                ds = (p * (dp - delta)).astype(BF)
                dk_s[g, k0 : k0 + kn, :] += nn(ds, q)
                part = nn(kt_ref[g, :, k0 : k0 + kn], ds)
                acc = part if acc is None else acc + part
            dq_s[i, :, q0 : q0 + TILE] = acc
        return carry

    lax.fori_loop(0, 2 * G, head, 0)
    low = iota((TILE, 128), 1) < 64
    for t in range(0, geo.TG, TILE):
        rows = slice(t, t + TILE)
        cos, sin = c_ref[rows, :], s_ref[rows, :]
        cols = []
        for g in range(G):
            v = jnp.concatenate([dq_s[2 * g, :, rows], dq_s[2 * g + 1, :, rows]], axis=0).T * 0.125
            cols.append(v * cos - swap_halves(v) * sin)
        ks, vs = [], []
        for g in range(G):
            k = dk_s[g, rows, :]
            ks.append(k + pltpu.roll(k, 64, 1))
            v = dv_s[g, rows, :]
            vs.append(v + pltpu.roll(v, 64, 1))
        other_k = ks[1] if G == 2 else 0.0
        other_v = vs[1] if G == 2 else 0.0
        k = jnp.where(low, ks[0], other_k)
        cols.append(k * cos - swap_halves(k) * sin)
        cols.append(jnp.where(low, vs[0], other_v))
        for x, col in enumerate(cols):
            y = col.astype(BF)
            for a, cnt, dst in geo.spread(me, t):
                out_ref[pl.ds(dst, cnt), x * 128 : x * 128 + 128] = y[a : a + cnt, :]


def finish_kernel(e, first, c_ref, *refs):
    owns, sibs = refs[:CH], refs[CH : 2 * CH]
    g_ref, u_ref, d_ref = refs[2 * CH :] if first else refs[2 * CH + 3 :]

    def put(srcs):
        rows = g_ref.shape[1] // CH
        for k, src in enumerate(srcs):
            g_ref[0, k * rows : (k + 1) * rows, :] = src[0].astype(F32)
            u_ref[0, k * rows : (k + 1) * rows, :] = src[1].astype(F32)
            d_ref[0, :, k * rows : (k + 1) * rows] = src[2].astype(F32).T

    @pl.when(pl.program_id(0) == 0)
    def _():
        put(owns)

    @pl.when(pl.program_id(0) == 1)
    def _():
        put(sibs)


def finish(e, E, core, owns, sibs, prev):
    _, rows, M = owns[0].shape
    Dh = rows * CH
    first = prev is None
    half = lambda s, c: jnp.where(s == 0, c[0], 1 - c[0])
    whole = pl.BlockSpec((3, rows, M), lambda s, c: (0, 0, 0))
    args = [*owns, *sibs] + ([] if first else list(prev))
    alias = {} if first else {2 * CH + 1: 0, 2 * CH + 2: 1, 2 * CH + 3: 2}
    return call(
        functools.partial(finish_kernel, e, first),
        (
            shape((E, 2 * Dh, M), F32),
            shape((E, 2 * Dh, M), F32),
            shape((E, M, 2 * Dh), F32),
        ),
        1e6,
        10e6,
        grid_spec=pltpu.PrefetchScalarGridSpec(
            num_scalar_prefetch=1,
            grid=(2,),
            in_specs=[whole] * (2 * CH)
            + ([] if first else [pl.BlockSpec(memory_space=pl.ANY)] * 3),
            out_specs=(
                pl.BlockSpec((1, Dh, M), lambda s, c: (e, half(s, c), 0)),
                pl.BlockSpec((1, Dh, M), lambda s, c: (e, half(s, c), 0)),
                pl.BlockSpec((1, M, Dh), lambda s, c: (e, 0, half(s, c))),
            ),
        ),
        input_output_aliases=alias,
        name=f"finish{e}",
    )(core, *args)


def per_device(
    tokens,
    d_out,
    routes,
    gates,
    segment,
    gain_attn,
    w_query,
    key_weight,
    value_weight,
    w_out,
    gain_ffn,
    w_gate,
    w_up,
    w_down,
):
    n = lax.axis_size("shard")
    me = lax.axis_index("shard")
    R = lax.axis_size("rep")
    rp = lax.axis_index("rep")
    core, pos = rp % 2, rp // 2
    T, D = tokens.shape
    geo = Geo(n, T, segment.shape[1])
    G, TG = geo.G, geo.TG
    E, _, M = w_gate.shape
    me1 = me.reshape(1).astype(jnp.int32)
    core1 = core.reshape(1).astype(jnp.int32)

    def px(v, m):
        return lax.ppermute(v, "shard", [(i, i ^ m) for i in range(n)])

    def at(v, i):
        return lax.dynamic_index_in_dim(v, i, 0, keepdims=False)

    def gather(v):
        if not geo.relay:
            return [v] + [px(v, m) for m in range(1, n)]
        h = v.shape[0] // 2
        a, b = px(v, 1), px(v, 2)
        return [v, a, b, px(a[:h], 2), px(b[h:], 1)]

    def tie(vals, deps):
        vals, deps = tuple(vals), tuple(deps)
        return lax.optimization_barrier(vals + deps)[: len(vals)]

    L = R // 2

    def pz(v, pairs):
        return lax.ppermute(v, "rep", [(2 * a + k, 2 * b + k) for a, b in pairs for k in (0, 1)])

    def sib(v):
        return lax.ppermute(v, "rep", [(i, i ^ 1) for i in range(R)])

    def plus(a, b):
        return (a.astype(F32) + b.astype(F32)).astype(BF)

    class Sums:
        def __init__(self):
            self.live, self.done = [], []

        def add(self, tag, keep, send):
            self.live.append([tag, 0, plus(keep, sib(send))])

        def step(self, k, acc):
            mid = L // 2
            if k < mid - 1:
                return plus(acc, pz(acc, [(k, k + 1), (L - 1 - k, L - 2 - k)]))
            if k == mid - 1:
                return plus(acc, pz(acc, [(mid - 1, mid), (mid, mid - 1)])) if L > 1 else acc
            s = k - mid
            new = pz(acc, [(mid - 1 - s, mid - 2 - s), (mid + s, mid + 1 + s)])
            return jnp.where((pos == mid - 2 - s) | (pos == mid + 1 + s), new, acc)

        def advance(self, vals):
            vals = tuple(vals)
            got = lax.optimization_barrier(vals + tuple(c[2] for c in self.live))
            vals, accs = got[: len(vals)], got[len(vals) :]
            fresh, rest = True, []
            for chunk, acc in zip(self.live, accs):
                tag, k, _ = chunk
                if k == L - 1:
                    self.done.append((tag, acc, sib(acc)))
                elif k > 0 or fresh:
                    fresh = fresh and k > 0
                    rest.append([tag, k + 1, self.step(k, acc)])
                else:
                    rest.append([tag, k, acc])
            self.live = rest
            return vals

        def pair(self, tag):
            return next((c[1], c[2]) for c in self.done if c[0] == tag)

    sums = Sums()

    r = w_query.shape[0]
    qc, kc = w_query.shape[1] // n, key_weight.shape[1] // n
    W = qc + 2 * kc
    gains = jnp.concatenate([gain_attn, gain_ffn])[None]
    gains = jnp.pad(jnp.broadcast_to(gains[None], (n, 1, 2 * r)), ((0, 0), (0, 15), (0, 0)))
    wmsg = jnp.concatenate(
        [
            w_query.reshape(r, n, qc).transpose(1, 0, 2),
            key_weight.reshape(r, n, kc).transpose(1, 0, 2),
            value_weight.reshape(r, n, kc).transpose(1, 0, 2),
        ],
        axis=2,
    )
    wmsg = jnp.concatenate([wmsg, gains], axis=1)
    got_w = [at(wmsg, me)] + [px(at(wmsg, me ^ m), m) for m in range(1, n)]
    tok = gather(tokens)

    got_w = jnp.stack(got_w)
    in_order = [at(got_w, me ^ j) for j in range(n)]
    w_own = jnp.concatenate([v[:r] for v in in_order], axis=0)
    gain_a = jnp.concatenate([v[r : r + 1, :r] for v in in_order], axis=1)
    gain_f = jnp.concatenate([v[r : r + 1, r : 2 * r] for v in in_order], axis=1)
    if G == 1:
        wk, wv = w_own[:, qc : qc + kc], w_own[:, qc + kc :]
        w_cols = jnp.concatenate([w_own[:, :qc], wk, wk, wv, wv], axis=1)
    else:
        w_cols = w_own
    WC = w_cols.shape[1]

    seg = segment[0]
    CT = seg.shape[0]
    start = jnp.sum((seg[None, :] < seg[:, None]).astype(jnp.int32), axis=1)
    place = jnp.concatenate(
        [
            jnp.arange(PROMPT, dtype=jnp.int32),
            PROMPT + jnp.arange(CT, dtype=jnp.int32) - start,
        ]
    )
    freq = jnp.exp(jnp.arange(HEAD // 2).astype(F32) * (-2.0 * math.log(10000.0) / HEAD))
    ang = place.astype(F32)[:, None] * freq[None, :]
    cs, sn = jnp.cos(ang), jnp.sin(ang)
    cos4 = jnp.concatenate([cs, cs, cs, cs], axis=1)
    sin4 = jnp.concatenate([-sn, sn, -sn, sn], axis=1)
    segc, segr = seg[:, None], seg[None, :]

    d_late, wo_late, routes_late, w_cols, cos4, sin4, *tok = tie(
        (d_out, at(w_out.reshape(2, r // 2, D), core), routes, w_cols, cos4, sin4, *tok), ()
    )
    wo_half = gather(wo_late)

    np_ = len(geo.pieces())
    normed, q, kd, vd, kt, vt = call(
        functools.partial(qkv_kernel, geo),
        (
            shape((n * T, D), BF),
            shape((2 * G, TG, 128), BF),
            shape((G, TG, 128), BF),
            shape((G, TG, 128), BF),
            shape((G, 64, TG), BF),
            shape((G, 64, TG), BF),
        ),
        2 * TG * D * WC,
        12e6,
        in_specs=[SM] + [VM] * (np_ + 4),
        out_specs=(VM,) * 6,
        scratch_shapes=[pltpu.VMEM((TG, WC), F32)],
        name="qkv",
    )(me1, *tok, w_cols, gain_a, cos4, sin4)

    atts, lses, own_att = [], [], []
    for g in range(G):
        o, lse = call(
            functools.partial(att_kernel, geo),
            (shape((n * T, 128), BF), shape((2, 1, TG), F32)),
            1e9,
            3e6,
            2 * TG * TG * 0.6,
            grid=(1,),
            in_specs=[
                SM,
                pl.BlockSpec((2, TG, 128), lambda i, g=g: (g, 0, 0)),
                pl.BlockSpec((1, TG, 128), lambda i, g=g: (g, 0, 0)),
                pl.BlockSpec((1, 64, TG), lambda i, g=g: (g, 0, 0)),
                VM,
                VM,
            ],
            out_specs=(VM, VM),
            name=f"attend{g}",
        )(me1, q, kd, vt, segc, segr)
        own_att.append(o)
        lses.append(lse)
        atts += gather(o)
        if g == 0:
            half = jnp.concatenate(wo_half, axis=0).reshape(n, 1, r // 2, D)
            other = sib(half)
            both_ = jnp.where(core == 0, jnp.concatenate([half, other], 1), jnp.concatenate([other, half], 1))
            wo_rel = both_.reshape(n * r, D)
            dense = jnp.sum(
                jnp.where(
                    routes_late[None] == jnp.arange(EXPERTS, dtype=jnp.int32)[:, None, None],
                    gates[None],
                    0.0,
                ),
                axis=2,
            ).reshape(n, E, T)
            gm = [at(dense, me)] + [px(at(dense, me ^ m), m) for m in range(1, n)]
            gm = jnp.concatenate(gm, axis=1).T
    lse = jnp.concatenate(lses, axis=0)
    (d_late,) = tie((d_late,), own_att)
    dout = jnp.concatenate(gather(d_late), axis=0)
    dout_t = dout.T

    hidden, x, xt = call(
        functools.partial(hidden_kernel, geo, len(atts)),
        (shape((T, D), F32), shape((n * T, D), BF), shape((D, n * T), BF)),
        2 * TG * D * D,
        16e6,
        in_specs=[VM] * (len(atts) + np_ + 2),
        out_specs=(VM,) * 3,
        name="hidden",
    )(*atts, *tok, wo_rel, gain_f)

    early = E // 2
    late = E - early
    dx = act = None
    for e in range(early):
        act, dx, *wg_ = expert_full(
            n, T, E, e, core1, x, dout, gm, w_gate, w_up, w_down, xt, dout_t, dx, act
        )
        for k in range(CH):
            sums.add((e, k), wg_[CH + k], wg_[k])
        x, act, dx = sums.advance((x, act, dx))
    gg = ug = None
    order = [m for m in range(n - 1, -1, -1)]
    parts, came = {}, {}
    for t, j in enumerate(order):
        act, gg, ug, p = expert_block(
            n, T, E, j, early, late, x, dout, gm, w_gate, w_up, w_down, dx, act, gg, ug
        )
        parts[j] = p
        if j:
            came[j] = px(p, j)
        if t % 2 == 1:
            x, act, gg, ug = sums.advance((x, act, gg, ug))
        else:
            x, act, gg, ug = tie((x, act, gg, ug), (p,))
    for i in range(late):
        wg_ = weight_grad(n * T, M, early + i, i, core1, xt, dout_t, gg, ug, act)
        for k in range(CH):
            sums.add((early + i, k), wg_[CH + k], wg_[k])
        gg, act = tie((gg, act), wg_)
    came = [parts[0]] + [came[m] for m in order[:-1]]
    came = sums.advance((*came, act))
    came, act = came[:-1], came[-1]

    hidden_grad, branch, gain_f_part = norm_back(came, d_out, hidden, gain_f, True)
    (act,) = tie((act,), (branch,))
    branches = gather(branch)

    wd2 = w_down.reshape(E * M, D)
    mix = [
        jnp.dot(act[j * T : (j + 1) * T], wd2, preferred_element_type=F32).astype(
            F32 if j == 0 else BF
        )
        for j in range(n)
    ]
    mix = sums.advance(mix)
    branches = sums.advance(branches)
    mix = tie(mix, branches)
    mix_sum = hidden + mix[0]
    for m in range(n - 1, 0, -1):
        mix_sum = mix_sum + px(mix[m], m).astype(F32)
    mixed = mix_sum.astype(BF)

    dqkv = call(
        functools.partial(att_back_kernel, geo),
        shape((n * T, WC), BF),
        4e9,
        12e6,
        4 * TG * TG * 0.6,
        in_specs=[SM] + [VM] * (np_ + 10),
        out_specs=VM,
        scratch_shapes=[
            pltpu.VMEM((2 * G, TG, 128), BF),
            pltpu.VMEM((G, TG, 128), F32),
            pltpu.VMEM((G, TG, 128), F32),
            pltpu.VMEM((2 * G, 64, TG), F32),
        ],
        name="attend_back",
    )(me1, *branches, w_out, q, kd, kt, vd, lse, segc, segr, cos4, sin4)
    mixed, dqkv = sums.advance((mixed, dqkv))

    back = {j: nt(dqkv[j * T : (j + 1) * T], w_cols).astype(BF) for j in order}
    came = [back[0]] + [px(back[m], m) for m in range(n - 1, 0, -1)]

    dw = lax.dot_general(normed, dqkv, (((0,), (0,)), ((), ())), preferred_element_type=F32)
    ga_part = jnp.sum(dw * w_cols.astype(F32), axis=1).reshape(n, 1, r)
    if G == 1:
        dw = jnp.concatenate(
            [dw[:, :qc], dw[:, qc : qc + kc], dw[:, qc + 2 * kc : qc + 3 * kc]], axis=1
        )
    extra = jnp.concatenate([ga_part, gain_f_part.reshape(n, 1, r)], axis=2)
    extra = jnp.pad(extra, ((0, 0), (0, 15), (0, 0)))
    gmsg = jnp.concatenate([dw.reshape(n, r, W), extra], axis=1).astype(BF)
    got = [at(gmsg, me)] + [px(at(gmsg, me ^ m), m) for m in range(1, n)]
    got = jnp.stack(got).reshape(2, n // 2, r + 16, W)
    branch_all = jnp.concatenate(branches, axis=0)
    g_out = jnp.concatenate(
        [
            lax.dot_general(o, branch_all, (((0,), (0,)), ((), ())), preferred_element_type=F32)
            for o in own_att
        ],
        axis=0,
    ).astype(BF)
    g_out = g_out.reshape(2, r // 2, D)
    sums.add("out", at(g_out, core), at(g_out, 1 - core))
    sums.add("small", at(got, core), at(got, 1 - core))

    prev = None
    finished = 0

    def finishing(limit):
        nonlocal prev, finished
        while finished < limit and sum(c[0][0] == finished for c in sums.done) == CH:
            owns, sibs = zip(*[sums.pair((finished, k)) for k in range(CH)])
            prev = finish(finished, E, core1, owns, sibs, prev)
            finished += 1

    came = sums.advance(came)
    (d_tokens,) = norm_back(came, hidden_grad, tokens, gain_a, False)
    (d_tokens,) = sums.advance((d_tokens,))
    while sums.live:
        finishing(E - 1)
        if prev is None:
            sums.advance(())
        else:
            prev = sums.advance(prev)
    finishing(E)
    g_gate, g_up, g_down = prev

    def both(tag):
        v, other = sums.pair(tag)
        return jnp.where(core == 0, jnp.stack([v, other]), jnp.stack([other, v])).astype(F32)

    g_out_all = both("out").reshape(r, D)
    small = both("small").reshape(n, r + 16, W)
    in_order = [at(small, me ^ j) for j in range(n)]
    g_q = jnp.concatenate([v[:r, :qc] for v in in_order], axis=1)
    g_k = jnp.concatenate([v[:r, qc : qc + kc] for v in in_order], axis=1)
    g_v = jnp.concatenate([v[:r, qc + kc :] for v in in_order], axis=1)
    extra = jnp.sum(small[:, r, :], axis=0)
    g_ga = extra[:r] / gain_attn.astype(F32)
    g_gf = extra[r:]
    return (mixed, d_tokens, g_ga, g_q, g_k, g_v, g_out_all, g_gf, g_gate, g_up, g_down)


def solution(mesh):
    rows = P(("rep", "shard"), None)
    own = P("shard", None)
    own3 = P("shard", None, None)
    vec = P("shard")
    return jax.shard_map(
        per_device,
        mesh=mesh,
        in_specs=(
            rows,
            rows,
            rows,
            rows,
            P("rep", None),
            vec,
            own,
            own,
            own,
            own,
            vec,
            own3,
            own3,
            own3,
        ),
        out_specs=(rows, rows, vec, own, own, own, own, vec, own3, own3, own3),
        check_vma=False,
    )
```

```python
import functools
import math

import jax
import jax.numpy as jnp
from jax import lax
from jax.experimental import pallas as pl
from jax.experimental.pallas import tpu as pltpu
from jax.sharding import PartitionSpec as P

QUERY_HEADS = 16
KEY_VALUE_HEADS = 8
HEAD = 64
EXPERTS = 16
PROMPT = 1024
EPS = 1e-06
F32 = jnp.float32
BF = jnp.bfloat16
TILE = 256
VMEM_LIMIT = 26 * 1024 * 1024


def nn(a, b):
    return lax.dot_general(a, b, (((1,), (0,)), ((), ())), preferred_element_type=F32)


def nt(a, b):
    return lax.dot_general(a, b, (((1,), (1,)), ((), ())), preferred_element_type=F32)


def tn(a, b):
    return lax.dot_general(a, b, (((0,), (0,)), ((), ())), preferred_element_type=F32)


COST = 0.25


def call(kernel, out_shape, flops, nbytes, trans=0, **kw):
    return pl.pallas_call(
        kernel,
        out_shape=out_shape,
        compiler_params=pltpu.CompilerParams(vmem_limit_bytes=VMEM_LIMIT),
        cost_estimate=pl.CostEstimate(
            flops=int(COST * flops), bytes_accessed=int(COST * nbytes), transcendentals=int(COST * trans)
        ),
        **kw,
    )


VM = pl.BlockSpec(memory_space=pltpu.VMEM)
SM = pl.BlockSpec(memory_space=pltpu.SMEM)


def shape(dims, dtype):
    return jax.ShapeDtypeStruct(dims, dtype)


class Geo:
    def __init__(self, n, rows, conts):
        self.n = n
        self.T = rows
        self.PS = PROMPT // n
        self.CT = conts
        self.CS = conts // n
        self.TG = PROMPT + conts
        self.G = KEY_VALUE_HEADS // n
        self.relay = n == 4

    def pieces(self):
        out = [(m, 0, self.T) for m in range(self.n)]
        if self.relay:
            half = self.T // 2
            out = out[:-1] + [(3, 0, half), (3, half, half)]
        return out

    def places(self, me, m, off, rows):
        j = me ^ m
        out = []
        lead = max(0, min(self.PS, off + rows) - off)
        if lead:
            out.append((0, lead, pl.multiple_of(j * self.PS + off, 32)))
        if rows > lead:
            start = off + lead - self.PS
            out.append((lead, rows - lead, pl.multiple_of(PROMPT + j * self.CS + start, 32)))
        return out

    def tiles(self):
        out = []
        for i in range(PROMPT // TILE):
            ks = [(0, i * TILE, 0)] if i else []
            out.append((i * TILE, ks + [(i * TILE, TILE, 1)]))
        for c in range(self.CT // TILE):
            ks = [(0, PROMPT, 0)]
            if c:
                ks.append((PROMPT + (c - 1) * TILE, TILE, 2))
            ks.append((PROMPT + c * TILE, TILE, 3))
            out.append((PROMPT + c * TILE, ks))
        return out

    def spread(self, me, start):
        out = []
        if start < PROMPT:
            step = min(self.PS, TILE)
            for a in range(0, TILE, step):
                j = (start + a) // self.PS
                off = (start + a) % self.PS
                out.append((a, step, pl.multiple_of((me ^ j) * self.T + off, 32)))
        else:
            step = min(self.CS, TILE)
            for a in range(0, TILE, step):
                j = (start - PROMPT + a) // self.CS
                off = (start - PROMPT + a) % self.CS
                out.append((a, step, pl.multiple_of((me ^ j) * self.T + self.PS + off, 32)))
        return out


def iota(dims, axis):
    return lax.broadcasted_iota(jnp.int32, dims, axis)


def swap_halves(v):
    lane = iota(v.shape, 1)
    first = (lane & 32) == 0
    return jnp.where(first, pltpu.roll(v, 96, 1), pltpu.roll(v, 32, 1))


def masked(s, kind, q0, k0, segc_ref, segr_ref):
    if kind == 0:
        return s
    ok = None
    if kind != 2:
        ok = iota(s.shape, 0) <= iota(s.shape, 1)
    if kind != 1:
        same = segc_ref[k0 - PROMPT : k0 - PROMPT + TILE, :] == segr_ref[:, q0 - PROMPT : q0 - PROMPT + TILE]
        ok = same if ok is None else ok & same
    return jnp.where(ok, s, -1e30)


def qkv_kernel(geo, me_ref, *refs):
    np_ = len(geo.pieces())
    toks = refs[:np_]
    n = geo.n
    msgs = refs[np_ : np_ + n]
    c_ref, s_ref = refs[np_ + n : np_ + n + 2]
    (normed_ref, q_ref, kd_ref, vd_ref, kt_ref, vt_ref, w_ref, ga_ref, gf_ref, raw) = refs[
        np_ + n + 2 :
    ]
    me = me_ref[0]
    G = geo.G
    r = msgs[0].shape[0] - 16
    for m, msg in enumerate(msgs):
        w_ref[pl.ds(pl.multiple_of((me ^ m) * r, 128), r), :] = msg[:r, :]
        gains = msg[r : r + 16, :].astype(F32)[:1, :]
        for j in range(n):

            @pl.when((me ^ m) == j)
            def _():
                ga_ref[:, j * r : (j + 1) * r] = gains[:, :r]
                gf_ref[:, j * r : (j + 1) * r] = gains[:, r : 2 * r]

    gain = ga_ref[...]
    for (m, off, rows), tok in zip(geo.pieces(), toks):
        v = tok[...].astype(F32)
        r = lax.rsqrt(jnp.mean(v * v, axis=-1, keepdims=True) + EPS)
        x = (v * r * gain).astype(BF)
        normed_ref[m * geo.T + off : m * geo.T + off + rows, :] = x
        y = nn(x, w_ref[...])
        for a, cnt, dst in geo.places(me, m, off, rows):
            raw[pl.ds(dst, cnt), :] = y[a : a + cnt, :]
    for t in range(0, geo.TG, TILE):
        rows = slice(t, t + TILE)
        cos, sin = c_ref[rows, :], s_ref[rows, :]
        low = iota((TILE, 128), 1) < 64
        for g in range(G):
            v = raw[rows, g * 256 : g * 256 + 128]
            q = (v * cos + swap_halves(v) * sin).astype(BF).astype(F32) * 0.125
            q_ref[2 * g, rows, :] = jnp.where(low, q, 0.0).astype(BF)
            q_ref[2 * g + 1, rows, :] = jnp.where(low, 0.0, q).astype(BF)
            kv = raw[rows, g * 256 + 128 : g * 256 + 256]
            vk = pltpu.roll(kv, 64, 1)
            k = jnp.where(low, kv, vk)
            k = (k * cos + swap_halves(k) * sin).astype(BF)
            v = jnp.where(low, vk, kv)
            kd_ref[g, rows, :] = k
            vd_ref[g, rows, :] = v.astype(BF)
            kt_ref[g, :, rows] = k.astype(F32).T[:64, :].astype(BF)
            vt_ref[g, :, rows] = v.T[:64, :].astype(BF)


def columns_kernel(geo, me_ref, wq_ref, wk_ref, wv_ref, ga_ref, gf_ref, *outs):
    me = me_ref[0]
    r = wq_ref.shape[0]
    low = iota((r, 128), 1) < 64
    gains = jnp.concatenate([ga_ref[...], gf_ref[...]], axis=1)
    gains = jnp.broadcast_to(gains, (16, gains.shape[1]))
    for j in range(geo.n):
        cols = []
        for g in range(geo.G):
            h = j * geo.G + g
            pair = slice(h // 2 * 128, h // 2 * 128 + 128)
            k = wk_ref[:, pair].astype(F32)
            v = wv_ref[:, pair].astype(F32)
            if h % 2 == 0:
                kv = jnp.where(low, k, pltpu.roll(v, 64, 1))
            else:
                kv = jnp.where(low, pltpu.roll(k, 64, 1), v)
            cols += [wq_ref[:, h * 128 : h * 128 + 128], kv.astype(BF)]
        block = jnp.concatenate(cols, axis=1)
        for m, out in enumerate(outs):

            @pl.when((me ^ m) == j)
            def _():
                out[:r, :] = block
                out[r:, :] = gains


def pack_kernel(d_ref, r_ref, g_ref, segc_ref, segr_ref, out_ref, c_ref, s_ref):
    D = d_ref.shape[1]
    out_ref[:, :D] = d_ref[...]
    lane = iota((d_ref.shape[0], 128), 1)
    gate = jnp.zeros(lane.shape, F32)
    for k in range(r_ref.shape[1]):
        hit = (lane & (EXPERTS - 1)) == r_ref[:, k : k + 1]
        gate = gate + jnp.where(hit, g_ref[:, k : k + 1], 0.0)
    top = gate.astype(BF).astype(F32)
    mid = (gate - top).astype(BF).astype(F32)
    low = gate - top - mid
    term = jnp.where(lane < EXPERTS, top, jnp.where(lane < 2 * EXPERTS, mid, low))
    out_ref[:, D:] = jnp.where(lane < 3 * EXPERTS, term, 0.0).astype(BF)

    lane = iota((1, 128), 1)
    freq = jnp.exp((lane & 31).astype(F32) * (-2.0 * math.log(10000.0) / HEAD))
    sign = jnp.where((lane & 32) == 0, -1.0, 1.0)
    for t in range(0, c_ref.shape[0], TILE):
        row = iota((TILE, 1), 0).astype(F32) + float(t)
        if t >= PROMPT:
            own = segc_ref[t - PROMPT : t - PROMPT + TILE, :]
            start = jnp.sum(jnp.where(segr_ref[...] < own, 1.0, 0.0), axis=1, keepdims=True)
            row = row - start
        ang = row * freq
        c_ref[t : t + TILE, :] = jnp.cos(ang)
        s_ref[t : t + TILE, :] = jnp.sin(ang) * sign


def att_kernel(geo, me_ref, q_ref, kd_ref, vt_ref, segc_ref, segr_ref, o_ref, lse_ref):
    me = me_ref[0]
    for q0, keys in geo.tiles():
        outs = []
        for h in range(2):
            q = q_ref[h, q0 : q0 + TILE, :]
            ss = [
                masked(nt(kd_ref[0, k0 : k0 + kn, :], q), kind, q0, k0, segc_ref, segr_ref)
                for k0, kn, kind in keys
            ]
            top = functools.reduce(
                jnp.maximum, [jnp.max(s, axis=0, keepdims=True) for s in ss]
            )
            ps = [jnp.exp(s - top) for s in ss]
            total = functools.reduce(
                jnp.add, [jnp.sum(p, axis=0, keepdims=True) for p in ps]
            )
            lse_ref[h, :, q0 : q0 + TILE] = top + jnp.log(total)
            inv = 1.0 / total
            acc = None
            for p, (k0, kn, kind) in zip(ps, keys):
                part = nn(vt_ref[0, :, k0 : k0 + kn], (p * inv).astype(BF))
                acc = part if acc is None else acc + part
            outs.append(acc)
        o = jnp.concatenate(outs, axis=0).T.astype(BF)
        for a, cnt, dst in geo.spread(me, q0):
            o_ref[pl.ds(dst, cnt), :] = o[a : a + cnt, :]


def hidden_kernel(geo, natt, s_ref, *refs):
    pieces = geo.pieces()
    np_ = len(pieces)
    atts = refs[:natt]
    toks = refs[natt : natt + np_]
    mine_ref, other_ref, gain_ref = refs[natt + np_ : natt + np_ + 3]
    hid_ref, x_ref, w_ref = refs[natt + np_ + 3 :]
    half = mine_ref.shape[0] // geo.n
    for m in range(geo.n):
        own = pl.multiple_of((2 * m + s_ref[0]) * half, 64)
        sib = pl.multiple_of((2 * m + 1 - s_ref[0]) * half, 64)
        w_ref[pl.ds(own, half), :] = mine_ref[m * half : (m + 1) * half, :]
        w_ref[pl.ds(sib, half), :] = other_ref[m * half : (m + 1) * half, :]
    gain = gain_ref[...].astype(F32)
    index = {}
    k = 0
    for g in range(geo.G):
        for m, off, rows in att_pieces(geo):
            index[(m, g, off)] = (atts[k], off, rows)
            k += 1

    def att_rows(m, g, row, cnt):
        for (mm, gg, _), (ref, off, rows) in index.items():
            if mm == m and gg == g and off <= row and row + cnt <= off + rows:
                return ref[row - off : row - off + cnt, :]
        raise ValueError("piece")

    for (j, off, rows), tok in zip(pieces, toks):
        lhs = jnp.concatenate(
            [
                att_rows(m, g, (m ^ j) * geo.T + off, rows)
                for m in range(geo.n)
                for g in range(geo.G)
            ],
            axis=1,
        )
        h = tok[...].astype(F32) + nn(lhs, w_ref[...])
        if j == 0:
            hid_ref[...] = h
        r = lax.rsqrt(jnp.mean(h * h, axis=-1, keepdims=True) + EPS)
        x_ref[j * geo.T + off : j * geo.T + off + rows, :] = (h * r * gain).astype(BF)


def att_pieces(geo):
    rows = geo.n * geo.T
    out = [(m, 0, rows) for m in range(geo.n)]
    if geo.relay:
        out = out[:-1] + [(3, 0, rows // 2), (3, rows // 2, rows // 2)]
    return out


CH = 1


def expert_rows(x, dout, wg, wu, wd, gate):
    g = nn(x, wg)
    u = nn(x, wu)
    back = nt(dout, wd) * gate
    s = 1.0 / (1.0 + jnp.exp(-g))
    sil = g * s
    act = (sil * u * gate).astype(BF)
    gg = (back * u * (s + sil * (1.0 - s))).astype(BF)
    ug = (back * sil).astype(BF)
    return act, gg, ug


def gate_column(gm_ref, expert):
    lane = iota(gm_ref.shape, 1)
    mine = (lane == expert) | (lane == EXPERTS + expert) | (lane == 2 * EXPERTS + expert)
    return jnp.sum(jnp.where(mine, gm_ref[...].astype(F32), 0.0), axis=1, keepdims=True)


def put_grads(outs, x_ref, do_ref, gg_ref, ug_ref, ac_ref):
    cols = x_ref.shape[1] // len(outs)
    for k, out in enumerate(outs):
        x = x_ref[:, k * cols : (k + 1) * cols]
        out[0] = tn(x, gg_ref[...]).astype(BF)
        out[1] = tn(x, ug_ref[...]).astype(BF)
        out[2] = tn(do_ref[:, k * cols : (k + 1) * cols], ac_ref[...]).astype(BF)


def expert_kernel(n, T, E, e, s_ref, *refs):
    x_ref, do_ref, gm_ref, wg_ref, wu_ref, wd_ref, xc_ref, dc_ref = refs[:8]
    act_ref, gg_ref, ug_ref, send = refs[-7 - CH : -3 - CH]
    keeps = refs[-3 - CH : -3]
    gg_s, ug_s, ac_s = refs[-3:]
    r = pl.program_id(0)

    @pl.when(r < n)
    def _():
        act, gg, ug = expert_rows(
            x_ref[...],
            do_ref[...],
            wg_ref[0],
            wu_ref[0],
            wd_ref[0],
            gate_column(gm_ref, s_ref[1] * E + e),
        )
        rows = pl.ds(pl.multiple_of(r * T, 128), T)
        gg_s[rows, :] = gg
        ug_s[rows, :] = ug
        ac_s[rows, :] = act
        act_ref[...] = act
        gg_ref[...] = gg
        ug_ref[...] = ug

    @pl.when(r == n)
    def _():
        put_grads([send], xc_ref, dc_ref, gg_s, ug_s, ac_s)

    @pl.when(r == n + 1)
    def _():
        put_grads(keeps, xc_ref, dc_ref, gg_s, ug_s, ac_s)


def expert(n, T, E, e, scal, x, dout, wg, wu, wd, kept):
    D, M = wg.shape[1:]
    row = lambda r, c: (jnp.minimum(r, n - 1), 0)
    gate = lambda r, c: (jnp.minimum(r, n - 1), D // 128)
    half = lambda r, c: (0, jnp.where(r == n + 1, c[0], 1 - c[0]))
    fix = lambda r, c: (e, 0, 0)
    whole = lambda r, c: (0, 0, 0)
    block = pl.BlockSpec((T, M), lambda r, c: (jnp.minimum(r, n - 1), e))
    in_specs = [
        pl.BlockSpec((T, D), row),
        pl.BlockSpec((T, D), row),
        pl.BlockSpec((T, 128), gate),
        pl.BlockSpec((1, D, M), fix),
        pl.BlockSpec((1, D, M), fix),
        pl.BlockSpec((1, M, D), fix),
        pl.BlockSpec((n * T, D // 2), half),
        pl.BlockSpec((n * T, D // 2), half),
    ]
    args = [x, dout, dout, wg, wu, wd, x, dout]
    alias = {}
    if kept is not None:
        in_specs += [pl.BlockSpec(memory_space=pl.ANY)] * 3
        args += list(kept)
        alias = {9: 0, 10: 1, 11: 2}
    out = call(
        functools.partial(expert_kernel, n, T, E, e),
        (pltpu.HBM((n * T, E * M), BF),) * 3
        + (shape((3, D // 2, M), BF),)
        + (shape((3, D // 2 // CH, M), BF),) * CH,
        12 * n * T * D * M,
        20e6,
        grid_spec=pltpu.PrefetchScalarGridSpec(
            num_scalar_prefetch=1,
            grid=(n + 2,),
            in_specs=in_specs,
            out_specs=(block,) * 3
            + (pl.BlockSpec((3, D // 2, M), whole),)
            + (pl.BlockSpec((3, D // 2 // CH, M), whole),) * CH,
            scratch_shapes=[pltpu.VMEM((n * T, M), BF)] * 3,
        ),
        input_output_aliases=alias,
        name=f"expert{e}",
    )(scal, *args)
    return out[:3], out[3], out[4:]


def forward_kernel(E, e0, s_ref, x_ref, do_ref, gm_ref, wg_ref, wu_ref, wd_ref, *refs):
    act_ref, gg_ref, ug_ref = refs[-3:]
    act, gg, ug = expert_rows(
        x_ref[...],
        do_ref[...],
        wg_ref[0],
        wu_ref[0],
        wd_ref[0],
        gate_column(gm_ref, s_ref[1] * E + e0 + pl.program_id(0)),
    )
    act_ref[...] = act
    gg_ref[...] = gg
    ug_ref[...] = ug


def forwards(n, T, E, e0, scal, x, dout, wg, wu, wd, kept):
    D, M = wg.shape[1:]
    R = n * T // 2
    any_ = pl.BlockSpec(memory_space=pl.ANY)
    row = pl.BlockSpec((R, D), lambda i, r, c: (r, 0))
    fix = lambda i, r, c: (e0 + i, 0, 0)
    block = pl.BlockSpec((R, M), lambda i, r, c: (r, e0 + i))
    return call(
        functools.partial(forward_kernel, E, e0),
        (pltpu.HBM((n * T, E * M), BF),) * 3,
        6 * (E - e0) * n * T * D * M,
        (E - e0) * 12e6,
        grid_spec=pltpu.PrefetchScalarGridSpec(
            num_scalar_prefetch=1,
            grid=(E - e0, 2),
            in_specs=[
                row,
                row,
                pl.BlockSpec((R, 128), lambda i, r, c: (r, D // 128)),
                pl.BlockSpec((1, D, M), fix),
                pl.BlockSpec((1, D, M), fix),
                pl.BlockSpec((1, M, D), fix),
                any_,
                any_,
                any_,
            ],
            out_specs=(block,) * 3,
        ),
        input_output_aliases={7: 0, 8: 1, 9: 2},
        name="forwards",
    )(scal, x, dout, dout, wg, wu, wd, *kept)


def input_grad_kernel(E, T, gg_ref, ug_ref, wg_ref, wu_ref, *refs):
    outs, acc = refs[:-1], refs[-1]
    i = pl.program_id(0)
    v = nt(gg_ref[...], wg_ref[0]) + nt(ug_ref[...], wu_ref[0])

    @pl.when(i == 0)
    def _():
        acc[...] = v

    @pl.when(i > 0)
    def _():
        acc[...] += v

    @pl.when(i == E - 1)
    def _():
        put_blocks(T, acc, outs)


def input_grad(T, E, first, rows, gg, ug, wg, wu):
    D, M = wg.shape[1:]
    R = sum(rows)
    block = pl.BlockSpec((R, M), lambda i: (first // R, i))
    weight = pl.BlockSpec((1, D, M), lambda i: (i, 0, 0))
    return call(
        functools.partial(input_grad_kernel, E, T),
        tuple(shape((v, D), BF) for v in rows),
        4 * E * R * D * M,
        16e6,
        grid=(E,),
        in_specs=[block, block, weight, weight],
        out_specs=tuple(pl.BlockSpec((v, D), lambda i: (0, 0)) for v in rows),
        scratch_shapes=[pltpu.VMEM((R, D), F32)],
        name=f"input_grad{first}",
    )(gg, ug, wg, wu)


def weight_grad_kernel(s_ref, x_ref, do_ref, gg_ref, ug_ref, ac_ref, send, *keeps):
    @pl.when(pl.program_id(0) == 0)
    def _():
        put_grads([send], x_ref, do_ref, gg_ref, ug_ref, ac_ref)

    @pl.when(pl.program_id(0) == 1)
    def _():
        put_grads(keeps, x_ref, do_ref, gg_ref, ug_ref, ac_ref)


def weight_grad(M, e, scal, x, dout, act, gg, ug):
    R, D = x.shape
    half = lambda s, c: (0, jnp.where(s == 1, c[0], 1 - c[0]))
    whole = lambda s, c: (0, 0, 0)
    block = pl.BlockSpec((R, M), lambda s, c: (0, e))
    out = call(
        weight_grad_kernel,
        (shape((3, D // 2, M), BF),) + (shape((3, D // 2 // CH, M), BF),) * CH,
        6 * R * D * M,
        14e6,
        grid_spec=pltpu.PrefetchScalarGridSpec(
            num_scalar_prefetch=1,
            grid=(2,),
            in_specs=[
                pl.BlockSpec((R, D // 2), half),
                pl.BlockSpec((R, D // 2), half),
                block,
                block,
                block,
            ],
            out_specs=(pl.BlockSpec((3, D // 2, M), whole),)
            + (pl.BlockSpec((3, D // 2 // CH, M), whole),) * CH,
        ),
        name=f"weight_grad{e}",
    )(scal, x, dout, gg, ug, act)
    return out[0], out[1:]


def norm_back_kernel(count, low, *refs):
    parts = refs[:count]
    base_ref, v_ref, gain_ref = refs[count : count + 3]
    outs = refs[count + 3 :]
    grad = parts[0][...].astype(F32)
    for p in parts[1:]:
        grad = grad + p[...].astype(F32)
    v = v_ref[...].astype(F32)
    r = lax.rsqrt(jnp.mean(v * v, axis=-1, keepdims=True) + EPS)
    gv = gain_ref[...].astype(F32) * grad
    res = (
        base_ref[...].astype(F32)
        + r * gv
        - v * (r * r * r * jnp.mean(gv * v, axis=-1, keepdims=True))
    )
    outs[0][...] = res
    if low:
        outs[1][...] = res.astype(BF)
        part = jnp.sum(grad * v * r, axis=0, keepdims=True)

        @pl.when(pl.program_id(0) == 0)
        def _():
            outs[2][...] = part

        @pl.when(pl.program_id(0) > 0)
        def _():
            outs[2][...] += part


def norm_back(parts, base, v, gain, low):
    T, D = v.shape
    B = 128
    row = pl.BlockSpec((B, D), lambda i: (i, 0))
    one = pl.BlockSpec((1, D), lambda i: (0, 0))
    out = [shape((T, D), F32)]
    specs = [row]
    if low:
        out += [shape((T, D), BF), shape((1, D), F32)]
        specs += [row, one]
    return call(
        functools.partial(norm_back_kernel, len(parts), low),
        tuple(out),
        20 * T * D,
        T * D * 16,
        grid=(T // B,),
        in_specs=[row] * len(parts) + [row, row, one],
        out_specs=tuple(specs),
        name="norm_back",
    )(*parts, base, v, gain)


def att_back_kernel(geo, gi, me_ref, *refs):
    pieces = geo.pieces()
    np_ = len(pieces)
    brs = refs[:np_]
    (w_ref, q_ref, kd_ref, kt_ref, vd_ref, lse_ref, segc_ref, segr_ref, c_ref, s_ref) = refs[
        np_ : np_ + 10
    ]
    out_ref, do_s, dk_s, dv_s, dq_s = refs[np_ + 10 :]
    me = me_ref[0]
    for (m, off, rows), br in zip(pieces, brs):
        y = nt(br[...], w_ref[...])
        low = iota((rows, 128), 1) < 64
        lo = jnp.where(low, y, 0.0).astype(BF)
        hi = jnp.where(low, 0.0, y).astype(BF)
        for a, cnt, dst in geo.places(me, m, off, rows):
            do_s[0, pl.ds(dst, cnt), :] = lo[a : a + cnt, :]
            do_s[1, pl.ds(dst, cnt), :] = hi[a : a + cnt, :]
    dk_s[...] = jnp.zeros_like(dk_s)
    dv_s[...] = jnp.zeros_like(dv_s)

    def head(i, carry):
        g = 0
        for q0, keys in geo.tiles():
            q = q_ref[i, q0 : q0 + TILE, :]
            do = do_s[i, q0 : q0 + TILE, :]
            lse = lse_ref[i, :, q0 : q0 + TILE]
            ps, dps = [], []
            delta = None
            for k0, kn, kind in keys:
                s = masked(nt(kd_ref[g, k0 : k0 + kn, :], q), kind, q0, k0, segc_ref, segr_ref)
                p = jnp.exp(s - lse)
                dp = nt(vd_ref[g, k0 : k0 + kn, :], do)
                dv_s[g, k0 : k0 + kn, :] += nn(p.astype(BF), do)
                d = jnp.sum(p * dp, axis=0, keepdims=True)
                delta = d if delta is None else delta + d
                ps.append(p)
                dps.append(dp)
            acc = None
            for p, dp, (k0, kn, kind) in zip(ps, dps, keys):
                ds = (p * (dp - delta)).astype(BF)
                dk_s[g, k0 : k0 + kn, :] += nn(ds, q)
                part = nn(kt_ref[g, :, k0 : k0 + kn], ds)
                acc = part if acc is None else acc + part
            dq_s[i, :, q0 : q0 + TILE] = acc
        return carry

    lax.fori_loop(0, 2, head, 0)
    low = iota((TILE, 128), 1) < 64
    for t in range(0, geo.TG, TILE):
        rows = slice(t, t + TILE)
        cos, sin = c_ref[rows, :], s_ref[rows, :]
        v = jnp.concatenate([dq_s[0, :, rows], dq_s[1, :, rows]], axis=0).T * 0.125
        dq = v * cos - swap_halves(v) * sin
        k = dk_s[0, rows, :]
        k = k + pltpu.roll(k, 64, 1)
        k = k * cos - swap_halves(k) * sin
        v = dv_s[0, rows, :]
        for x, col in enumerate((dq, jnp.where(low, k, v + pltpu.roll(v, 64, 1)))):
            y = col.astype(BF)
            for a, cnt, dst in geo.spread(me, t):
                out_ref[pl.ds(dst, cnt), x * 128 : x * 128 + 128] = y[a : a + cnt, :]


def mix_kernel(T, act_ref, w_ref, *refs):
    outs, acc = refs[:-1], refs[-1]
    i = pl.program_id(0)
    v = nn(act_ref[...], w_ref[0])

    @pl.when(i == 0)
    def _():
        acc[...] = v

    @pl.when(i > 0)
    def _():
        acc[...] += v

    @pl.when(i == pl.num_programs(0) - 1)
    def _():
        put_blocks(T, acc, outs)


def mix_parts(n, T, rows, act, wd):
    E, M, D = wd.shape
    return call(
        functools.partial(mix_kernel, T),
        (shape((T, D), F32),) + tuple(shape((v, D), BF) for v in rows[1:]),
        2 * n * T * E * M * D,
        10e6,
        grid=(E,),
        in_specs=[
            pl.BlockSpec((n * T, M), lambda i: (0, i)),
            pl.BlockSpec((1, M, D), lambda i: (i, 0, 0)),
        ],
        out_specs=tuple(pl.BlockSpec((v, D), lambda i: (0, 0)) for v in rows),
        scratch_shapes=[pltpu.VMEM((n * T, D), F32)],
        name="mix",
    )(act, wd)


def back_kernel(T, G, w_ref, *refs):
    ys, outs = refs[:G], refs[G:]
    at = 0
    for out in outs:
        rows = out.shape[0]
        v = None
        for g, y in enumerate(ys):
            p = nt(y[at : at + rows, :], w_ref[:, g * 256 : (g + 1) * 256])
            v = p if v is None else v + p
        out[...] = v.astype(BF)
        at += rows


def head_grad_kernel(geo, first, s_ref, x_ref, y_ref, w_ref, gf_ref, *outs):
    me = s_ref[1]
    r = w_ref.shape[0] // geo.n
    ones = jnp.ones((16, 256), BF)
    row = iota((16, 256), 0)
    for j in range(geo.n):
        dw = tn(x_ref[:, j * r : (j + 1) * r], y_ref[...])
        prod = dw * w_ref[j * r : (j + 1) * r, :].astype(F32)
        hi = prod.astype(BF)
        lo = (prod - hi.astype(F32)).astype(BF)
        gain = nt(ones, hi) + nt(ones, lo)
        below = gf_ref[:, j * r : (j + 1) * r] if first else jnp.zeros((1, r), F32)
        if r < 256:
            gain = jnp.concatenate([gain, jnp.zeros((16, 256 - r), F32)], axis=1)
            below = jnp.concatenate([below, jnp.zeros((1, 256 - r), F32)], axis=1)
        extra = jnp.where(row == 0, gain, jnp.where(row == 1, below, 0.0)).astype(BF)
        low = dw.astype(BF)
        for m, out in enumerate(outs):

            @pl.when((me ^ m) == j)
            def _():
                out[:r, :] = low
                out[r:, :] = extra


def out_grad_kernel(np_, G, s_ref, *refs):
    brs, atts = refs[:np_], refs[np_ : np_ + G]
    send, keep = refs[np_ + G], refs[np_ + G + 1]
    per = []
    for o in atts:
        v, at_ = None, 0
        for br in brs:
            rows = br.shape[0]
            p = tn(o[at_ : at_ + rows, :], br[...])
            v = p if v is None else v + p
            at_ += rows
        per.append(v)
    v = jnp.concatenate(per, axis=0).astype(BF)
    lead, rows = send.shape[0], send.shape[1]
    half = v.shape[0] // 2
    count = rows // half

    def put(out, top):
        for a in range(lead):
            for b in range(count):
                c = (a * count + b) * 256
                out[a, b * half : (b + 1) * half, :] = v[top : top + half, c : c + 256]

    @pl.when(s_ref[0] == 0)
    def _():
        put(keep, 0)
        put(send, half)

    @pl.when(s_ref[0] == 1)
    def _():
        put(keep, half)
        put(send, 0)


def combine_kernel(ops, wide, k, *refs):
    end = (refs[0][0] == 0) | (refs[0][0] == refs[0][1])
    ins, outs = refs[1 : 1 + k], refs[len(refs) - len(ops) :]

    def plus(a, b):
        return (ins[a][...].astype(F32) + ins[b][...].astype(F32)).astype(BF)

    for (kind, *at), w, out in zip(ops, wide, outs):

        def work():
            if kind == "add":
                out[...] = plus(*at)
                return

            @pl.when(end)
            def _():
                out[...] = plus(*at[:2]) if kind == "merge" else ins[at[0]][...]

            @pl.when(jnp.logical_not(end))
            def _():
                out[...] = plus(*at[2:]) if kind == "merge" else ins[at[1]][...]

        if w:
            work()
        else:
            pl.when((pl.program_id(0) == 0) & (pl.program_id(1) == 0))(work)


def combine(pos, ops):
    arrays, specs, keys, coded, outs, out_specs, wide = [], [], [], [], [], [], []

    def spec(w, block, part):
        if w:
            half = (1, block[0] // 2, block[1])
            return pl.BlockSpec(half, lambda i, h, p: (i, 2 * part + h, 0))
        return pl.BlockSpec(block, lambda i, h, p: (0,) * len(block))

    for kind, args, place in ops:
        a = args[0][0]
        w = a.shape[0] == 3
        block = a.shape[1:] if w else a.shape
        at = []
        for v, part in args:
            key = (id(v), part)
            if key not in keys:
                keys.append(key)
                arrays.append(v)
                specs.append(spec(w, block, part))
            at.append(keys.index(key))
        coded.append((kind, *at))
        wide.append(w)
        if place is None:
            outs.append(shape(a.shape, BF))
            out_specs.append(spec(w, block, 0))
        else:
            outs.append(shape((3, CH * block[0], block[1]), BF))
            out_specs.append(spec(w, block, place[1]))
    k = len(arrays)
    alias = {}
    for i, (_, _, place) in enumerate(ops):
        if place is not None and place[0] is not None:
            alias[1 + len(arrays)] = i
            arrays.append(place[0])
            specs.append(pl.BlockSpec(memory_space=pl.ANY))
    out = call(
        functools.partial(combine_kernel, coded, wide, k),
        tuple(outs),
        1e6,
        1e6,
        grid_spec=pltpu.PrefetchScalarGridSpec(
            num_scalar_prefetch=1,
            grid=(3, 2),
            in_specs=specs,
            out_specs=tuple(out_specs),
        ),
        input_output_aliases=alias,
        name="combine",
    )(pos, *arrays)
    return list(out)


def relay_kernel(h, near_ref, far_ref, a_ref, b_ref, near_out, far_out):
    near_out[:h, :] = near_ref[:h, :]
    near_out[h:, :] = (near_ref[h:, :].astype(F32) + a_ref[...].astype(F32)).astype(BF)
    far_out[:h, :] = (far_ref[:h, :].astype(F32) + b_ref[...].astype(F32)).astype(BF)
    far_out[h:, :] = far_ref[h:, :]


def relay_add(p1, p2, a, b):
    T, D = p1.shape
    return call(
        functools.partial(relay_kernel, T // 2),
        (shape((T, D), BF),) * 2,
        1e6,
        4e6,
        in_specs=[VM] * 4,
        out_specs=(VM,) * 2,
        name="relay_add",
    )(p1, p2, a, b)


def put_blocks(T, acc, outs, first=0):
    at = first
    for out in outs:
        rows = out.shape[0]
        out[...] = acc[at : at + rows, :].astype(out.dtype)
        at += rows


def finish_kernel(e, first, c_ref, own_ref, sib_ref, *refs):
    g_ref, u_ref, d_ref = refs if first else refs[3:]

    def put(src):
        g_ref[0] = src[0].astype(F32)
        u_ref[0] = src[1].astype(F32)
        d_ref[0] = src[2].astype(F32).T

    @pl.when(pl.program_id(0) < 2)
    def _():
        put(own_ref)

    @pl.when(pl.program_id(0) >= 2)
    def _():
        put(sib_ref)


def finish(e, E, core, own, sib, prev):
    _, Dh, M = own.shape
    rows = Dh // 2
    first = prev is None
    half = lambda s, c: jnp.where(s < 2, 2 * c[0] + s, 2 * (1 - c[0]) + s - 2)
    any_ = pl.BlockSpec(memory_space=pl.ANY)
    return call(
        functools.partial(finish_kernel, e, first),
        (
            shape((E, 2 * Dh, M), F32),
            shape((E, 2 * Dh, M), F32),
            shape((E, M, 2 * Dh), F32),
        ),
        1e6,
        10e6,
        grid_spec=pltpu.PrefetchScalarGridSpec(
            num_scalar_prefetch=1,
            grid=(4,),
            in_specs=[
                pl.BlockSpec((3, rows, M), lambda s, c: (0, jnp.minimum(s, 1), 0)),
                pl.BlockSpec((3, rows, M), lambda s, c: (0, jnp.maximum(s - 2, 0), 0)),
            ]
            + ([] if first else [any_] * 3),
            out_specs=(
                pl.BlockSpec((1, rows, M), lambda s, c: (e, half(s, c), 0)),
                pl.BlockSpec((1, rows, M), lambda s, c: (e, half(s, c), 0)),
                pl.BlockSpec((1, M, rows), lambda s, c: (e, 0, half(s, c))),
            ),
        ),
        input_output_aliases={} if first else {3: 0, 4: 1, 5: 2},
        name=f"finish{e}",
    )(core, own, sib, *([] if first else prev))


def per_device(
    tokens,
    d_out,
    routes,
    gates,
    segment,
    gain_attn,
    w_query,
    key_weight,
    value_weight,
    w_out,
    gain_ffn,
    w_gate,
    w_up,
    w_down,
):
    n = lax.axis_size("shard")
    me = lax.axis_index("shard")
    R = lax.axis_size("rep")
    rp = lax.axis_index("rep")
    core, pos = rp % 2, rp // 2
    T, D = tokens.shape
    geo = Geo(n, T, segment.shape[1])
    G, TG = geo.G, geo.TG
    E, _, M = w_gate.shape
    me1 = me.reshape(1).astype(jnp.int32)
    scal = jnp.stack([core, me]).astype(jnp.int32)

    def px(v, m):
        return lax.ppermute(v, "shard", [(i, i ^ m) for i in range(n)])

    def at(v, i):
        return lax.dynamic_index_in_dim(v, i, 0, keepdims=False)

    def near(v):
        return [v] + [px(v, m) for m in ((1, 2) if geo.relay else range(1, n))]

    def far(got):
        if not geo.relay:
            return list(got)
        v, a, b = got
        h = v.shape[0] // 2
        return [v, a, b, px(a[:h], 2), px(b[h:], 1)]

    def hbm(*vals):
        return [pltpu.with_memory_space_constraint(v, pltpu.HBM) for v in vals]

    def tie(vals, deps):
        vals, deps = tuple(vals), tuple(deps)
        return lax.optimization_barrier(vals + deps)[: len(vals)]

    L = R // 2

    def pz(v, pairs):
        return lax.ppermute(v, "rep", [(2 * a + k, 2 * b + k) for a, b in pairs for k in (0, 1)])

    def sib(v):
        return lax.ppermute(v, "rep", [(i, i ^ 1) for i in range(R)])

    pos1 = jnp.stack([pos, jnp.full((), L - 1)]).astype(jnp.int32)
    near_pairs = [(0, 1), (1, 0), (2, 3), (3, 2)]

    class Sums:
        def __init__(self):
            self.live, self.done, self.final = [], {}, {}

        def add(self, tag, keeps, send):
            if L != 4:
                both_ = jnp.stack([jnp.concatenate(keeps, axis=1), send])
                both_ = jnp.where(core == 0, both_, both_[::-1])
                both_ = lax.psum(both_, "rep")
                self.done[tag] = at(both_, core), at(both_, 1 - core)
                return
            new = sib(send)
            for k, keep in enumerate(keeps):
                self.live.append(
                    dict(tag=tag, part=k, parts=len(keeps), step=0, acc=keep, new=new)
                )

        def advance(self, vals, hold=(), starts=1):
            vals = tuple(vals)
            live = []
            for c in self.live:
                if c["tag"] in hold:
                    continue
                if c["step"] == 0:
                    if not starts:
                        continue
                    starts -= 1
                live.append(c)
            names = [(c, f) for c in live for f in ("acc", "new")]
            flat = []
            for c, f in names:
                if not any(c[f] is v for v in flat):
                    flat.append(c[f])
            got = lax.optimization_barrier(vals + tuple(flat))
            vals, fresh = got[: len(vals)], got[len(vals) :]
            for c, f in names:
                c[f] = next(b for a, b in zip(flat, fresh) if a is c[f])
            if not live:
                return vals
            ops, then = [], []
            into = [c for c in live if c["step"] == 0]
            out = [c for c in live if c["step"] == 2]

            def arrived(c):
                return [(c["acc"], 0), (c["new"], c["part"] if c["step"] == 0 else 0)]

            pairs = []
            for c in out:
                mate = next((d for d in into if d["acc"].shape == c["acc"].shape), None)
                if mate is not None:
                    into.remove(mate)
                pairs.append((mate, c))
            pairs += [(d, None) for d in into]
            for c in live:
                if c["step"] == 3:
                    whole = self.final.get(c["tag"])
                    place = None if c["parts"] == 1 else (whole, c["part"])
                    ops.append(("take", [(c["new"], 0), (c["acc"], 0)], place))
                    then.append(("done", c))
                elif c["step"] == 1:
                    ops.append(("add", arrived(c), None))
                    then.append(("mid", c))
            for d, c in pairs:
                if c is None:
                    ops.append(("add", arrived(d), None))
                    then.append(("in", d))
                elif d is None:
                    ops.append(("add", arrived(c), None))
                    then.append(("out", c))
                else:
                    ops.append(("add", arrived(d), None))
                    then.append(("acc", d))
                    ops.append(("merge", arrived(d) + arrived(c), None))
                    then.append(("both", d, c))
            res = combine(pos1, ops)
            waiting = [t for t, v in self.done.items() if len(v) == 1]
            got = lax.optimization_barrier(
                vals + tuple(res) + tuple(self.done[t][0] for t in waiting)
            )
            vals, res, old = (
                got[: len(vals)],
                got[len(vals) : len(vals) + len(res)],
                got[len(vals) + len(res) :],
            )
            for t, v in zip(waiting, old):
                self.done[t] = (v,)
            for (what, *cs), v in zip(then, res):
                c = cs[-1]
                if what == "done":
                    self.final[c["tag"]] = v
                    c["step"] = 4
                    if all(o["step"] == 4 or o["tag"] != c["tag"] for o in self.live):
                        self.done[c["tag"]] = (v,)
                elif what == "mid":
                    c.update(step=2, acc=v, new=pz(v, [(1, 2), (2, 1)]))
                elif what == "acc":
                    c.update(acc=v)
                elif what == "in":
                    c.update(step=1, acc=v, new=pz(v, [(0, 1), (3, 2)]))
                elif what == "out":
                    c.update(step=3, acc=v, new=pz(v, [(1, 0), (2, 3)]))
                else:
                    new = pz(v, near_pairs)
                    cs[0].update(step=1, new=new)
                    c.update(step=3, acc=v, new=new)
            self.live = [c for c in self.live if c["step"] < 4]
            return vals

        def whole(self, tag):
            if len(self.done[tag]) == 1:
                self.done[tag] = (*self.done[tag], sib(*self.done[tag]))
            return self.done[tag]

    sums = Sums()

    def scatter(parts):
        return [parts[0]] + [px(parts[m], m) for m in range(n - 1, 0, -1)]

    def scatter_near(parts):
        if not geo.relay:
            return scatter(parts)
        p0, p1, p2, upper, lower = parts
        return [p0, p1, p2, px(upper, 1), px(lower, 2)]

    def scatter_far(came):
        if not geo.relay:
            return list(came)
        p0, p1, p2, a, b = came
        p1, p2 = relay_add(p1, p2, b, a)
        p0, *_ = tie((p0,), (p1, p2))
        return [p0, px(p1, 1), px(p2, 2)]

    halves = [T] * n if not geo.relay else [T] * (n - 1) + [T // 2] * 2

    r = w_query.shape[0]
    W = G * 256
    segc, segr = segment.reshape(-1, 1), segment
    near_tok = near(tokens)
    wmsg = call(
        functools.partial(columns_kernel, geo),
        (shape((r + 16, W), BF),) * n,
        1e6,
        2e6,
        in_specs=[SM] + [VM] * 5,
        out_specs=(VM,) * n,
        name="columns",
    )(me1, w_query, key_weight, value_weight, gain_attn.reshape(1, r), gain_ffn.reshape(1, r))
    got_w = [wmsg[0]] + [px(wmsg[m], m) for m in range(1, n)]
    dmsg, cos4, sin4 = call(
        pack_kernel,
        (shape((T, D + 128), BF), shape((TG, 128), F32), shape((TG, 128), F32)),
        1e6,
        2e6,
        in_specs=[VM] * 5,
        out_specs=(VM,) * 3,
        name="pack",
    )(d_out, routes, gates, segc, segr)
    wo_own = at(w_out.reshape(2, r // 2, D), core)
    dmsg, cos4, wo_own, *near_tok = tie((dmsg, cos4, wo_own, *near_tok), ())
    tok = far(near_tok)
    near_wo = near(wo_own)
    dmsg, *rest = tie((dmsg, *tok, *near_wo, *got_w), ())
    np_ = len(tok)
    tok, near_wo, got_w = rest[:np_], rest[np_ : -n], rest[-n:]
    near_d = near(dmsg)
    wo_half = far(near_wo)

    normed, q, kd, vd, kt, vt, w_cols, gain_a, gain_f = call(
        functools.partial(qkv_kernel, geo),
        (
            shape((n * T, D), BF),
            shape((2 * G, TG, 128), BF),
            shape((G, TG, 128), BF),
            shape((G, TG, 128), BF),
            shape((G, 64, TG), BF),
            shape((G, 64, TG), BF),
            shape((D, W), BF),
            shape((1, D), F32),
            shape((1, D), F32),
        ),
        2 * TG * D * W,
        12e6,
        in_specs=[SM] + [VM] * (np_ + n + 2),
        out_specs=(VM,) * 9,
        scratch_shapes=[pltpu.VMEM((TG, W), F32)],
        name="qkv",
    )(me1, *tok, *got_w, cos4, sin4)

    atts, lses, own_att = [], [], []
    near_o = None
    for g in range(G):
        o, lse = call(
            functools.partial(att_kernel, geo),
            (shape((n * T, 128), BF), shape((2, 1, TG), F32)),
            1e9,
            3e6,
            2 * TG * TG * 0.6,
            grid=(1,),
            in_specs=[
                SM,
                pl.BlockSpec((2, TG, 128), lambda i, g=g: (g, 0, 0)),
                pl.BlockSpec((1, TG, 128), lambda i, g=g: (g, 0, 0)),
                pl.BlockSpec((1, 64, TG), lambda i, g=g: (g, 0, 0)),
                VM,
                VM,
            ],
            out_specs=(VM, VM),
            name=f"attend{g}",
        )(me1, q, kd, vt, segc, segr)
        own_att.append(o)
        lses.append(lse)
        if g == 0:
            k = len(near_d)
            o, q, *rest = tie((o, q, *near_d, *wo_half), ())
            near_d, wo_half = rest[:k], rest[k:]
            wo_mine = jnp.concatenate(wo_half, axis=0)
            wo_sib = sib(wo_mine)
            near_o = near(o)
        else:
            o, *near_o = tie((o, *near_o), ())
            atts += far(near_o)
            near_o = near(o)
    near_d, near_o = list(near_d), list(near_o)
    wo_mine, wo_sib, *rest = tie((wo_mine, wo_sib, *near_d, *near_o, *atts), ())
    k = len(near_d)
    near_d, near_o, atts = rest[:k], rest[k : k + len(near_o)], rest[k + len(near_o) :]
    atts += far(near_o)
    douts = far(near_d)
    lse = jnp.concatenate(lses, axis=0)

    hidden, x = call(
        functools.partial(hidden_kernel, geo, len(atts)),
        (shape((T, D), F32), shape((n * T, D), BF)),
        2 * TG * D * D,
        16e6,
        in_specs=[SM] + [VM] * (len(atts) + np_ + 3),
        out_specs=(VM,) * 2,
        scratch_shapes=[pltpu.VMEM((D, D), BF)],
        name="hidden",
    )(scal, *atts, *tok, wo_mine, wo_sib, gain_f)
    x, *douts = tie((x, *douts), ())
    dout = jnp.concatenate(douts, axis=0)

    w_gate, w_up, w_down = hbm(w_gate, w_up, w_down)
    early = E // 2
    kept = None
    for e in range(early):
        kept, send, keeps = expert(n, T, E, e, scal, x, dout, w_gate, w_up, w_down, kept)
        kept = hbm(*kept)
        sums.add(e, keeps, send)
        if e == 0:
            x, *kept = sums.advance((x, *kept))
    kept = hbm(*forwards(n, T, E, early, scal, x, dout, w_gate, w_up, w_down, kept))
    x, act, gg, ug = sums.advance((x, *kept))

    def weights(e, x, act, gg, ug):
        send, keeps = weight_grad(M, e, scal, x, dout, act, gg, ug)
        sums.add(e, keeps, send)
        return tie((x, act, gg, ug), (send,))

    parts = {}
    (parts[n - 1],) = input_grad(T, E, (n - 1) * T, [T], gg, ug, w_gate, w_up)
    far_part = px(parts[n - 1], n - 1)
    gg, x, _ = tie((gg, x, parts[n - 1]), ())
    x, act, gg, ug = weights(early, x, act, gg, ug)
    if n == 4:
        first = input_grad(T, E, 0, [T] * (n - 1), gg, ug, w_gate, w_up)
    else:
        first = [
            v
            for m in range(n - 1)
            for v in input_grad(T, E, m * T, [T], gg, ug, w_gate, w_up)
        ]
    *first, far_part, x, act, gg, ug = sums.advance((*first, far_part, x, act, gg, ug))
    came = [first[0], far_part] + [px(first[m], m) for m in range(n - 2, 0, -1)]
    rest = []
    for e in range(early + 1, E):
        send, keeps = weight_grad(M, e, scal, x, dout, act, gg, ug)
        rest += [send, *keeps]
    k = len(came)
    came = tie((*came, act, *rest), ())
    came, act, rest = came[:k], came[k], came[k + 1 :]
    for e in range(early + 1, E):
        sums.add(e, rest[1 : 1 + CH], rest[0])
        rest = rest[1 + CH :]

    hidden_grad, branch, gain_f_part = norm_back(came, d_out, hidden, gain_f, True)
    (act,) = tie((act,), (branch,))
    branches = near(branch)
    mix = sums.advance((*mix_parts(n, T, [T] * n, act, w_down), *branches))
    mix, branches = mix[:n], far(mix[n:])

    prev = None
    finished = 0

    def finishing(most):
        nonlocal prev, finished
        while finished < most and finished in sums.done:
            prev = finish(finished, E, scal, *sums.whole(finished), prev)
            finished += 1

    def tie_finished(vals):
        nonlocal prev
        if prev is None:
            return tuple(vals)
        got = lax.optimization_barrier(tuple(vals) + tuple(prev))
        prev = got[-3:]
        return got[:-3]

    finishing(1)
    w_out_ = w_out
    nb = len(branches)
    *branches, q, kd = tie_finished((*branches, q, kd))
    mix = list(tie(mix, branches))
    mix_far = px(mix[n - 1], n - 1)

    def attend_back(g, q, kd):
        return call(
            functools.partial(att_back_kernel, geo, g),
            shape((n * T, 256), BF),
            4e9 / G,
            8e6,
            4 * TG * TG * 0.6 / G,
            grid=(1,),
            in_specs=[SM]
            + [VM] * nb
            + [
                pl.BlockSpec((128, D), lambda i: (g, 0)),
                pl.BlockSpec((2, TG, 128), lambda i: (g, 0, 0)),
                pl.BlockSpec((1, TG, 128), lambda i: (g, 0, 0)),
                pl.BlockSpec((1, 64, TG), lambda i: (g, 0, 0)),
                pl.BlockSpec((1, TG, 128), lambda i: (g, 0, 0)),
                pl.BlockSpec((2, 1, TG), lambda i: (g, 0, 0)),
            ]
            + [VM] * 4,
            out_specs=VM,
            scratch_shapes=[
                pltpu.VMEM((2, TG, 128), BF),
                pltpu.VMEM((1, TG, 128), F32),
                pltpu.VMEM((1, TG, 128), F32),
                pltpu.VMEM((2, 64, TG), F32),
            ],
            name=f"attend_back{g}",
        )(me1, *branches, *hbm(w_out_, q, kd, kt, vd, lse, segc, segr, cos4, sin4))

    def head_grad(g, y):
        return call(
            functools.partial(head_grad_kernel, geo, g == 0),
            (shape((r + 16, 256), BF),) * n,
            1e9,
            4e6,
            grid=(1,),
            in_specs=[
                SM,
                VM,
                VM,
                pl.BlockSpec((D, 256), lambda i: (0, g)),
                VM,
            ],
            out_specs=(VM,) * n,
            name=f"head_grad{g}",
        )(scal, normed, y, w_cols, gain_f_part)

    lead = n // 2
    orows = r // 2 * (D // 256) // lead

    def add_small(g, arrived, out=None):
        got = jnp.stack(arrived).reshape(2, lead, r + 16, 256)
        keep, send = at(got, core), at(got, 1 - core)
        if out is not None:
            keep = jnp.concatenate([keep, out[1]], axis=1)
            send = jnp.concatenate([send, out[0]], axis=1)
        sums.add(("small", g), [keep], send)

    out = call(
        functools.partial(out_grad_kernel, nb, G),
        (shape((lead, orows, 256), BF),) * 2,
        1e9,
        4e6,
        in_specs=[SM] + [VM] * (nb + G),
        out_specs=(VM, VM),
        name="out_grad",
    )(scal, *branches, *own_att)
    ys = [attend_back(0, q, kd)]
    msgs = head_grad(0, ys[0])
    q, kd, mix_far, *got = sums.advance((q, kd, mix_far, *msgs, *out))
    msgs, out = got[:n], got[n:]
    arrived = [msgs[0]] + [px(msgs[m], m) for m in range(1, n)]
    if G == 2:
        ys.append(attend_back(1, q, kd))
    got = tie((*ys, *arrived), ())
    ys, arrived = got[:G], got[G:]
    add_small(0, arrived, out)
    arrived = []
    if G == 2:
        msgs = head_grad(1, ys[1])
        ys = tie(ys, msgs[:1])
        arrived = [msgs[0]] + [px(msgs[m], m) for m in range(1, n)]
    back = call(
        functools.partial(back_kernel, T, G),
        tuple(shape((v, D), BF) for v in halves),
        1e9,
        8e6,
        in_specs=[VM] * (1 + G),
        out_specs=(VM,) * len(halves),
        name="back",
    )(w_cols, *ys)
    came = scatter_near(back)
    k = len(came)
    got = sums.advance((*came, *arrived))
    came, arrived = scatter_far(got[:k]), got[k:]
    if G == 2:
        add_small(1, arrived)
    finishing(E // 2)
    (came[0],) = tie_finished(came[:1])
    big = tuple(range(E))
    (came[0],) = sums.advance(came[:1], hold=big)
    finishing(E - 1)
    came = tie_finished(came)
    k = len(came)
    got = sums.advance((*came, *mix))
    came, mix = got[:k], got[k:]
    mix = [mix[0], mix_far] + [px(mix[m], m) for m in range(n - 2, 0, -1)]
    (d_tokens,) = norm_back(came, hidden_grad, tokens, gain_a, False)
    d_tokens, hidden, *mix = sums.advance((d_tokens, hidden, *mix))
    mix_sum = hidden
    for v in mix:
        mix_sum = mix_sum + v.astype(F32)
    mixed = mix_sum.astype(BF)
    while sums.live:
        finishing(E)
        if prev is None:
            sums.advance(())
        else:
            prev = sums.advance(prev)
    finishing(E)
    g_gate, g_up, g_down = prev

    def both(tag):
        v, other = sums.whole(tag)
        return jnp.where(core == 0, jnp.stack([v, other]), jnp.stack([other, v])).astype(F32)

    small = [both(("small", g)) for g in range(G)]
    g_out_all = small[0][:, :, r + 16 :, :].reshape(2, D // 256, r // 2, 256)
    g_out_all = g_out_all.transpose(0, 2, 1, 3).reshape(r, D)
    small = [v[:, :, : r + 16].reshape(n, r + 16, 256) for v in small]
    in_order = [[at(v, me ^ j) for v in small] for j in range(n)]

    def pick(lo, hi):
        return jnp.concatenate([v[:r, lo:hi] for pair in in_order for v in pair], axis=1)

    g_q, g_k, g_v = pick(0, 128), pick(128, 192), pick(192, 256)
    g_ga = sum(jnp.sum(v[:, r, :r], axis=0) for v in small) / gain_attn.astype(F32)
    g_gf = jnp.sum(small[0][:, r + 1, :r], axis=0)
    return (mixed, d_tokens, g_ga, g_q, g_k, g_v, g_out_all, g_gf, g_gate, g_up, g_down)


def solution(mesh):
    rows = P(("rep", "shard"), None)
    own = P("shard", None)
    own3 = P("shard", None, None)
    vec = P("shard")
    return jax.shard_map(
        per_device,
        mesh=mesh,
        in_specs=(
            rows,
            rows,
            rows,
            rows,
            P("rep", None),
            vec,
            own,
            own,
            own,
            own,
            vec,
            own3,
            own3,
            own3,
        ),
        out_specs=(rows, rows, vec, own, own, own, own, vec, own3, own3, own3),
        check_vma=False,
    )
```

```python
import functools
import math

import jax
import jax.numpy as jnp
from jax import lax
from jax.experimental import pallas as pl
from jax.experimental.pallas import tpu as pltpu
from jax.sharding import PartitionSpec as P

QUERY_HEADS = 16
KEY_VALUE_HEADS = 8
HEAD = 64
EXPERTS = 16
PROMPT = 1024
EPS = 1e-06
F32 = jnp.float32
BF = jnp.bfloat16
TILE = 256
VMEM_LIMIT = 26 * 1024 * 1024


def nn(a, b):
    return lax.dot_general(a, b, (((1,), (0,)), ((), ())), preferred_element_type=F32)


def nt(a, b):
    return lax.dot_general(a, b, (((1,), (1,)), ((), ())), preferred_element_type=F32)


def tn(a, b):
    return lax.dot_general(a, b, (((0,), (0,)), ((), ())), preferred_element_type=F32)


COST = 0.25


def call(kernel, out_shape, flops, nbytes, trans=0, **kw):
    return pl.pallas_call(
        kernel,
        out_shape=out_shape,
        compiler_params=pltpu.CompilerParams(vmem_limit_bytes=VMEM_LIMIT),
        cost_estimate=pl.CostEstimate(
            flops=int(COST * flops), bytes_accessed=int(COST * nbytes), transcendentals=int(COST * trans)
        ),
        **kw,
    )


VM = pl.BlockSpec(memory_space=pltpu.VMEM)
SM = pl.BlockSpec(memory_space=pltpu.SMEM)


def shape(dims, dtype):
    return jax.ShapeDtypeStruct(dims, dtype)


class Geo:
    def __init__(self, n, rows, conts):
        self.n = n
        self.T = rows
        self.PS = PROMPT // n
        self.CT = conts
        self.CS = conts // n
        self.TG = PROMPT + conts
        self.G = KEY_VALUE_HEADS // n
        self.relay = n == 4

    def pieces(self):
        out = [(m, 0, self.T) for m in range(self.n)]
        if self.relay:
            half = self.T // 2
            out = out[:-1] + [(3, 0, half), (3, half, half)]
        return out

    def places(self, me, m, off, rows):
        j = me ^ m
        out = []
        lead = max(0, min(self.PS, off + rows) - off)
        if lead:
            out.append((0, lead, pl.multiple_of(j * self.PS + off, 32)))
        if rows > lead:
            start = off + lead - self.PS
            out.append((lead, rows - lead, pl.multiple_of(PROMPT + j * self.CS + start, 32)))
        return out

    def tiles(self):
        out = []
        for i in range(PROMPT // TILE):
            ks = [(0, i * TILE, 0)] if i else []
            out.append((i * TILE, ks + [(i * TILE, TILE, 1)]))
        for c in range(self.CT // TILE):
            ks = [(0, PROMPT, 0)]
            if c:
                ks.append((PROMPT + (c - 1) * TILE, TILE, 2))
            ks.append((PROMPT + c * TILE, TILE, 3))
            out.append((PROMPT + c * TILE, ks))
        return out

    def spread(self, me, start):
        out = []
        if start < PROMPT:
            step = min(self.PS, TILE)
            for a in range(0, TILE, step):
                j = (start + a) // self.PS
                off = (start + a) % self.PS
                out.append((a, step, pl.multiple_of((me ^ j) * self.T + off, 32)))
        else:
            step = min(self.CS, TILE)
            for a in range(0, TILE, step):
                j = (start - PROMPT + a) // self.CS
                off = (start - PROMPT + a) % self.CS
                out.append((a, step, pl.multiple_of((me ^ j) * self.T + self.PS + off, 32)))
        return out


def iota(dims, axis):
    return lax.broadcasted_iota(jnp.int32, dims, axis)


def swap_halves(v):
    lane = iota(v.shape, 1)
    first = (lane & 32) == 0
    return jnp.where(first, pltpu.roll(v, 96, 1), pltpu.roll(v, 32, 1))


def masked(s, kind, q0, k0, segc_ref, segr_ref):
    if kind == 0:
        return s
    ok = None
    if kind != 2:
        ok = iota(s.shape, 0) <= iota(s.shape, 1)
    if kind != 1:
        same = segc_ref[k0 - PROMPT : k0 - PROMPT + TILE, :] == segr_ref[:, q0 - PROMPT : q0 - PROMPT + TILE]
        ok = same if ok is None else ok & same
    return jnp.where(ok, s, -1e30)


def qkv_kernel(geo, me_ref, *refs):
    np_ = len(geo.pieces())
    toks = refs[:np_]
    n = geo.n
    msgs = refs[np_ : np_ + n]
    c_ref, s_ref = refs[np_ + n : np_ + n + 2]
    (normed_ref, q_ref, kd_ref, vd_ref, kt_ref, vt_ref, w_ref, ga_ref, gf_ref, raw) = refs[
        np_ + n + 2 :
    ]
    me = me_ref[0]
    G = geo.G
    r = msgs[0].shape[0] - 16
    for m, msg in enumerate(msgs):
        w_ref[pl.ds(pl.multiple_of((me ^ m) * r, 128), r), :] = msg[:r, :]
        gains = msg[r : r + 16, :].astype(F32)[:1, :]
        for j in range(n):

            @pl.when((me ^ m) == j)
            def _():
                ga_ref[:, j * r : (j + 1) * r] = gains[:, :r]
                gf_ref[:, j * r : (j + 1) * r] = gains[:, r : 2 * r]

    gain = ga_ref[...]
    for (m, off, rows), tok in zip(geo.pieces(), toks):
        v = tok[...].astype(F32)
        r = lax.rsqrt(jnp.mean(v * v, axis=-1, keepdims=True) + EPS)
        x = (v * r * gain).astype(BF)
        normed_ref[m * geo.T + off : m * geo.T + off + rows, :] = x
        y = nn(x, w_ref[...])
        for a, cnt, dst in geo.places(me, m, off, rows):
            raw[pl.ds(dst, cnt), :] = y[a : a + cnt, :]
    for t in range(0, geo.TG, TILE):
        rows = slice(t, t + TILE)
        cos, sin = c_ref[rows, :], s_ref[rows, :]
        low = iota((TILE, 128), 1) < 64
        for g in range(G):
            v = raw[rows, g * 256 : g * 256 + 128]
            q = (v * cos + swap_halves(v) * sin).astype(BF).astype(F32) * 0.125
            q_ref[2 * g, rows, :] = jnp.where(low, q, 0.0).astype(BF)
            q_ref[2 * g + 1, rows, :] = jnp.where(low, 0.0, q).astype(BF)
            kv = raw[rows, g * 256 + 128 : g * 256 + 256]
            vk = pltpu.roll(kv, 64, 1)
            k = jnp.where(low, kv, vk)
            k = (k * cos + swap_halves(k) * sin).astype(BF)
            v = jnp.where(low, vk, kv)
            kd_ref[g, rows, :] = k
            vd_ref[g, rows, :] = v.astype(BF)
            kt_ref[g, :, rows] = k.astype(F32).T[:64, :].astype(BF)
            vt_ref[g, :, rows] = v.T[:64, :].astype(BF)


def columns_kernel(geo, me_ref, wq_ref, wk_ref, wv_ref, ga_ref, gf_ref, *outs):
    me = me_ref[0]
    r = wq_ref.shape[0]
    low = iota((r, 128), 1) < 64
    gains = jnp.concatenate([ga_ref[...], gf_ref[...]], axis=1)
    gains = jnp.broadcast_to(gains, (16, gains.shape[1]))
    for j in range(geo.n):
        cols = []
        for g in range(geo.G):
            h = j * geo.G + g
            pair = slice(h // 2 * 128, h // 2 * 128 + 128)
            k = wk_ref[:, pair].astype(F32)
            v = wv_ref[:, pair].astype(F32)
            if h % 2 == 0:
                kv = jnp.where(low, k, pltpu.roll(v, 64, 1))
            else:
                kv = jnp.where(low, pltpu.roll(k, 64, 1), v)
            cols += [wq_ref[:, h * 128 : h * 128 + 128], kv.astype(BF)]
        block = jnp.concatenate(cols, axis=1)
        for m, out in enumerate(outs):

            @pl.when((me ^ m) == j)
            def _():
                out[:r, :] = block
                out[r:, :] = gains


def pack_kernel(d_ref, r_ref, g_ref, segc_ref, segr_ref, out_ref, c_ref, s_ref):
    D = d_ref.shape[1]
    out_ref[:, :D] = d_ref[...]
    lane = iota((d_ref.shape[0], 128), 1)
    gate = jnp.zeros(lane.shape, F32)
    for k in range(r_ref.shape[1]):
        hit = (lane & (EXPERTS - 1)) == r_ref[:, k : k + 1]
        gate = gate + jnp.where(hit, g_ref[:, k : k + 1], 0.0)
    top = gate.astype(BF).astype(F32)
    mid = (gate - top).astype(BF).astype(F32)
    low = gate - top - mid
    term = jnp.where(lane < EXPERTS, top, jnp.where(lane < 2 * EXPERTS, mid, low))
    out_ref[:, D:] = jnp.where(lane < 3 * EXPERTS, term, 0.0).astype(BF)

    lane = iota((1, 128), 1)
    freq = jnp.exp((lane & 31).astype(F32) * (-2.0 * math.log(10000.0) / HEAD))
    sign = jnp.where((lane & 32) == 0, -1.0, 1.0)
    for t in range(0, c_ref.shape[0], TILE):
        row = iota((TILE, 1), 0).astype(F32) + float(t)
        if t >= PROMPT:
            own = segc_ref[t - PROMPT : t - PROMPT + TILE, :]
            start = jnp.sum(jnp.where(segr_ref[...] < own, 1.0, 0.0), axis=1, keepdims=True)
            row = row - start
        ang = row * freq
        c_ref[t : t + TILE, :] = jnp.cos(ang)
        s_ref[t : t + TILE, :] = jnp.sin(ang) * sign


def att_kernel(geo, me_ref, q_ref, kd_ref, vt_ref, segc_ref, segr_ref, o_ref, lse_ref):
    me = me_ref[0]
    for q0, keys in geo.tiles():
        outs = []
        for h in range(2):
            q = q_ref[h, q0 : q0 + TILE, :]
            ss = [
                masked(nt(kd_ref[0, k0 : k0 + kn, :], q), kind, q0, k0, segc_ref, segr_ref)
                for k0, kn, kind in keys
            ]
            top = functools.reduce(
                jnp.maximum, [jnp.max(s, axis=0, keepdims=True) for s in ss]
            )
            ps = [jnp.exp(s - top) for s in ss]
            total = functools.reduce(
                jnp.add, [jnp.sum(p, axis=0, keepdims=True) for p in ps]
            )
            lse_ref[h, :, q0 : q0 + TILE] = top + jnp.log(total)
            inv = 1.0 / total
            acc = None
            for p, (k0, kn, kind) in zip(ps, keys):
                part = nn(vt_ref[0, :, k0 : k0 + kn], (p * inv).astype(BF))
                acc = part if acc is None else acc + part
            outs.append(acc)
        o = jnp.concatenate(outs, axis=0).T.astype(BF)
        for a, cnt, dst in geo.spread(me, q0):
            o_ref[pl.ds(dst, cnt), :] = o[a : a + cnt, :]


def hidden_kernel(geo, natt, s_ref, *refs):
    pieces = geo.pieces()
    np_ = len(pieces)
    atts = refs[:natt]
    toks = refs[natt : natt + np_]
    mine_ref, other_ref, gain_ref = refs[natt + np_ : natt + np_ + 3]
    hid_ref, x_ref, w_ref = refs[natt + np_ + 3 :]
    half = mine_ref.shape[0] // geo.n
    for m in range(geo.n):
        own = pl.multiple_of((2 * m + s_ref[0]) * half, 64)
        sib = pl.multiple_of((2 * m + 1 - s_ref[0]) * half, 64)
        w_ref[pl.ds(own, half), :] = mine_ref[m * half : (m + 1) * half, :]
        w_ref[pl.ds(sib, half), :] = other_ref[m * half : (m + 1) * half, :]
    gain = gain_ref[...].astype(F32)
    index = {}
    k = 0
    for g in range(geo.G):
        for m, off, rows in att_pieces(geo):
            index[(m, g, off)] = (atts[k], off, rows)
            k += 1

    def att_rows(m, g, row, cnt):
        for (mm, gg, _), (ref, off, rows) in index.items():
            if mm == m and gg == g and off <= row and row + cnt <= off + rows:
                return ref[row - off : row - off + cnt, :]
        raise ValueError("piece")

    for (j, off, rows), tok in zip(pieces, toks):
        lhs = jnp.concatenate(
            [
                att_rows(m, g, (m ^ j) * geo.T + off, rows)
                for m in range(geo.n)
                for g in range(geo.G)
            ],
            axis=1,
        )
        h = tok[...].astype(F32) + nn(lhs, w_ref[...])
        if j == 0:
            hid_ref[...] = h
        r = lax.rsqrt(jnp.mean(h * h, axis=-1, keepdims=True) + EPS)
        x_ref[j * geo.T + off : j * geo.T + off + rows, :] = (h * r * gain).astype(BF)


def att_pieces(geo):
    rows = geo.n * geo.T
    out = [(m, 0, rows) for m in range(geo.n)]
    if geo.relay:
        out = out[:-1] + [(3, 0, rows // 2), (3, rows // 2, rows // 2)]
    return out


CH = 1


def expert_rows(x, dout, wg, wu, wd, gate):
    g = nn(x, wg)
    u = nn(x, wu)
    back = nt(dout, wd) * gate
    s = 1.0 / (1.0 + jnp.exp(-g))
    sil = g * s
    act = (sil * u * gate).astype(BF)
    gg = (back * u * (s + sil * (1.0 - s))).astype(BF)
    ug = (back * sil).astype(BF)
    return act, gg, ug


def gate_column(gm_ref, expert):
    lane = iota(gm_ref.shape, 1)
    mine = (lane == expert) | (lane == EXPERTS + expert) | (lane == 2 * EXPERTS + expert)
    return jnp.sum(jnp.where(mine, gm_ref[...].astype(F32), 0.0), axis=1, keepdims=True)


def put_grads(outs, x_ref, do_ref, gg_ref, ug_ref, ac_ref):
    cols = x_ref.shape[1] // len(outs)
    for k, out in enumerate(outs):
        x = x_ref[:, k * cols : (k + 1) * cols]
        out[0] = tn(x, gg_ref[...]).astype(BF)
        out[1] = tn(x, ug_ref[...]).astype(BF)
        out[2] = tn(do_ref[:, k * cols : (k + 1) * cols], ac_ref[...]).astype(BF)


def expert_kernel(n, T, E, e, s_ref, *refs):
    x_ref, do_ref, gm_ref, wg_ref, wu_ref, wd_ref, xc_ref, dc_ref = refs[:8]
    act_ref, gg_ref, ug_ref, send = refs[-7 - CH : -3 - CH]
    keeps = refs[-3 - CH : -3]
    gg_s, ug_s, ac_s = refs[-3:]
    r = pl.program_id(0)

    @pl.when(r < n)
    def _():
        act, gg, ug = expert_rows(
            x_ref[...],
            do_ref[...],
            wg_ref[0],
            wu_ref[0],
            wd_ref[0],
            gate_column(gm_ref, s_ref[1] * E + e),
        )
        rows = pl.ds(pl.multiple_of(r * T, 128), T)
        gg_s[rows, :] = gg
        ug_s[rows, :] = ug
        ac_s[rows, :] = act
        act_ref[...] = act
        gg_ref[...] = gg
        ug_ref[...] = ug

    @pl.when(r == n)
    def _():
        put_grads([send], xc_ref, dc_ref, gg_s, ug_s, ac_s)

    @pl.when(r == n + 1)
    def _():
        put_grads(keeps, xc_ref, dc_ref, gg_s, ug_s, ac_s)


def expert(n, T, E, e, scal, x, dout, wg, wu, wd, kept):
    D, M = wg.shape[1:]
    row = lambda r, c: (jnp.minimum(r, n - 1), 0)
    gate = lambda r, c: (jnp.minimum(r, n - 1), D // 128)
    half = lambda r, c: (0, jnp.where(r == n + 1, c[0], 1 - c[0]))
    fix = lambda r, c: (e, 0, 0)
    whole = lambda r, c: (0, 0, 0)
    block = pl.BlockSpec((T, M), lambda r, c: (jnp.minimum(r, n - 1), e))
    in_specs = [
        pl.BlockSpec((T, D), row),
        pl.BlockSpec((T, D), row),
        pl.BlockSpec((T, 128), gate),
        pl.BlockSpec((1, D, M), fix),
        pl.BlockSpec((1, D, M), fix),
        pl.BlockSpec((1, M, D), fix),
        pl.BlockSpec((n * T, D // 2), half),
        pl.BlockSpec((n * T, D // 2), half),
    ]
    args = [x, dout, dout, wg, wu, wd, x, dout]
    alias = {}
    if kept is not None:
        in_specs += [pl.BlockSpec(memory_space=pl.ANY)] * 3
        args += list(kept)
        alias = {9: 0, 10: 1, 11: 2}
    out = call(
        functools.partial(expert_kernel, n, T, E, e),
        (pltpu.HBM((n * T, E * M), BF),) * 3
        + (shape((3, D // 2, M), BF),)
        + (shape((3, D // 2 // CH, M), BF),) * CH,
        12 * n * T * D * M,
        20e6,
        grid_spec=pltpu.PrefetchScalarGridSpec(
            num_scalar_prefetch=1,
            grid=(n + 2,),
            in_specs=in_specs,
            out_specs=(block,) * 3
            + (pl.BlockSpec((3, D // 2, M), whole),)
            + (pl.BlockSpec((3, D // 2 // CH, M), whole),) * CH,
            scratch_shapes=[pltpu.VMEM((n * T, M), BF)] * 3,
        ),
        input_output_aliases=alias,
        name=f"expert{e}",
    )(scal, *args)
    return out[:3], out[3], out[4:]


def forward_kernel(E, e0, s_ref, x_ref, do_ref, gm_ref, wg_ref, wu_ref, wd_ref, *refs):
    act_ref, gg_ref, ug_ref = refs[-3:]
    act, gg, ug = expert_rows(
        x_ref[...],
        do_ref[...],
        wg_ref[0],
        wu_ref[0],
        wd_ref[0],
        gate_column(gm_ref, s_ref[1] * E + e0 + pl.program_id(0)),
    )
    act_ref[...] = act
    gg_ref[...] = gg
    ug_ref[...] = ug


def forwards(n, T, E, e0, scal, x, dout, wg, wu, wd, kept):
    D, M = wg.shape[1:]
    R = n * T // 2
    any_ = pl.BlockSpec(memory_space=pl.ANY)
    row = pl.BlockSpec((R, D), lambda i, r, c: (r, 0))
    fix = lambda i, r, c: (e0 + i, 0, 0)
    block = pl.BlockSpec((R, M), lambda i, r, c: (r, e0 + i))
    return call(
        functools.partial(forward_kernel, E, e0),
        (pltpu.HBM((n * T, E * M), BF),) * 3,
        6 * (E - e0) * n * T * D * M,
        (E - e0) * 12e6,
        grid_spec=pltpu.PrefetchScalarGridSpec(
            num_scalar_prefetch=1,
            grid=(E - e0, 2),
            in_specs=[
                row,
                row,
                pl.BlockSpec((R, 128), lambda i, r, c: (r, D // 128)),
                pl.BlockSpec((1, D, M), fix),
                pl.BlockSpec((1, D, M), fix),
                pl.BlockSpec((1, M, D), fix),
                any_,
                any_,
                any_,
            ],
            out_specs=(block,) * 3,
        ),
        input_output_aliases={7: 0, 8: 1, 9: 2},
        name="forwards",
    )(scal, x, dout, dout, wg, wu, wd, *kept)


def input_grad_kernel(E, T, gg_ref, ug_ref, wg_ref, wu_ref, *refs):
    outs, acc = refs[:-1], refs[-1]
    i = pl.program_id(0)
    v = nt(gg_ref[...], wg_ref[0]) + nt(ug_ref[...], wu_ref[0])

    @pl.when(i == 0)
    def _():
        acc[...] = v

    @pl.when(i > 0)
    def _():
        acc[...] += v

    @pl.when(i == E - 1)
    def _():
        put_blocks(T, acc, outs)


def input_grad(T, E, first, rows, gg, ug, wg, wu):
    D, M = wg.shape[1:]
    R = sum(rows)
    block = pl.BlockSpec((R, M), lambda i: (first // R, i))
    weight = pl.BlockSpec((1, D, M), lambda i: (i, 0, 0))
    return call(
        functools.partial(input_grad_kernel, E, T),
        tuple(shape((v, D), BF) for v in rows),
        4 * E * R * D * M,
        16e6,
        grid=(E,),
        in_specs=[block, block, weight, weight],
        out_specs=tuple(pl.BlockSpec((v, D), lambda i: (0, 0)) for v in rows),
        scratch_shapes=[pltpu.VMEM((R, D), F32)],
        name=f"input_grad{first}",
    )(gg, ug, wg, wu)


def weight_grad_kernel(s_ref, x_ref, do_ref, gg_ref, ug_ref, ac_ref, send, *keeps):
    @pl.when(pl.program_id(0) == 0)
    def _():
        put_grads([send], x_ref, do_ref, gg_ref, ug_ref, ac_ref)

    @pl.when(pl.program_id(0) == 1)
    def _():
        put_grads(keeps, x_ref, do_ref, gg_ref, ug_ref, ac_ref)


def weight_grad(M, e, scal, x, dout, act, gg, ug):
    R, D = x.shape
    half = lambda s, c: (0, jnp.where(s == 1, c[0], 1 - c[0]))
    whole = lambda s, c: (0, 0, 0)
    block = pl.BlockSpec((R, M), lambda s, c: (0, e))
    out = call(
        weight_grad_kernel,
        (shape((3, D // 2, M), BF),) + (shape((3, D // 2 // CH, M), BF),) * CH,
        6 * R * D * M,
        14e6,
        grid_spec=pltpu.PrefetchScalarGridSpec(
            num_scalar_prefetch=1,
            grid=(2,),
            in_specs=[
                pl.BlockSpec((R, D // 2), half),
                pl.BlockSpec((R, D // 2), half),
                block,
                block,
                block,
            ],
            out_specs=(pl.BlockSpec((3, D // 2, M), whole),)
            + (pl.BlockSpec((3, D // 2 // CH, M), whole),) * CH,
        ),
        name=f"weight_grad{e}",
    )(scal, x, dout, gg, ug, act)
    return out[0], out[1:]


def norm_back_kernel(count, low, *refs):
    parts = refs[:count]
    base_ref, v_ref, gain_ref = refs[count : count + 3]
    outs = refs[count + 3 :]
    grad = parts[0][...].astype(F32)
    for p in parts[1:]:
        grad = grad + p[...].astype(F32)
    v = v_ref[...].astype(F32)
    r = lax.rsqrt(jnp.mean(v * v, axis=-1, keepdims=True) + EPS)
    gv = gain_ref[...].astype(F32) * grad
    res = (
        base_ref[...].astype(F32)
        + r * gv
        - v * (r * r * r * jnp.mean(gv * v, axis=-1, keepdims=True))
    )
    outs[0][...] = res
    if low:
        outs[1][...] = res.astype(BF)
        part = jnp.sum(grad * v * r, axis=0, keepdims=True)

        @pl.when(pl.program_id(0) == 0)
        def _():
            outs[2][...] = part

        @pl.when(pl.program_id(0) > 0)
        def _():
            outs[2][...] += part


def norm_back(parts, base, v, gain, low):
    T, D = v.shape
    B = 128
    row = pl.BlockSpec((B, D), lambda i: (i, 0))
    one = pl.BlockSpec((1, D), lambda i: (0, 0))
    out = [shape((T, D), F32)]
    specs = [row]
    if low:
        out += [shape((T, D), BF), shape((1, D), F32)]
        specs += [row, one]
    return call(
        functools.partial(norm_back_kernel, len(parts), low),
        tuple(out),
        20 * T * D,
        T * D * 16,
        grid=(T // B,),
        in_specs=[row] * len(parts) + [row, row, one],
        out_specs=tuple(specs),
        name="norm_back",
    )(*parts, base, v, gain)


def att_back_kernel(geo, gi, me_ref, *refs):
    pieces = geo.pieces()
    np_ = len(pieces)
    brs = refs[:np_]
    (w_ref, q_ref, kd_ref, kt_ref, vd_ref, lse_ref, segc_ref, segr_ref, c_ref, s_ref) = refs[
        np_ : np_ + 10
    ]
    out_ref, do_s, dk_s, dv_s, dq_s = refs[np_ + 10 :]
    me = me_ref[0]
    for (m, off, rows), br in zip(pieces, brs):
        y = nt(br[...], w_ref[...])
        low = iota((rows, 128), 1) < 64
        lo = jnp.where(low, y, 0.0).astype(BF)
        hi = jnp.where(low, 0.0, y).astype(BF)
        for a, cnt, dst in geo.places(me, m, off, rows):
            do_s[0, pl.ds(dst, cnt), :] = lo[a : a + cnt, :]
            do_s[1, pl.ds(dst, cnt), :] = hi[a : a + cnt, :]
    dk_s[...] = jnp.zeros_like(dk_s)
    dv_s[...] = jnp.zeros_like(dv_s)

    def head(i, carry):
        g = 0
        for q0, keys in geo.tiles():
            q = q_ref[i, q0 : q0 + TILE, :]
            do = do_s[i, q0 : q0 + TILE, :]
            lse = lse_ref[i, :, q0 : q0 + TILE]
            ps, dps = [], []
            delta = None
            for k0, kn, kind in keys:
                s = masked(nt(kd_ref[g, k0 : k0 + kn, :], q), kind, q0, k0, segc_ref, segr_ref)
                p = jnp.exp(s - lse)
                dp = nt(vd_ref[g, k0 : k0 + kn, :], do)
                dv_s[g, k0 : k0 + kn, :] += nn(p.astype(BF), do)
                d = jnp.sum(p * dp, axis=0, keepdims=True)
                delta = d if delta is None else delta + d
                ps.append(p)
                dps.append(dp)
            acc = None
            for p, dp, (k0, kn, kind) in zip(ps, dps, keys):
                ds = (p * (dp - delta)).astype(BF)
                dk_s[g, k0 : k0 + kn, :] += nn(ds, q)
                part = nn(kt_ref[g, :, k0 : k0 + kn], ds)
                acc = part if acc is None else acc + part
            dq_s[i, :, q0 : q0 + TILE] = acc
        return carry

    lax.fori_loop(0, 2, head, 0)
    low = iota((TILE, 128), 1) < 64
    for t in range(0, geo.TG, TILE):
        rows = slice(t, t + TILE)
        cos, sin = c_ref[rows, :], s_ref[rows, :]
        v = jnp.concatenate([dq_s[0, :, rows], dq_s[1, :, rows]], axis=0).T * 0.125
        dq = v * cos - swap_halves(v) * sin
        k = dk_s[0, rows, :]
        k = k + pltpu.roll(k, 64, 1)
        k = k * cos - swap_halves(k) * sin
        v = dv_s[0, rows, :]
        for x, col in enumerate((dq, jnp.where(low, k, v + pltpu.roll(v, 64, 1)))):
            y = col.astype(BF)
            for a, cnt, dst in geo.spread(me, t):
                out_ref[pl.ds(dst, cnt), x * 128 : x * 128 + 128] = y[a : a + cnt, :]


def mix_kernel(T, act_ref, w_ref, *refs):
    outs, acc = refs[:-1], refs[-1]
    i = pl.program_id(0)
    v = nn(act_ref[...], w_ref[0])

    @pl.when(i == 0)
    def _():
        acc[...] = v

    @pl.when(i > 0)
    def _():
        acc[...] += v

    @pl.when(i == pl.num_programs(0) - 1)
    def _():
        put_blocks(T, acc, outs)


def mix_parts(n, T, rows, act, wd):
    E, M, D = wd.shape
    return call(
        functools.partial(mix_kernel, T),
        (shape((T, D), F32),) + tuple(shape((v, D), BF) for v in rows[1:]),
        2 * n * T * E * M * D,
        10e6,
        grid=(E,),
        in_specs=[
            pl.BlockSpec((n * T, M), lambda i: (0, i)),
            pl.BlockSpec((1, M, D), lambda i: (i, 0, 0)),
        ],
        out_specs=tuple(pl.BlockSpec((v, D), lambda i: (0, 0)) for v in rows),
        scratch_shapes=[pltpu.VMEM((n * T, D), F32)],
        name="mix",
    )(act, wd)


def back_kernel(T, G, w_ref, *refs):
    ys, outs = refs[:G], refs[G:]
    at = 0
    for out in outs:
        rows = out.shape[0]
        v = None
        for g, y in enumerate(ys):
            p = nt(y[at : at + rows, :], w_ref[:, g * 256 : (g + 1) * 256])
            v = p if v is None else v + p
        out[...] = v.astype(BF)
        at += rows


def head_grad_kernel(geo, first, s_ref, x_ref, y_ref, w_ref, gf_ref, *outs):
    me = s_ref[1]
    r = w_ref.shape[0] // geo.n
    ones = jnp.ones((16, 256), BF)
    row = iota((16, 256), 0)
    for j in range(geo.n):
        dw = tn(x_ref[:, j * r : (j + 1) * r], y_ref[...])
        prod = dw * w_ref[j * r : (j + 1) * r, :].astype(F32)
        hi = prod.astype(BF)
        lo = (prod - hi.astype(F32)).astype(BF)
        gain = nt(ones, hi) + nt(ones, lo)
        below = gf_ref[:, j * r : (j + 1) * r] if first else jnp.zeros((1, r), F32)
        if r < 256:
            gain = jnp.concatenate([gain, jnp.zeros((16, 256 - r), F32)], axis=1)
            below = jnp.concatenate([below, jnp.zeros((1, 256 - r), F32)], axis=1)
        extra = jnp.where(row == 0, gain, jnp.where(row == 1, below, 0.0)).astype(BF)
        low = dw.astype(BF)
        for m, out in enumerate(outs):

            @pl.when((me ^ m) == j)
            def _():
                out[:r, :] = low
                out[r:, :] = extra


def out_grad_kernel(np_, G, s_ref, *refs):
    brs, atts = refs[:np_], refs[np_ : np_ + G]
    send, keep = refs[np_ + G], refs[np_ + G + 1]
    per = []
    for o in atts:
        v, at_ = None, 0
        for br in brs:
            rows = br.shape[0]
            p = tn(o[at_ : at_ + rows, :], br[...])
            v = p if v is None else v + p
            at_ += rows
        per.append(v)
    v = jnp.concatenate(per, axis=0).astype(BF)
    lead, rows = send.shape[0], send.shape[1]
    half = v.shape[0] // 2
    count = rows // half

    def put(out, top):
        for a in range(lead):
            for b in range(count):
                c = (a * count + b) * 256
                out[a, b * half : (b + 1) * half, :] = v[top : top + half, c : c + 256]

    @pl.when(s_ref[0] == 0)
    def _():
        put(keep, 0)
        put(send, half)

    @pl.when(s_ref[0] == 1)
    def _():
        put(keep, half)
        put(send, 0)


def combine_kernel(ops, wide, k, *refs):
    end = (refs[0][0] == 0) | (refs[0][0] == refs[0][1])
    ins, outs = refs[1 : 1 + k], refs[len(refs) - len(ops) :]

    def plus(a, b):
        return (ins[a][...].astype(F32) + ins[b][...].astype(F32)).astype(BF)

    for (kind, *at), w, out in zip(ops, wide, outs):

        def work():
            if kind == "add":
                out[...] = plus(*at)
                return

            @pl.when(end)
            def _():
                out[...] = plus(*at[:2]) if kind == "merge" else ins[at[0]][...]

            @pl.when(jnp.logical_not(end))
            def _():
                out[...] = plus(*at[2:]) if kind == "merge" else ins[at[1]][...]

        if w:
            work()
        else:
            pl.when((pl.program_id(0) == 0) & (pl.program_id(1) == 0))(work)


def combine(pos, ops):
    arrays, specs, keys, coded, outs, out_specs, wide = [], [], [], [], [], [], []

    def spec(w, block, part):
        if w:
            half = (1, block[0] // 2, block[1])
            return pl.BlockSpec(half, lambda i, h, p: (i, 2 * part + h, 0))
        return pl.BlockSpec(block, lambda i, h, p: (0,) * len(block))

    for kind, args, place in ops:
        a = args[0][0]
        w = a.shape[0] == 3
        block = a.shape[1:] if w else a.shape
        at = []
        for v, part in args:
            key = (id(v), part)
            if key not in keys:
                keys.append(key)
                arrays.append(v)
                specs.append(spec(w, block, part))
            at.append(keys.index(key))
        coded.append((kind, *at))
        wide.append(w)
        if place is None:
            outs.append(shape(a.shape, BF))
            out_specs.append(spec(w, block, 0))
        else:
            outs.append(shape((3, CH * block[0], block[1]), BF))
            out_specs.append(spec(w, block, place[1]))
    k = len(arrays)
    alias = {}
    for i, (_, _, place) in enumerate(ops):
        if place is not None and place[0] is not None:
            alias[1 + len(arrays)] = i
            arrays.append(place[0])
            specs.append(pl.BlockSpec(memory_space=pl.ANY))
    out = call(
        functools.partial(combine_kernel, coded, wide, k),
        tuple(outs),
        1e6,
        1e6,
        grid_spec=pltpu.PrefetchScalarGridSpec(
            num_scalar_prefetch=1,
            grid=(3, 2),
            in_specs=specs,
            out_specs=tuple(out_specs),
        ),
        input_output_aliases=alias,
        name="combine",
    )(pos, *arrays)
    return list(out)


def put_blocks(T, acc, outs, first=0):
    at = first
    for out in outs:
        rows = out.shape[0]
        out[...] = acc[at : at + rows, :].astype(out.dtype)
        at += rows


def finish_kernel(e, first, c_ref, own_ref, sib_ref, *refs):
    g_ref, u_ref, d_ref = refs if first else refs[3:]

    def put(src):
        g_ref[0] = src[0].astype(F32)
        u_ref[0] = src[1].astype(F32)
        d_ref[0] = src[2].astype(F32).T

    @pl.when(pl.program_id(0) < 2)
    def _():
        put(own_ref)

    @pl.when(pl.program_id(0) >= 2)
    def _():
        put(sib_ref)


def finish(e, E, core, own, sib, prev):
    _, Dh, M = own.shape
    rows = Dh // 2
    first = prev is None
    half = lambda s, c: jnp.where(s < 2, 2 * c[0] + s, 2 * (1 - c[0]) + s - 2)
    any_ = pl.BlockSpec(memory_space=pl.ANY)
    return call(
        functools.partial(finish_kernel, e, first),
        (
            shape((E, 2 * Dh, M), F32),
            shape((E, 2 * Dh, M), F32),
            shape((E, M, 2 * Dh), F32),
        ),
        1e6,
        10e6,
        grid_spec=pltpu.PrefetchScalarGridSpec(
            num_scalar_prefetch=1,
            grid=(4,),
            in_specs=[
                pl.BlockSpec((3, rows, M), lambda s, c: (0, jnp.minimum(s, 1), 0)),
                pl.BlockSpec((3, rows, M), lambda s, c: (0, jnp.maximum(s - 2, 0), 0)),
            ]
            + ([] if first else [any_] * 3),
            out_specs=(
                pl.BlockSpec((1, rows, M), lambda s, c: (e, half(s, c), 0)),
                pl.BlockSpec((1, rows, M), lambda s, c: (e, half(s, c), 0)),
                pl.BlockSpec((1, M, rows), lambda s, c: (e, 0, half(s, c))),
            ),
        ),
        input_output_aliases={} if first else {3: 0, 4: 1, 5: 2},
        name=f"finish{e}",
    )(core, own, sib, *([] if first else prev))


def last_kernel(n, r, s_ref, *refs):
    halves = (refs[0:2], refs[2:4])
    gain_ref, ga_ref, q_ref, k_ref, v_ref, o_ref, gf_ref = refs[4:]
    core, me = s_ref[0], s_ref[1]
    lead = n // 2
    low = iota((r, 128), 1) < 64
    ga = jnp.zeros((1, 256), F32)
    gf = jnp.zeros((1, 256), F32)
    for side, pair in enumerate(halves):
        hh = core if side == 0 else 1 - core
        for l in range(lead):
            one, two = pair[0][l, :r, :].astype(F32), pair[1][l, :r, :].astype(F32)
            kv0, kv1 = one[:, 128:], two[:, 128:]
            k = jnp.where(low, kv0, pltpu.roll(kv1, 64, 1))
            v = jnp.where(low, pltpu.roll(kv0, 64, 1), kv1)
            for j in range(n):

                @pl.when((me ^ (hh * lead + l)) == j)
                def _():
                    q_ref[:, j * 256 : j * 256 + 128] = one[:, :128]
                    q_ref[:, j * 256 + 128 : j * 256 + 256] = two[:, :128]
                    k_ref[:, j * 128 : j * 128 + 128] = k
                    v_ref[:, j * 128 : j * 128 + 128] = v

            below = pair[0][l, r : r + 16, :].astype(F32)
            ga = ga + below[:1, :] + pair[1][l, r : r + 16, :].astype(F32)[:1, :]
            gf = gf + below[1:2, :]
            count = (pair[0].shape[1] - r - 16) // (r // 2)
            for b in range(count):
                c = (l * count + b) * 256
                at = r + 16 + b * (r // 2)
                o_ref[pl.ds(pl.multiple_of(hh * (r // 2), 128), r // 2), c : c + 256] = pair[0][
                    l, at : at + r // 2, :
                ].astype(F32)
    ga_ref[...] = ga[:, :r] / gain_ref[...].astype(F32)
    gf_ref[...] = gf[:, :r]


def mixed_kernel(*refs):
    v = refs[0][...]
    for p in refs[1:-1]:
        v = v + p[...].astype(F32)
    refs[-1][...] = v.astype(BF)


def mixed_sum(hidden, parts):
    T, D = hidden.shape
    row = pl.BlockSpec((T // 2, D), lambda i: (i, 0))
    return call(
        mixed_kernel,
        shape((T, D), BF),
        1e6,
        6e6,
        grid=(2,),
        in_specs=[row] * (1 + len(parts)),
        out_specs=row,
        name="mixed",
    )(hidden, *parts)


def per_device(
    tokens,
    d_out,
    routes,
    gates,
    segment,
    gain_attn,
    w_query,
    key_weight,
    value_weight,
    w_out,
    gain_ffn,
    w_gate,
    w_up,
    w_down,
):
    n = lax.axis_size("shard")
    me = lax.axis_index("shard")
    R = lax.axis_size("rep")
    rp = lax.axis_index("rep")
    core, pos = rp % 2, rp // 2
    T, D = tokens.shape
    geo = Geo(n, T, segment.shape[1])
    G, TG = geo.G, geo.TG
    E, _, M = w_gate.shape
    me1 = me.reshape(1).astype(jnp.int32)
    scal = jnp.stack([core, me]).astype(jnp.int32)

    def px(v, m):
        return lax.ppermute(v, "shard", [(i, i ^ m) for i in range(n)])

    def at(v, i):
        return lax.dynamic_index_in_dim(v, i, 0, keepdims=False)

    def near(v):
        return [v] + [px(v, m) for m in ((1, 2) if geo.relay else range(1, n))]

    def far(got):
        if not geo.relay:
            return list(got)
        v, a, b = got
        h = v.shape[0] // 2
        return [v, a, b, px(a[:h], 2), px(b[h:], 1)]

    def hbm(*vals):
        return [pltpu.with_memory_space_constraint(v, pltpu.HBM) for v in vals]

    def tie(vals, deps):
        vals, deps = tuple(vals), tuple(deps)
        return lax.optimization_barrier(vals + deps)[: len(vals)]

    L = R // 2

    def pz(v, pairs):
        return lax.ppermute(v, "rep", [(2 * a + k, 2 * b + k) for a, b in pairs for k in (0, 1)])

    def sib(v):
        return lax.ppermute(v, "rep", [(i, i ^ 1) for i in range(R)])

    pos1 = jnp.stack([pos, jnp.full((), L - 1)]).astype(jnp.int32)
    near_pairs = [(0, 1), (1, 0), (2, 3), (3, 2)]

    class Sums:
        def __init__(self):
            self.live, self.done, self.final = [], {}, {}

        def add(self, tag, keeps, send, quick=False):
            if L != 4:
                both_ = jnp.stack([jnp.concatenate(keeps, axis=1), send])
                both_ = jnp.where(core == 0, both_, both_[::-1])
                both_ = lax.psum(both_, "rep")
                self.done[tag] = at(both_, core), at(both_, 1 - core)
                return
            new = sib(send)
            for k, keep in enumerate(keeps):
                self.live.append(
                    dict(
                        tag=tag,
                        part=k,
                        parts=len(keeps),
                        step=0,
                        acc=keep,
                        new=new,
                        quick=quick,
                    )
                )

        def meet(self, chunks, vals):
            names = [(c, f) for c in chunks for f in ("acc", "new")]
            flat = []
            for c, f in names:
                if not any(c[f] is v for v in flat):
                    flat.append(c[f])
            got = lax.optimization_barrier(tuple(vals) + tuple(flat))
            fresh = got[len(vals) :]
            for c, f in names:
                c[f] = next(b for a, b in zip(flat, fresh) if a is c[f])
            return got[: len(vals)]

        def advance(self, vals, more=(), hold=(), starts=1):
            live = []
            for c in self.live:
                if c["tag"] in hold:
                    continue
                if c["step"] == 0:
                    if not starts:
                        continue
                    starts -= 1
                live.append(c)
            vals = self.meet([c for c in live if c["step"] > 0], vals)
            vals = self.meet(live, (*vals, *more))
            if not live:
                return vals
            ops, then = [], []
            into = [c for c in live if c["step"] == 0 and not c["quick"]]
            out = [c for c in live if c["step"] == 2 and not c["quick"]]

            def arrived(c):
                return [(c["acc"], 0), (c["new"], c["part"] if c["step"] == 0 else 0)]

            pairs = []
            for c in out:
                mate = next((d for d in into if d["acc"].shape == c["acc"].shape), None)
                if mate is not None:
                    into.remove(mate)
                pairs.append((mate, c))
            pairs += [(d, None) for d in into]
            for c in live:
                if c["quick"]:
                    ops.append(("add", arrived(c), None))
                    then.append(("quick", c))
                elif c["step"] == 3:
                    whole = self.final.get(c["tag"])
                    place = None if c["parts"] == 1 else (whole, c["part"])
                    ops.append(("take", [(c["new"], 0), (c["acc"], 0)], place))
                    then.append(("done", c))
                elif c["step"] == 1:
                    ops.append(("add", arrived(c), None))
                    then.append(("mid", c))
            for d, c in pairs:
                if c is None:
                    ops.append(("add", arrived(d), None))
                    then.append(("in", d))
                elif d is None:
                    ops.append(("add", arrived(c), None))
                    then.append(("out", c))
                else:
                    ops.append(("add", arrived(d), None))
                    then.append(("acc", d))
                    ops.append(("merge", arrived(d) + arrived(c), None))
                    then.append(("both", d, c))
            res = combine(pos1, ops)
            waiting = [t for t, v in self.done.items() if len(v) == 1]
            got = lax.optimization_barrier(
                vals + tuple(res) + tuple(self.done[t][0] for t in waiting)
            )
            vals, res, old = (
                got[: len(vals)],
                got[len(vals) : len(vals) + len(res)],
                got[len(vals) + len(res) :],
            )
            for t, v in zip(waiting, old):
                self.done[t] = (v,)
            for (what, *cs), v in zip(then, res):
                c = cs[-1]
                if what == "quick":
                    step = c["step"]
                    if step == 2:
                        c["step"] = 4
                        self.done[c["tag"]] = (v,)
                    else:
                        far_pairs = [(0, 2), (2, 0), (1, 3), (3, 1)]
                        c.update(step=step + 1, acc=v, new=pz(v, far_pairs if step else near_pairs))
                elif what == "done":
                    self.final[c["tag"]] = v
                    c["step"] = 4
                    if all(o["step"] == 4 or o["tag"] != c["tag"] for o in self.live):
                        self.done[c["tag"]] = (v,)
                elif what == "mid":
                    c.update(step=2, acc=v, new=pz(v, [(1, 2), (2, 1)]))
                elif what == "acc":
                    c.update(acc=v)
                elif what == "in":
                    c.update(step=1, acc=v, new=pz(v, [(0, 1), (3, 2)]))
                elif what == "out":
                    c.update(step=3, acc=v, new=pz(v, [(1, 0), (2, 3)]))
                else:
                    new = pz(v, near_pairs)
                    cs[0].update(step=1, new=new)
                    c.update(step=3, acc=v, new=new)
            self.live = [c for c in self.live if c["step"] < 4]
            return vals

        def with_done(self, vals):
            waiting = [t for t, v in self.done.items() if len(v) == 1]
            got = lax.optimization_barrier(
                tuple(vals) + tuple(self.done[t][0] for t in waiting)
            )
            for t, v in zip(waiting, got[len(vals) :]):
                self.done[t] = (v,)
            return got[: len(vals)]

        def whole(self, tag):
            if len(self.done[tag]) == 1:
                self.done[tag] = (*self.done[tag], sib(*self.done[tag]))
            return self.done[tag]

    sums = Sums()

    def scatter(parts):
        return [parts[0]] + [px(parts[m], m) for m in range(n - 1, 0, -1)]

    r = w_query.shape[0]
    W = G * 256
    segc, segr = segment.reshape(-1, 1), segment
    near_tok = near(tokens)
    wmsg = call(
        functools.partial(columns_kernel, geo),
        (shape((r + 16, W), BF),) * n,
        1e6,
        2e6,
        in_specs=[SM] + [VM] * 5,
        out_specs=(VM,) * n,
        name="columns",
    )(me1, w_query, key_weight, value_weight, gain_attn.reshape(1, r), gain_ffn.reshape(1, r))
    got_w = [wmsg[0]] + [px(wmsg[m], m) for m in range(1, n)]
    dmsg, cos4, sin4 = call(
        pack_kernel,
        (shape((T, D + 128), BF), shape((TG, 128), F32), shape((TG, 128), F32)),
        1e6,
        2e6,
        in_specs=[VM] * 5,
        out_specs=(VM,) * 3,
        name="pack",
    )(d_out, routes, gates, segc, segr)
    wo_own = at(w_out.reshape(2, r // 2, D), core)
    dmsg, cos4, wo_own, *near_tok = tie((dmsg, cos4, wo_own, *near_tok), ())
    tok = far(near_tok)
    near_wo = near(wo_own)
    dmsg, *rest = tie((dmsg, *tok, *near_wo, *got_w), ())
    np_ = len(tok)
    tok, near_wo, got_w = rest[:np_], rest[np_ : -n], rest[-n:]
    near_d = near(dmsg)
    wo_half = far(near_wo)

    normed, q, kd, vd, kt, vt, w_cols, gain_a, gain_f = call(
        functools.partial(qkv_kernel, geo),
        (
            shape((n * T, D), BF),
            shape((2 * G, TG, 128), BF),
            shape((G, TG, 128), BF),
            shape((G, TG, 128), BF),
            shape((G, 64, TG), BF),
            shape((G, 64, TG), BF),
            shape((D, W), BF),
            shape((1, D), F32),
            shape((1, D), F32),
        ),
        2 * TG * D * W,
        12e6,
        in_specs=[SM] + [VM] * (np_ + n + 2),
        out_specs=(VM,) * 9,
        scratch_shapes=[pltpu.VMEM((TG, W), F32)],
        name="qkv",
    )(me1, *tok, *got_w, cos4, sin4)

    atts, lses, own_att = [], [], []
    near_o = None
    for g in range(G):
        o, lse = call(
            functools.partial(att_kernel, geo),
            (shape((n * T, 128), BF), shape((2, 1, TG), F32)),
            1e9,
            3e6,
            2 * TG * TG * 0.6,
            grid=(1,),
            in_specs=[
                SM,
                pl.BlockSpec((2, TG, 128), lambda i, g=g: (g, 0, 0)),
                pl.BlockSpec((1, TG, 128), lambda i, g=g: (g, 0, 0)),
                pl.BlockSpec((1, 64, TG), lambda i, g=g: (g, 0, 0)),
                VM,
                VM,
            ],
            out_specs=(VM, VM),
            name=f"attend{g}",
        )(me1, q, kd, vt, segc, segr)
        own_att.append(o)
        lses.append(lse)
        if g == 0:
            k = len(near_d)
            o, q, *rest = tie((o, q, *near_d, *wo_half), ())
            near_d, wo_half = rest[:k], rest[k:]
            wo_mine = jnp.concatenate(wo_half, axis=0)
            wo_sib = sib(wo_mine)
            near_o = near(o)
        else:
            o, *near_o = tie((o, *near_o), ())
            atts += far(near_o)
            near_o = near(o)
    near_d, near_o = list(near_d), list(near_o)
    wo_mine, wo_sib, *rest = tie((wo_mine, wo_sib, *near_d, *near_o, *atts), ())
    k = len(near_d)
    near_d, near_o, atts = rest[:k], rest[k : k + len(near_o)], rest[k + len(near_o) :]
    atts += far(near_o)
    douts = far(near_d)
    lse = jnp.concatenate(lses, axis=0)

    hidden, x = call(
        functools.partial(hidden_kernel, geo, len(atts)),
        (shape((T, D), F32), shape((n * T, D), BF)),
        2 * TG * D * D,
        16e6,
        in_specs=[SM] + [VM] * (len(atts) + np_ + 3),
        out_specs=(VM,) * 2,
        scratch_shapes=[pltpu.VMEM((D, D), BF)],
        name="hidden",
    )(scal, *atts, *tok, wo_mine, wo_sib, gain_f)
    x, *douts = tie((x, *douts), ())
    dout = jnp.concatenate(douts, axis=0)

    w_gate, w_up, w_down = hbm(w_gate, w_up, w_down)
    early = E // 2
    kept = None
    for e in range(early):
        kept, send, keeps = expert(n, T, E, e, scal, x, dout, w_gate, w_up, w_down, kept)
        kept = hbm(*kept)
        sums.add(e, keeps, send)
        if e == 0:
            x, *kept = sums.advance((x, *kept))
    kept = hbm(*forwards(n, T, E, early, scal, x, dout, w_gate, w_up, w_down, kept))
    (last,) = input_grad(T, E, (n - 1) * T, [T], *kept[1:], w_gate, w_up)
    x, act, gg, ug, last = sums.advance((x, *kept, last))

    def weights(e, x, act, gg, ug):
        send, keeps = weight_grad(M, e, scal, x, dout, act, gg, ug)
        sums.add(e, keeps, send)
        return tie((x, act, gg, ug), (send,))

    far_part = px(last, n - 1)
    x, act, gg, ug = weights(early, x, act, gg, ug)
    if n == 4:
        first = input_grad(T, E, 0, [T] * (n - 1), gg, ug, w_gate, w_up)
    else:
        first = [
            v
            for m in range(n - 1)
            for v in input_grad(T, E, m * T, [T], gg, ug, w_gate, w_up)
        ]
    *first, x, act, gg, ug, far_part = sums.advance((*first, x, act, gg, ug), (far_part,))
    came = [first[0], far_part] + [px(first[m], m) for m in range(n - 2, 0, -1)]
    rest = []
    for e in range(early + 1, E):
        send, keeps = weight_grad(M, e, scal, x, dout, act, gg, ug)
        rest += [send, *keeps]
    k = len(came)
    came = tie((*came, act, *rest), ())
    came, act, rest = came[:k], came[k], came[k + 1 :]
    for e in range(early + 1, E):
        sums.add(e, rest[1 : 1 + CH], rest[0])
        rest = rest[1 + CH :]

    hidden_grad, branch, gain_f_part = norm_back(came, d_out, hidden, gain_f, True)
    (act,) = tie((act,), (branch,))
    branches = near(branch)
    mix = sums.advance(mix_parts(n, T, [T] * n, act, w_down), branches)
    mix, branches = mix[:n], far(mix[n:])

    prev = None
    finished = 0

    def finishing(most):
        nonlocal prev, finished
        while finished < most and finished in sums.done:
            prev = finish(finished, E, scal, *sums.whole(finished), prev)
            finished += 1

    def tie_finished(vals):
        nonlocal prev
        if prev is None:
            return tuple(vals)
        got = lax.optimization_barrier(tuple(vals) + tuple(prev))
        prev = got[-3:]
        return got[:-3]

    finishing(1)
    w_out_ = w_out
    nb = len(branches)
    *branches, q, kd = tie_finished((*branches, q, kd))
    mix = list(tie(mix, branches))
    mix_far = px(mix[n - 1], n - 1)

    def attend_back(g, q, kd):
        return call(
            functools.partial(att_back_kernel, geo, g),
            shape((n * T, 256), BF),
            4e9 / G,
            8e6,
            4 * TG * TG * 0.6 / G,
            grid=(1,),
            in_specs=[SM]
            + [VM] * nb
            + [
                pl.BlockSpec((128, D), lambda i: (g, 0)),
                pl.BlockSpec((2, TG, 128), lambda i: (g, 0, 0)),
                pl.BlockSpec((1, TG, 128), lambda i: (g, 0, 0)),
                pl.BlockSpec((1, 64, TG), lambda i: (g, 0, 0)),
                pl.BlockSpec((1, TG, 128), lambda i: (g, 0, 0)),
                pl.BlockSpec((2, 1, TG), lambda i: (g, 0, 0)),
            ]
            + [VM] * 4,
            out_specs=VM,
            scratch_shapes=[
                pltpu.VMEM((2, TG, 128), BF),
                pltpu.VMEM((1, TG, 128), F32),
                pltpu.VMEM((1, TG, 128), F32),
                pltpu.VMEM((2, 64, TG), F32),
            ],
            name=f"attend_back{g}",
        )(me1, *branches, *hbm(w_out_, q, kd, kt, vd, lse, segc, segr, cos4, sin4))

    def head_grad(g, y):
        return call(
            functools.partial(head_grad_kernel, geo, g == 0),
            (shape((r + 16, 256), BF),) * n,
            1e9,
            4e6,
            grid=(1,),
            in_specs=[
                SM,
                VM,
                VM,
                pl.BlockSpec((D, 256), lambda i: (0, g)),
                VM,
            ],
            out_specs=(VM,) * n,
            name=f"head_grad{g}",
        )(scal, normed, y, w_cols, gain_f_part)

    lead = n // 2
    orows = r // 2 * (D // 256) // lead

    def add_small(g, arrived, out=None):
        got = jnp.stack(arrived).reshape(2, lead, r + 16, 256)
        keep, send = at(got, core), at(got, 1 - core)
        if out is not None:
            keep = jnp.concatenate([keep, out[1]], axis=1)
            send = jnp.concatenate([send, out[0]], axis=1)
        sums.add(("small", g), [keep], send, quick=True)

    out = call(
        functools.partial(out_grad_kernel, nb, G),
        (shape((lead, orows, 256), BF),) * 2,
        1e9,
        4e6,
        in_specs=[SM] + [VM] * (nb + G),
        out_specs=(VM, VM),
        name="out_grad",
    )(scal, *branches, *own_att)
    ys = [attend_back(0, q, kd)]
    msgs = head_grad(0, ys[0])
    q, kd, *got, mix_far = sums.advance((q, kd, *msgs, *out), (mix_far,))
    msgs, out = got[:n], got[n:]
    arrived = [msgs[0]] + [px(msgs[m], m) for m in range(1, n)]
    if G == 2:
        ys.append(attend_back(1, q, kd))
    got = tie((*ys, *arrived), ())
    ys, arrived = got[:G], got[G:]
    add_small(0, arrived, out)
    arrived = []
    if G == 2:
        msgs = head_grad(1, ys[1])
        ys = tie(ys, msgs[:1])
        arrived = [msgs[0]] + [px(msgs[m], m) for m in range(1, n)]
    back = call(
        functools.partial(back_kernel, T, G),
        (shape((T, D), BF),) * n,
        1e9,
        8e6,
        in_specs=[VM] * (1 + G),
        out_specs=(VM,) * n,
        name="back",
    )(w_cols, *ys)
    came = scatter(back)
    came[0], *arrived = sums.advance(came[:1], arrived)
    if G == 2:
        add_small(1, arrived)
    k = len(came)
    got = sums.advance((), (*came, *mix))
    came, mix = got[:k], got[k:]
    mix = [mix[0], mix_far] + [px(mix[m], m) for m in range(n - 2, 0, -1)]
    (d_tokens,) = norm_back(came, hidden_grad, tokens, gain_a, False)
    finishing(E // 2)
    (d_tokens,) = tie_finished((d_tokens,))
    (d_tokens,) = sums.advance((d_tokens,))
    finishing(E - 1)
    (d_tokens,) = tie_finished((d_tokens,))
    while sums.live:
        finishing(E)
        (d_tokens,) = tie_finished((d_tokens,))
        (d_tokens,) = sums.advance((d_tokens,))
    finishing(E)
    mixed = mixed_sum(hidden, mix)
    g_gate, g_up, g_down = prev

    if G == 2:
        one, two = sums.whole(("small", 0)), sums.whole(("small", 1))
        g_ga, g_q, g_k, g_v, g_out_all, g_gf = call(
            functools.partial(last_kernel, n, r),
            (
                shape((1, r), F32),
                shape((r, QUERY_HEADS * HEAD), F32),
                shape((r, KEY_VALUE_HEADS * HEAD), F32),
                shape((r, KEY_VALUE_HEADS * HEAD), F32),
                shape((r, D), F32),
                shape((1, r), F32),
            ),
            1e6,
            5e6,
            in_specs=[SM] + [VM] * 5,
            out_specs=(VM,) * 6,
            name="last",
        )(scal, one[0], two[0], one[1], two[1], gain_attn.reshape(1, r))
        g_ga, g_gf = g_ga.reshape(r), g_gf.reshape(r)
    else:
        v, other = sums.whole(("small", 0))
        v = jnp.where(core == 0, jnp.stack([v, other]), jnp.stack([other, v])).astype(F32)
        g_out_all = v[:, :, r + 16 :, :].reshape(2, D // 256, r // 2, 256)
        g_out_all = g_out_all.transpose(0, 2, 1, 3).reshape(r, D)
        v = v[:, :, : r + 16].reshape(n, r + 16, 256)
        in_order = [at(v, me ^ j)[:r] for j in range(n)]
        g_q, g_k, g_v = [
            jnp.concatenate([b[:, lo:hi] for b in in_order], axis=1)
            for lo, hi in ((0, 128), (128, 192), (192, 256))
        ]
        g_ga = jnp.sum(v[:, r, :r], axis=0) / gain_attn.astype(F32)
        g_gf = jnp.sum(v[:, r + 1, :r], axis=0)
    return (mixed, d_tokens, g_ga, g_q, g_k, g_v, g_out_all, g_gf, g_gate, g_up, g_down)


def solution(mesh):
    rows = P(("rep", "shard"), None)
    own = P("shard", None)
    own3 = P("shard", None, None)
    vec = P("shard")
    return jax.shard_map(
        per_device,
        mesh=mesh,
        in_specs=(
            rows,
            rows,
            rows,
            rows,
            P("rep", None),
            vec,
            own,
            own,
            own,
            own,
            vec,
            own3,
            own3,
            own3,
        ),
        out_specs=(rows, rows, vec, own, own, own, own, vec, own3, own3, own3),
        check_vma=False,
    )
```

```python
import functools
import math

import jax
import jax.numpy as jnp
from jax import lax
from jax.experimental import pallas as pl
from jax.experimental.pallas import tpu as pltpu
from jax.sharding import PartitionSpec as P

QUERY_HEADS = 16
KEY_VALUE_HEADS = 8
HEAD = 64
EXPERTS = 16
PROMPT = 1024
EPS = 1e-06
F32 = jnp.float32
BF = jnp.bfloat16
TILE = 256
VMEM_LIMIT = 26 * 1024 * 1024


def nn(a, b):
    return lax.dot_general(a, b, (((1,), (0,)), ((), ())), preferred_element_type=F32)


def nt(a, b):
    return lax.dot_general(a, b, (((1,), (1,)), ((), ())), preferred_element_type=F32)


def tn(a, b):
    return lax.dot_general(a, b, (((0,), (0,)), ((), ())), preferred_element_type=F32)


COST = 0.25


def call(kernel, out_shape, flops, nbytes, trans=0, **kw):
    return pl.pallas_call(
        kernel,
        out_shape=out_shape,
        compiler_params=pltpu.CompilerParams(vmem_limit_bytes=VMEM_LIMIT),
        cost_estimate=pl.CostEstimate(
            flops=int(COST * flops), bytes_accessed=int(COST * nbytes), transcendentals=int(COST * trans)
        ),
        **kw,
    )


VM = pl.BlockSpec(memory_space=pltpu.VMEM)
SM = pl.BlockSpec(memory_space=pltpu.SMEM)


def shape(dims, dtype):
    return jax.ShapeDtypeStruct(dims, dtype)


class Geo:
    def __init__(self, n, rows, conts):
        self.n = n
        self.T = rows
        self.PS = PROMPT // n
        self.CT = conts
        self.CS = conts // n
        self.TG = PROMPT + conts
        self.G = KEY_VALUE_HEADS // n
        self.relay = n == 4

    def pieces(self):
        out = [(m, 0, self.T) for m in range(self.n)]
        if self.relay:
            half = self.T // 2
            out = out[:-1] + [(3, 0, half), (3, half, half)]
        return out

    def places(self, me, m, off, rows):
        j = me ^ m
        out = []
        lead = max(0, min(self.PS, off + rows) - off)
        if lead:
            out.append((0, lead, pl.multiple_of(j * self.PS + off, 32)))
        if rows > lead:
            start = off + lead - self.PS
            out.append((lead, rows - lead, pl.multiple_of(PROMPT + j * self.CS + start, 32)))
        return out

    def tiles(self):
        out = []
        for i in range(PROMPT // TILE):
            ks = [(0, i * TILE, 0)] if i else []
            out.append((i * TILE, ks + [(i * TILE, TILE, 1)]))
        for c in range(self.CT // TILE):
            ks = [(0, PROMPT, 0)]
            if c:
                ks.append((PROMPT + (c - 1) * TILE, TILE, 2))
            ks.append((PROMPT + c * TILE, TILE, 3))
            out.append((PROMPT + c * TILE, ks))
        return out

    def spread(self, me, start):
        out = []
        if start < PROMPT:
            step = min(self.PS, TILE)
            for a in range(0, TILE, step):
                j = (start + a) // self.PS
                off = (start + a) % self.PS
                out.append((a, step, pl.multiple_of((me ^ j) * self.T + off, 32)))
        else:
            step = min(self.CS, TILE)
            for a in range(0, TILE, step):
                j = (start - PROMPT + a) // self.CS
                off = (start - PROMPT + a) % self.CS
                out.append((a, step, pl.multiple_of((me ^ j) * self.T + self.PS + off, 32)))
        return out


def iota(dims, axis):
    return lax.broadcasted_iota(jnp.int32, dims, axis)


def swap_halves(v):
    lane = iota(v.shape, 1)
    first = (lane & 32) == 0
    return jnp.where(first, pltpu.roll(v, 96, 1), pltpu.roll(v, 32, 1))


def masked(s, kind, q0, k0, segc_ref, segr_ref):
    if kind == 0:
        return s
    ok = None
    if kind != 2:
        ok = iota(s.shape, 0) <= iota(s.shape, 1)
    if kind != 1:
        same = segc_ref[k0 - PROMPT : k0 - PROMPT + TILE, :] == segr_ref[:, q0 - PROMPT : q0 - PROMPT + TILE]
        ok = same if ok is None else ok & same
    return jnp.where(ok, s, -1e30)


def qkv_kernel(geo, me_ref, *refs):
    np_ = len(geo.pieces())
    toks = refs[:np_]
    n = geo.n
    msgs = refs[np_ : np_ + n]
    c_ref, s_ref = refs[np_ + n : np_ + n + 2]
    (normed_ref, q_ref, kd_ref, vd_ref, kt_ref, vt_ref, w_ref, ga_ref, gf_ref, raw) = refs[
        np_ + n + 2 :
    ]
    me = me_ref[0]
    G = geo.G
    r = msgs[0].shape[0] - 16
    for m, msg in enumerate(msgs):
        w_ref[pl.ds(pl.multiple_of((me ^ m) * r, 128), r), :] = msg[:r, :]
        gains = msg[r : r + 16, :].astype(F32)[:1, :]
        for j in range(n):

            @pl.when((me ^ m) == j)
            def _():
                ga_ref[:, j * r : (j + 1) * r] = gains[:, :r]
                gf_ref[:, j * r : (j + 1) * r] = gains[:, r : 2 * r]

    gain = ga_ref[...]
    for (m, off, rows), tok in zip(geo.pieces(), toks):
        v = tok[...].astype(F32)
        r = lax.rsqrt(jnp.mean(v * v, axis=-1, keepdims=True) + EPS)
        x = (v * r * gain).astype(BF)
        normed_ref[m * geo.T + off : m * geo.T + off + rows, :] = x
        y = nn(x, w_ref[...])
        for a, cnt, dst in geo.places(me, m, off, rows):
            raw[pl.ds(dst, cnt), :] = y[a : a + cnt, :]
    for t in range(0, geo.TG, TILE):
        rows = slice(t, t + TILE)
        cos, sin = c_ref[rows, :], s_ref[rows, :]
        low = iota((TILE, 128), 1) < 64
        for g in range(G):
            v = raw[rows, g * 256 : g * 256 + 128]
            q = (v * cos + swap_halves(v) * sin).astype(BF).astype(F32) * 0.125
            q_ref[2 * g, rows, :] = jnp.where(low, q, 0.0).astype(BF)
            q_ref[2 * g + 1, rows, :] = jnp.where(low, 0.0, q).astype(BF)
            kv = raw[rows, g * 256 + 128 : g * 256 + 256]
            vk = pltpu.roll(kv, 64, 1)
            k = jnp.where(low, kv, vk)
            k = (k * cos + swap_halves(k) * sin).astype(BF)
            v = jnp.where(low, vk, kv)
            kd_ref[g, rows, :] = k
            vd_ref[g, rows, :] = v.astype(BF)
            kt_ref[g, :, rows] = k.astype(F32).T[:64, :].astype(BF)
            vt_ref[g, :, rows] = v.T[:64, :].astype(BF)


def columns_kernel(geo, me_ref, wq_ref, wk_ref, wv_ref, ga_ref, gf_ref, *outs):
    me = me_ref[0]
    r = wq_ref.shape[0]
    low = iota((r, 128), 1) < 64
    gains = jnp.concatenate([ga_ref[...], gf_ref[...]], axis=1)
    gains = jnp.broadcast_to(gains, (16, gains.shape[1]))
    for j in range(geo.n):
        cols = []
        for g in range(geo.G):
            h = j * geo.G + g
            pair = slice(h // 2 * 128, h // 2 * 128 + 128)
            k = wk_ref[:, pair].astype(F32)
            v = wv_ref[:, pair].astype(F32)
            if h % 2 == 0:
                kv = jnp.where(low, k, pltpu.roll(v, 64, 1))
            else:
                kv = jnp.where(low, pltpu.roll(k, 64, 1), v)
            cols += [wq_ref[:, h * 128 : h * 128 + 128], kv.astype(BF)]
        block = jnp.concatenate(cols, axis=1)
        for m, out in enumerate(outs):

            @pl.when((me ^ m) == j)
            def _():
                out[:r, :] = block
                out[r:, :] = gains


def pack_kernel(d_ref, r_ref, g_ref, segc_ref, segr_ref, out_ref, c_ref, s_ref):
    D = d_ref.shape[1]
    out_ref[:, :D] = d_ref[...]
    lane = iota((d_ref.shape[0], 128), 1)
    gate = jnp.zeros(lane.shape, F32)
    for k in range(r_ref.shape[1]):
        hit = (lane & (EXPERTS - 1)) == r_ref[:, k : k + 1]
        gate = gate + jnp.where(hit, g_ref[:, k : k + 1], 0.0)
    top = gate.astype(BF).astype(F32)
    mid = (gate - top).astype(BF).astype(F32)
    low = gate - top - mid
    term = jnp.where(lane < EXPERTS, top, jnp.where(lane < 2 * EXPERTS, mid, low))
    out_ref[:, D:] = jnp.where(lane < 3 * EXPERTS, term, 0.0).astype(BF)

    lane = iota((1, 128), 1)
    freq = jnp.exp((lane & 31).astype(F32) * (-2.0 * math.log(10000.0) / HEAD))
    sign = jnp.where((lane & 32) == 0, -1.0, 1.0)
    for t in range(0, c_ref.shape[0], TILE):
        row = iota((TILE, 1), 0).astype(F32) + float(t)
        if t >= PROMPT:
            own = segc_ref[t - PROMPT : t - PROMPT + TILE, :]
            start = jnp.sum(jnp.where(segr_ref[...] < own, 1.0, 0.0), axis=1, keepdims=True)
            row = row - start
        ang = row * freq
        c_ref[t : t + TILE, :] = jnp.cos(ang)
        s_ref[t : t + TILE, :] = jnp.sin(ang) * sign


def att_kernel(geo, me_ref, q_ref, kd_ref, vt_ref, segc_ref, segr_ref, o_ref, lse_ref):
    me = me_ref[0]
    for q0, keys in geo.tiles():
        outs = []
        for h in range(2):
            q = q_ref[h, q0 : q0 + TILE, :]
            ss = [
                masked(nt(kd_ref[0, k0 : k0 + kn, :], q), kind, q0, k0, segc_ref, segr_ref)
                for k0, kn, kind in keys
            ]
            top = functools.reduce(
                jnp.maximum, [jnp.max(s, axis=0, keepdims=True) for s in ss]
            )
            ps = [jnp.exp(s - top) for s in ss]
            total = functools.reduce(
                jnp.add, [jnp.sum(p, axis=0, keepdims=True) for p in ps]
            )
            lse_ref[h, :, q0 : q0 + TILE] = top + jnp.log(total)
            inv = 1.0 / total
            acc = None
            for p, (k0, kn, kind) in zip(ps, keys):
                part = nn(vt_ref[0, :, k0 : k0 + kn], (p * inv).astype(BF))
                acc = part if acc is None else acc + part
            outs.append(acc)
        o = jnp.concatenate(outs, axis=0).T.astype(BF)
        for a, cnt, dst in geo.spread(me, q0):
            o_ref[pl.ds(dst, cnt), :] = o[a : a + cnt, :]


def hidden_kernel(geo, natt, s_ref, *refs):
    pieces = geo.pieces()
    np_ = len(pieces)
    atts = refs[:natt]
    toks = refs[natt : natt + np_]
    mine_ref, other_ref, gain_ref = refs[natt + np_ : natt + np_ + 3]
    hid_ref, x_ref, w_ref = refs[natt + np_ + 3 :]
    half = mine_ref.shape[0] // geo.n
    for m in range(geo.n):
        own = pl.multiple_of((2 * m + s_ref[0]) * half, 64)
        sib = pl.multiple_of((2 * m + 1 - s_ref[0]) * half, 64)
        w_ref[pl.ds(own, half), :] = mine_ref[m * half : (m + 1) * half, :]
        w_ref[pl.ds(sib, half), :] = other_ref[m * half : (m + 1) * half, :]
    gain = gain_ref[...].astype(F32)
    index = {}
    k = 0
    for g in range(geo.G):
        for m, off, rows in att_pieces(geo):
            index[(m, g, off)] = (atts[k], off, rows)
            k += 1

    def att_rows(m, g, row, cnt):
        for (mm, gg, _), (ref, off, rows) in index.items():
            if mm == m and gg == g and off <= row and row + cnt <= off + rows:
                return ref[row - off : row - off + cnt, :]
        raise ValueError("piece")

    for (j, off, rows), tok in zip(pieces, toks):
        lhs = jnp.concatenate(
            [
                att_rows(m, g, (m ^ j) * geo.T + off, rows)
                for m in range(geo.n)
                for g in range(geo.G)
            ],
            axis=1,
        )
        h = tok[...].astype(F32) + nn(lhs, w_ref[...])
        if j == 0:
            hid_ref[...] = h
        r = lax.rsqrt(jnp.mean(h * h, axis=-1, keepdims=True) + EPS)
        x_ref[j * geo.T + off : j * geo.T + off + rows, :] = (h * r * gain).astype(BF)


def att_pieces(geo):
    rows = geo.n * geo.T
    out = [(m, 0, rows) for m in range(geo.n)]
    if geo.relay:
        out = out[:-1] + [(3, 0, rows // 2), (3, rows // 2, rows // 2)]
    return out


CH = 1


def expert_rows(x, dout, wg, wu, wd, gate):
    g = nn(x, wg)
    u = nn(x, wu)
    back = nt(dout, wd) * gate
    s = 1.0 / (1.0 + jnp.exp(-g))
    sil = g * s
    act = (sil * u * gate).astype(BF)
    gg = (back * u * (s + sil * (1.0 - s))).astype(BF)
    ug = (back * sil).astype(BF)
    return act, gg, ug


def gate_column(gm_ref, expert):
    lane = iota(gm_ref.shape, 1)
    mine = (lane == expert) | (lane == EXPERTS + expert) | (lane == 2 * EXPERTS + expert)
    return jnp.sum(jnp.where(mine, gm_ref[...].astype(F32), 0.0), axis=1, keepdims=True)


def put_grads(outs, x_ref, do_ref, gg_ref, ug_ref, ac_ref):
    cols = x_ref.shape[1] // len(outs)
    for k, out in enumerate(outs):
        x = x_ref[:, k * cols : (k + 1) * cols]
        out[0] = tn(x, gg_ref[...]).astype(BF)
        out[1] = tn(x, ug_ref[...]).astype(BF)
        out[2] = tn(do_ref[:, k * cols : (k + 1) * cols], ac_ref[...]).astype(BF)


def expert_kernel(n, T, E, e, s_ref, *refs):
    x_ref, do_ref, gm_ref, wg_ref, wu_ref, wd_ref, xc_ref, dc_ref = refs[:8]
    act_ref, gg_ref, ug_ref, send = refs[-7 - CH : -3 - CH]
    keeps = refs[-3 - CH : -3]
    gg_s, ug_s, ac_s = refs[-3:]
    r = pl.program_id(0)

    @pl.when(r < n)
    def _():
        act, gg, ug = expert_rows(
            x_ref[...],
            do_ref[...],
            wg_ref[0],
            wu_ref[0],
            wd_ref[0],
            gate_column(gm_ref, s_ref[1] * E + e),
        )
        rows = pl.ds(pl.multiple_of(r * T, 128), T)
        gg_s[rows, :] = gg
        ug_s[rows, :] = ug
        ac_s[rows, :] = act
        act_ref[...] = act
        gg_ref[...] = gg
        ug_ref[...] = ug

    @pl.when(r == n)
    def _():
        put_grads([send], xc_ref, dc_ref, gg_s, ug_s, ac_s)

    @pl.when(r == n + 1)
    def _():
        put_grads(keeps, xc_ref, dc_ref, gg_s, ug_s, ac_s)


def expert(n, T, E, e, scal, x, dout, wg, wu, wd, kept):
    D, M = wg.shape[1:]
    row = lambda r, c: (jnp.minimum(r, n - 1), 0)
    gate = lambda r, c: (jnp.minimum(r, n - 1), D // 128)
    half = lambda r, c: (0, jnp.where(r == n + 1, c[0], 1 - c[0]))
    fix = lambda r, c: (e, 0, 0)
    whole = lambda r, c: (0, 0, 0)
    block = pl.BlockSpec((T, M), lambda r, c: (jnp.minimum(r, n - 1), e))
    in_specs = [
        pl.BlockSpec((T, D), row),
        pl.BlockSpec((T, D), row),
        pl.BlockSpec((T, 128), gate),
        pl.BlockSpec((1, D, M), fix),
        pl.BlockSpec((1, D, M), fix),
        pl.BlockSpec((1, M, D), fix),
        pl.BlockSpec((n * T, D // 2), half),
        pl.BlockSpec((n * T, D // 2), half),
    ]
    args = [x, dout, dout, wg, wu, wd, x, dout]
    alias = {}
    if kept is not None:
        in_specs += [pl.BlockSpec(memory_space=pl.ANY)] * 3
        args += list(kept)
        alias = {9: 0, 10: 1, 11: 2}
    out = call(
        functools.partial(expert_kernel, n, T, E, e),
        (pltpu.HBM((n * T, E * M), BF),) * 3
        + (shape((3, D // 2, M), BF),)
        + (shape((3, D // 2 // CH, M), BF),) * CH,
        12 * n * T * D * M,
        20e6,
        grid_spec=pltpu.PrefetchScalarGridSpec(
            num_scalar_prefetch=1,
            grid=(n + 2,),
            in_specs=in_specs,
            out_specs=(block,) * 3
            + (pl.BlockSpec((3, D // 2, M), whole),)
            + (pl.BlockSpec((3, D // 2 // CH, M), whole),) * CH,
            scratch_shapes=[pltpu.VMEM((n * T, M), BF)] * 3,
        ),
        input_output_aliases=alias,
        name=f"expert{e}",
    )(scal, *args)
    return out[:3], out[3], out[4:]


def forward_kernel(E, e0, s_ref, x_ref, do_ref, gm_ref, wg_ref, wu_ref, wd_ref, *refs):
    act_ref, gg_ref, ug_ref = refs[-3:]
    act, gg, ug = expert_rows(
        x_ref[...],
        do_ref[...],
        wg_ref[0],
        wu_ref[0],
        wd_ref[0],
        gate_column(gm_ref, s_ref[1] * E + e0 + pl.program_id(0)),
    )
    act_ref[...] = act
    gg_ref[...] = gg
    ug_ref[...] = ug


def forwards(n, T, E, e0, scal, x, dout, wg, wu, wd, kept):
    D, M = wg.shape[1:]
    R = n * T // 2
    any_ = pl.BlockSpec(memory_space=pl.ANY)
    row = pl.BlockSpec((R, D), lambda i, r, c: (r, 0))
    fix = lambda i, r, c: (e0 + i, 0, 0)
    block = pl.BlockSpec((R, M), lambda i, r, c: (r, e0 + i))
    return call(
        functools.partial(forward_kernel, E, e0),
        (pltpu.HBM((n * T, E * M), BF),) * 3,
        6 * (E - e0) * n * T * D * M,
        (E - e0) * 12e6,
        grid_spec=pltpu.PrefetchScalarGridSpec(
            num_scalar_prefetch=1,
            grid=(E - e0, 2),
            in_specs=[
                row,
                row,
                pl.BlockSpec((R, 128), lambda i, r, c: (r, D // 128)),
                pl.BlockSpec((1, D, M), fix),
                pl.BlockSpec((1, D, M), fix),
                pl.BlockSpec((1, M, D), fix),
                any_,
                any_,
                any_,
            ],
            out_specs=(block,) * 3,
        ),
        input_output_aliases={7: 0, 8: 1, 9: 2},
        name="forwards",
    )(scal, x, dout, dout, wg, wu, wd, *kept)


def input_grad_kernel(E, T, gg_ref, ug_ref, wg_ref, wu_ref, *refs):
    outs, acc = refs[:-1], refs[-1]
    i = pl.program_id(0)
    v = nt(gg_ref[...], wg_ref[0]) + nt(ug_ref[...], wu_ref[0])

    @pl.when(i == 0)
    def _():
        acc[...] = v

    @pl.when(i > 0)
    def _():
        acc[...] += v

    @pl.when(i == E - 1)
    def _():
        put_blocks(T, acc, outs)


def input_grad(T, E, first, rows, gg, ug, wg, wu):
    D, M = wg.shape[1:]
    R = sum(rows)
    block = pl.BlockSpec((R, M), lambda i: (first // R, i))
    weight = pl.BlockSpec((1, D, M), lambda i: (i, 0, 0))
    return call(
        functools.partial(input_grad_kernel, E, T),
        tuple(shape((v, D), BF) for v in rows),
        4 * E * R * D * M,
        16e6,
        grid=(E,),
        in_specs=[block, block, weight, weight],
        out_specs=tuple(pl.BlockSpec((v, D), lambda i: (0, 0)) for v in rows),
        scratch_shapes=[pltpu.VMEM((R, D), F32)],
        name=f"input_grad{first}",
    )(gg, ug, wg, wu)


def weight_grad_kernel(s_ref, x_ref, do_ref, gg_ref, ug_ref, ac_ref, send, *keeps):
    @pl.when(pl.program_id(0) == 0)
    def _():
        put_grads([send], x_ref, do_ref, gg_ref, ug_ref, ac_ref)

    @pl.when(pl.program_id(0) == 1)
    def _():
        put_grads(keeps, x_ref, do_ref, gg_ref, ug_ref, ac_ref)


def weight_grad(M, e, scal, x, dout, act, gg, ug):
    R, D = x.shape
    half = lambda s, c: (0, jnp.where(s == 1, c[0], 1 - c[0]))
    whole = lambda s, c: (0, 0, 0)
    block = pl.BlockSpec((R, M), lambda s, c: (0, e))
    out = call(
        weight_grad_kernel,
        (shape((3, D // 2, M), BF),) + (shape((3, D // 2 // CH, M), BF),) * CH,
        6 * R * D * M,
        14e6,
        grid_spec=pltpu.PrefetchScalarGridSpec(
            num_scalar_prefetch=1,
            grid=(2,),
            in_specs=[
                pl.BlockSpec((R, D // 2), half),
                pl.BlockSpec((R, D // 2), half),
                block,
                block,
                block,
            ],
            out_specs=(pl.BlockSpec((3, D // 2, M), whole),)
            + (pl.BlockSpec((3, D // 2 // CH, M), whole),) * CH,
        ),
        name=f"weight_grad{e}",
    )(scal, x, dout, gg, ug, act)
    return out[0], out[1:]


def norm_back_kernel(count, low, *refs):
    parts = refs[:count]
    base_ref, v_ref, gain_ref = refs[count : count + 3]
    outs = refs[count + 3 :]
    grad = parts[0][...].astype(F32)
    for p in parts[1:]:
        grad = grad + p[...].astype(F32)
    v = v_ref[...].astype(F32)
    r = lax.rsqrt(jnp.mean(v * v, axis=-1, keepdims=True) + EPS)
    gv = gain_ref[...].astype(F32) * grad
    res = (
        base_ref[...].astype(F32)
        + r * gv
        - v * (r * r * r * jnp.mean(gv * v, axis=-1, keepdims=True))
    )
    outs[0][...] = res
    if low:
        outs[1][...] = res.astype(BF)
        part = jnp.sum(grad * v * r, axis=0, keepdims=True)

        @pl.when(pl.program_id(0) == 0)
        def _():
            outs[2][...] = part

        @pl.when(pl.program_id(0) > 0)
        def _():
            outs[2][...] += part


def norm_back(parts, base, v, gain, low):
    T, D = v.shape
    B = 128
    row = pl.BlockSpec((B, D), lambda i: (i, 0))
    one = pl.BlockSpec((1, D), lambda i: (0, 0))
    out = [shape((T, D), F32)]
    specs = [row]
    if low:
        out += [shape((T, D), BF), shape((1, D), F32)]
        specs += [row, one]
    return call(
        functools.partial(norm_back_kernel, len(parts), low),
        tuple(out),
        20 * T * D,
        T * D * 16,
        grid=(T // B,),
        in_specs=[row] * len(parts) + [row, row, one],
        out_specs=tuple(specs),
        name="norm_back",
    )(*parts, base, v, gain)


def att_back_kernel(geo, gi, me_ref, *refs):
    pieces = geo.pieces()
    np_ = len(pieces)
    brs = refs[:np_]
    (w_ref, q_ref, kd_ref, kt_ref, vd_ref, lse_ref, segc_ref, segr_ref, c_ref, s_ref) = refs[
        np_ : np_ + 10
    ]
    out_ref, do_s, dk_s, dv_s, dq_s = refs[np_ + 10 :]
    me = me_ref[0]
    for (m, off, rows), br in zip(pieces, brs):
        y = nt(br[...], w_ref[...])
        low = iota((rows, 128), 1) < 64
        lo = jnp.where(low, y, 0.0).astype(BF)
        hi = jnp.where(low, 0.0, y).astype(BF)
        for a, cnt, dst in geo.places(me, m, off, rows):
            do_s[0, pl.ds(dst, cnt), :] = lo[a : a + cnt, :]
            do_s[1, pl.ds(dst, cnt), :] = hi[a : a + cnt, :]
    dk_s[...] = jnp.zeros_like(dk_s)
    dv_s[...] = jnp.zeros_like(dv_s)

    def head(i, carry):
        g = 0
        for q0, keys in geo.tiles():
            q = q_ref[i, q0 : q0 + TILE, :]
            do = do_s[i, q0 : q0 + TILE, :]
            lse = lse_ref[i, :, q0 : q0 + TILE]
            ps, dps = [], []
            delta = None
            for k0, kn, kind in keys:
                s = masked(nt(kd_ref[g, k0 : k0 + kn, :], q), kind, q0, k0, segc_ref, segr_ref)
                p = jnp.exp(s - lse)
                dp = nt(vd_ref[g, k0 : k0 + kn, :], do)
                dv_s[g, k0 : k0 + kn, :] += nn(p.astype(BF), do)
                d = jnp.sum(p * dp, axis=0, keepdims=True)
                delta = d if delta is None else delta + d
                ps.append(p)
                dps.append(dp)
            acc = None
            for p, dp, (k0, kn, kind) in zip(ps, dps, keys):
                ds = (p * (dp - delta)).astype(BF)
                dk_s[g, k0 : k0 + kn, :] += nn(ds, q)
                part = nn(kt_ref[g, :, k0 : k0 + kn], ds)
                acc = part if acc is None else acc + part
            dq_s[i, :, q0 : q0 + TILE] = acc
        return carry

    lax.fori_loop(0, 2, head, 0)
    low = iota((TILE, 128), 1) < 64
    for t in range(0, geo.TG, TILE):
        rows = slice(t, t + TILE)
        cos, sin = c_ref[rows, :], s_ref[rows, :]
        v = jnp.concatenate([dq_s[0, :, rows], dq_s[1, :, rows]], axis=0).T * 0.125
        dq = v * cos - swap_halves(v) * sin
        k = dk_s[0, rows, :]
        k = k + pltpu.roll(k, 64, 1)
        k = k * cos - swap_halves(k) * sin
        v = dv_s[0, rows, :]
        for x, col in enumerate((dq, jnp.where(low, k, v + pltpu.roll(v, 64, 1)))):
            y = col.astype(BF)
            for a, cnt, dst in geo.spread(me, t):
                out_ref[pl.ds(dst, cnt), x * 128 : x * 128 + 128] = y[a : a + cnt, :]


def mix_kernel(T, act_ref, w_ref, *refs):
    outs, acc = refs[:-1], refs[-1]
    i = pl.program_id(0)
    v = nn(act_ref[...], w_ref[0])

    @pl.when(i == 0)
    def _():
        acc[...] = v

    @pl.when(i > 0)
    def _():
        acc[...] += v

    @pl.when(i == pl.num_programs(0) - 1)
    def _():
        put_blocks(T, acc, outs)


def mix_parts(n, T, rows, act, wd):
    E, M, D = wd.shape
    return call(
        functools.partial(mix_kernel, T),
        (shape((T, D), F32),) + tuple(shape((v, D), BF) for v in rows[1:]),
        2 * n * T * E * M * D,
        10e6,
        grid=(E,),
        in_specs=[
            pl.BlockSpec((n * T, M), lambda i: (0, i)),
            pl.BlockSpec((1, M, D), lambda i: (i, 0, 0)),
        ],
        out_specs=tuple(pl.BlockSpec((v, D), lambda i: (0, 0)) for v in rows),
        scratch_shapes=[pltpu.VMEM((n * T, D), F32)],
        name="mix",
    )(act, wd)


def back_kernel(T, G, w_ref, *refs):
    ys, outs = refs[:G], refs[G:]
    at = 0
    for out in outs:
        rows = out.shape[0]
        v = None
        for g, y in enumerate(ys):
            p = nt(y[at : at + rows, :], w_ref[:, g * 256 : (g + 1) * 256])
            v = p if v is None else v + p
        out[...] = v.astype(BF)
        at += rows


def head_grad_kernel(geo, first, s_ref, x_ref, y_ref, w_ref, gf_ref, *outs):
    me = s_ref[1]
    r = w_ref.shape[0] // geo.n
    ones = jnp.ones((16, 256), BF)
    row = iota((16, 256), 0)
    for j in range(geo.n):
        dw = tn(x_ref[:, j * r : (j + 1) * r], y_ref[...])
        prod = dw * w_ref[j * r : (j + 1) * r, :].astype(F32)
        hi = prod.astype(BF)
        lo = (prod - hi.astype(F32)).astype(BF)
        gain = nt(ones, hi) + nt(ones, lo)
        below = gf_ref[:, j * r : (j + 1) * r] if first else jnp.zeros((1, r), F32)
        if r < 256:
            gain = jnp.concatenate([gain, jnp.zeros((16, 256 - r), F32)], axis=1)
            below = jnp.concatenate([below, jnp.zeros((1, 256 - r), F32)], axis=1)
        extra = jnp.where(row == 0, gain, jnp.where(row == 1, below, 0.0)).astype(BF)
        low = dw.astype(BF)
        for m, out in enumerate(outs):

            @pl.when((me ^ m) == j)
            def _():
                out[:r, :] = low
                out[r:, :] = extra


def out_grad_kernel(np_, G, s_ref, *refs):
    brs, atts = refs[:np_], refs[np_ : np_ + G]
    send, keep = refs[np_ + G], refs[np_ + G + 1]
    per = []
    for o in atts:
        v, at_ = None, 0
        for br in brs:
            rows = br.shape[0]
            p = tn(o[at_ : at_ + rows, :], br[...])
            v = p if v is None else v + p
            at_ += rows
        per.append(v)
    v = jnp.concatenate(per, axis=0).astype(BF)
    lead, rows = send.shape[0], send.shape[1]
    half = v.shape[0] // 2
    count = rows // half

    def put(out, top):
        for a in range(lead):
            for b in range(count):
                c = (a * count + b) * 256
                out[a, b * half : (b + 1) * half, :] = v[top : top + half, c : c + 256]

    @pl.when(s_ref[0] == 0)
    def _():
        put(keep, 0)
        put(send, half)

    @pl.when(s_ref[0] == 1)
    def _():
        put(keep, half)
        put(send, 0)


def combine_kernel(ops, wide, k, *refs):
    end = (refs[0][0] == 0) | (refs[0][0] == refs[0][1])
    ins, outs = refs[1 : 1 + k], refs[len(refs) - len(ops) :]

    def plus(a, b):
        return (ins[a][...].astype(F32) + ins[b][...].astype(F32)).astype(BF)

    for (kind, *at), w, out in zip(ops, wide, outs):

        def work():
            if kind == "add":
                out[...] = plus(*at)
                return

            @pl.when(end)
            def _():
                out[...] = plus(*at[:2]) if kind == "merge" else ins[at[0]][...]

            @pl.when(jnp.logical_not(end))
            def _():
                out[...] = plus(*at[2:]) if kind == "merge" else ins[at[1]][...]

        if w:
            work()
        else:
            pl.when((pl.program_id(0) == 0) & (pl.program_id(1) == 0))(work)


def combine(pos, ops):
    arrays, specs, keys, coded, outs, out_specs, wide = [], [], [], [], [], [], []

    def spec(w, block, part):
        if w:
            half = (1, block[0] // 2, block[1])
            return pl.BlockSpec(half, lambda i, h, p: (i, 2 * part + h, 0))
        return pl.BlockSpec(block, lambda i, h, p: (0,) * len(block))

    for kind, args, place in ops:
        a = args[0][0]
        w = a.shape[0] == 3
        block = a.shape[1:] if w else a.shape
        at = []
        for v, part in args:
            key = (id(v), part)
            if key not in keys:
                keys.append(key)
                arrays.append(v)
                specs.append(spec(w, block, part))
            at.append(keys.index(key))
        coded.append((kind, *at))
        wide.append(w)
        if place is None:
            outs.append(shape(a.shape, BF))
            out_specs.append(spec(w, block, 0))
        else:
            outs.append(shape((3, CH * block[0], block[1]), BF))
            out_specs.append(spec(w, block, place[1]))
    k = len(arrays)
    alias = {}
    for i, (_, _, place) in enumerate(ops):
        if place is not None and place[0] is not None:
            alias[1 + len(arrays)] = i
            arrays.append(place[0])
            specs.append(pl.BlockSpec(memory_space=pl.ANY))
    out = call(
        functools.partial(combine_kernel, coded, wide, k),
        tuple(outs),
        1e6,
        1e6,
        grid_spec=pltpu.PrefetchScalarGridSpec(
            num_scalar_prefetch=1,
            grid=(3, 2),
            in_specs=specs,
            out_specs=tuple(out_specs),
        ),
        input_output_aliases=alias,
        name="combine",
    )(pos, *arrays)
    return list(out)


def put_blocks(T, acc, outs, first=0):
    at = first
    for out in outs:
        rows = out.shape[0]
        out[...] = acc[at : at + rows, :].astype(out.dtype)
        at += rows


def finish_kernel(e, first, c_ref, own_ref, sib_ref, *refs):
    g_ref, u_ref, d_ref = refs if first else refs[3:]

    def put(src):
        g_ref[0] = src[0].astype(F32)
        u_ref[0] = src[1].astype(F32)
        d_ref[0] = src[2].astype(F32).T

    @pl.when(pl.program_id(0) < 2)
    def _():
        put(own_ref)

    @pl.when(pl.program_id(0) >= 2)
    def _():
        put(sib_ref)


def finish(e, E, core, own, sib, prev):
    _, Dh, M = own.shape
    rows = Dh // 2
    first = prev is None
    half = lambda s, c: jnp.where(s < 2, 2 * c[0] + s, 2 * (1 - c[0]) + s - 2)
    any_ = pl.BlockSpec(memory_space=pl.ANY)
    return call(
        functools.partial(finish_kernel, e, first),
        (
            shape((E, 2 * Dh, M), F32),
            shape((E, 2 * Dh, M), F32),
            shape((E, M, 2 * Dh), F32),
        ),
        1e6,
        10e6,
        grid_spec=pltpu.PrefetchScalarGridSpec(
            num_scalar_prefetch=1,
            grid=(4,),
            in_specs=[
                pl.BlockSpec((3, rows, M), lambda s, c: (0, jnp.minimum(s, 1), 0)),
                pl.BlockSpec((3, rows, M), lambda s, c: (0, jnp.maximum(s - 2, 0), 0)),
            ]
            + ([] if first else [any_] * 3),
            out_specs=(
                pl.BlockSpec((1, rows, M), lambda s, c: (e, half(s, c), 0)),
                pl.BlockSpec((1, rows, M), lambda s, c: (e, half(s, c), 0)),
                pl.BlockSpec((1, M, rows), lambda s, c: (e, 0, half(s, c))),
            ),
        ),
        input_output_aliases={} if first else {3: 0, 4: 1, 5: 2},
        name=f"finish{e}",
    )(core, own, sib, *([] if first else prev))


def last_kernel(n, r, s_ref, *refs):
    halves = (refs[0:2], refs[2:4])
    gain_ref, ga_ref, q_ref, k_ref, v_ref, o_ref, gf_ref = refs[4:]
    core, me = s_ref[0], s_ref[1]
    lead = n // 2
    low = iota((r, 128), 1) < 64
    ga = jnp.zeros((1, 256), F32)
    gf = jnp.zeros((1, 256), F32)
    for side, pair in enumerate(halves):
        hh = core if side == 0 else 1 - core
        for l in range(lead):
            one, two = pair[0][l, :r, :].astype(F32), pair[1][l, :r, :].astype(F32)
            kv0, kv1 = one[:, 128:], two[:, 128:]
            k = jnp.where(low, kv0, pltpu.roll(kv1, 64, 1))
            v = jnp.where(low, pltpu.roll(kv0, 64, 1), kv1)
            for j in range(n):

                @pl.when((me ^ (hh * lead + l)) == j)
                def _():
                    q_ref[:, j * 256 : j * 256 + 128] = one[:, :128]
                    q_ref[:, j * 256 + 128 : j * 256 + 256] = two[:, :128]
                    k_ref[:, j * 128 : j * 128 + 128] = k
                    v_ref[:, j * 128 : j * 128 + 128] = v

            below = pair[0][l, r : r + 16, :].astype(F32)
            ga = ga + below[:1, :] + pair[1][l, r : r + 16, :].astype(F32)[:1, :]
            gf = gf + below[1:2, :]
            count = (pair[0].shape[1] - r - 16) // (r // 2)
            for b in range(count):
                c = (l * count + b) * 256
                at = r + 16 + b * (r // 2)
                o_ref[pl.ds(pl.multiple_of(hh * (r // 2), 128), r // 2), c : c + 256] = pair[0][
                    l, at : at + r // 2, :
                ].astype(F32)
    ga_ref[...] = ga[:, :r] / gain_ref[...].astype(F32)
    gf_ref[...] = gf[:, :r]


def mixed_kernel(*refs):
    v = refs[0][...]
    for p in refs[1:-1]:
        v = v + p[...].astype(F32)
    refs[-1][...] = v.astype(BF)


def mixed_sum(hidden, parts):
    T, D = hidden.shape
    row = pl.BlockSpec((T // 2, D), lambda i: (i, 0))
    return call(
        mixed_kernel,
        shape((T, D), BF),
        1e6,
        6e6,
        grid=(2,),
        in_specs=[row] * (1 + len(parts)),
        out_specs=row,
        name="mixed",
    )(hidden, *parts)


def per_device(
    tokens,
    d_out,
    routes,
    gates,
    segment,
    gain_attn,
    w_query,
    key_weight,
    value_weight,
    w_out,
    gain_ffn,
    w_gate,
    w_up,
    w_down,
):
    n = lax.axis_size("shard")
    me = lax.axis_index("shard")
    R = lax.axis_size("rep")
    rp = lax.axis_index("rep")
    core, pos = rp % 2, rp // 2
    T, D = tokens.shape
    geo = Geo(n, T, segment.shape[1])
    G, TG = geo.G, geo.TG
    E, _, M = w_gate.shape
    me1 = me.reshape(1).astype(jnp.int32)
    scal = jnp.stack([core, me]).astype(jnp.int32)

    def px(v, m):
        return lax.ppermute(v, "shard", [(i, i ^ m) for i in range(n)])

    def at(v, i):
        return lax.dynamic_index_in_dim(v, i, 0, keepdims=False)

    def near(v):
        return [v] + [px(v, m) for m in ((1, 2) if geo.relay else range(1, n))]

    def far(got):
        if not geo.relay:
            return list(got)
        v, a, b = got
        h = v.shape[0] // 2
        return [v, a, b, px(a[:h], 2), px(b[h:], 1)]

    def hbm(*vals):
        return [pltpu.with_memory_space_constraint(v, pltpu.HBM) for v in vals]

    def tie(vals, deps):
        vals, deps = tuple(vals), tuple(deps)
        return lax.optimization_barrier(vals + deps)[: len(vals)]

    L = R // 2

    def pz(v, pairs):
        return lax.ppermute(v, "rep", [(2 * a + k, 2 * b + k) for a, b in pairs for k in (0, 1)])

    def sib(v):
        return lax.ppermute(v, "rep", [(i, i ^ 1) for i in range(R)])

    pos1 = jnp.stack([pos, jnp.full((), L - 1)]).astype(jnp.int32)
    near_pairs = [(0, 1), (1, 0), (2, 3), (3, 2)]

    class Sums:
        def __init__(self):
            self.live, self.done, self.final = [], {}, {}

        def add(self, tag, keeps, send):
            if L != 4:
                both_ = jnp.stack([jnp.concatenate(keeps, axis=1), send])
                both_ = jnp.where(core == 0, both_, both_[::-1])
                both_ = lax.psum(both_, "rep")
                self.done[tag] = at(both_, core), at(both_, 1 - core)
                return
            new = sib(send)
            for k, keep in enumerate(keeps):
                self.live.append(
                    dict(tag=tag, part=k, parts=len(keeps), step=0, acc=keep, new=new)
                )

        def meet(self, chunks, vals):
            names = [(c, f) for c in chunks for f in ("acc", "new")]
            flat = []
            for c, f in names:
                if not any(c[f] is v for v in flat):
                    flat.append(c[f])
            got = lax.optimization_barrier(tuple(vals) + tuple(flat))
            fresh = got[len(vals) :]
            for c, f in names:
                c[f] = next(b for a, b in zip(flat, fresh) if a is c[f])
            return got[: len(vals)]

        def advance(self, vals, more=(), hold=(), starts=1):
            live = []
            for c in self.live:
                if c["tag"] in hold:
                    continue
                if c["step"] == 0:
                    if not starts:
                        continue
                    starts -= 1
                live.append(c)
            vals = self.meet([c for c in live if c["step"] > 0], vals)
            vals = self.meet(live, (*vals, *more))
            if not live:
                return vals
            ops, then = [], []
            into = [c for c in live if c["step"] == 0]
            out = [c for c in live if c["step"] == 2]

            def arrived(c):
                return [(c["acc"], 0), (c["new"], c["part"] if c["step"] == 0 else 0)]

            pairs = []
            for c in out:
                mate = next((d for d in into if d["acc"].shape == c["acc"].shape), None)
                if mate is not None:
                    into.remove(mate)
                pairs.append((mate, c))
            pairs += [(d, None) for d in into]
            for c in live:
                if c["step"] == 3:
                    whole = self.final.get(c["tag"])
                    place = None if c["parts"] == 1 else (whole, c["part"])
                    ops.append(("take", [(c["new"], 0), (c["acc"], 0)], place))
                    then.append(("done", c))
                elif c["step"] == 1:
                    ops.append(("add", arrived(c), None))
                    then.append(("mid", c))
            for d, c in pairs:
                if c is None:
                    ops.append(("add", arrived(d), None))
                    then.append(("in", d))
                elif d is None:
                    ops.append(("add", arrived(c), None))
                    then.append(("out", c))
                else:
                    ops.append(("add", arrived(d), None))
                    then.append(("acc", d))
                    ops.append(("merge", arrived(d) + arrived(c), None))
                    then.append(("both", d, c))
            res = combine(pos1, ops)
            waiting = [t for t, v in self.done.items() if len(v) == 1]
            got = lax.optimization_barrier(
                vals + tuple(res) + tuple(self.done[t][0] for t in waiting)
            )
            vals, res, old = (
                got[: len(vals)],
                got[len(vals) : len(vals) + len(res)],
                got[len(vals) + len(res) :],
            )
            for t, v in zip(waiting, old):
                self.done[t] = (v,)
            for (what, *cs), v in zip(then, res):
                c = cs[-1]
                if what == "done":
                    self.final[c["tag"]] = v
                    c["step"] = 4
                    if all(o["step"] == 4 or o["tag"] != c["tag"] for o in self.live):
                        self.done[c["tag"]] = (v,)
                elif what == "mid":
                    c.update(step=2, acc=v, new=pz(v, [(1, 2), (2, 1)]))
                elif what == "acc":
                    c.update(acc=v)
                elif what == "in":
                    c.update(step=1, acc=v, new=pz(v, [(0, 1), (3, 2)]))
                elif what == "out":
                    c.update(step=3, acc=v, new=pz(v, [(1, 0), (2, 3)]))
                else:
                    new = pz(v, near_pairs)
                    cs[0].update(step=1, new=new)
                    c.update(step=3, acc=v, new=new)
            self.live = [c for c in self.live if c["step"] < 4]
            return vals

        def with_done(self, vals):
            waiting = [t for t, v in self.done.items() if len(v) == 1]
            got = lax.optimization_barrier(
                tuple(vals) + tuple(self.done[t][0] for t in waiting)
            )
            for t, v in zip(waiting, got[len(vals) :]):
                self.done[t] = (v,)
            return got[: len(vals)]

        def whole(self, tag):
            if len(self.done[tag]) == 1:
                self.done[tag] = (*self.done[tag], sib(*self.done[tag]))
            return self.done[tag]

    sums = Sums()

    def scatter(parts):
        return [parts[0]] + [px(parts[m], m) for m in range(n - 1, 0, -1)]

    r = w_query.shape[0]
    W = G * 256
    segc, segr = segment.reshape(-1, 1), segment
    near_tok = near(tokens)
    wmsg = call(
        functools.partial(columns_kernel, geo),
        (shape((r + 16, W), BF),) * n,
        1e6,
        2e6,
        in_specs=[SM] + [VM] * 5,
        out_specs=(VM,) * n,
        name="columns",
    )(me1, w_query, key_weight, value_weight, gain_attn.reshape(1, r), gain_ffn.reshape(1, r))
    got_w = [wmsg[0]] + [px(wmsg[m], m) for m in range(1, n)]
    dmsg, cos4, sin4 = call(
        pack_kernel,
        (shape((T, D + 128), BF), shape((TG, 128), F32), shape((TG, 128), F32)),
        1e6,
        2e6,
        in_specs=[VM] * 5,
        out_specs=(VM,) * 3,
        name="pack",
    )(d_out, routes, gates, segc, segr)
    wo_own = at(w_out.reshape(2, r // 2, D), core)
    dmsg, cos4, wo_own, *near_tok = tie((dmsg, cos4, wo_own, *near_tok), ())
    tok = far(near_tok)
    near_wo = near(wo_own)
    dmsg, *rest = tie((dmsg, *tok, *near_wo, *got_w), ())
    np_ = len(tok)
    tok, near_wo, got_w = rest[:np_], rest[np_ : -n], rest[-n:]
    near_d = near(dmsg)
    wo_half = far(near_wo)

    normed, q, kd, vd, kt, vt, w_cols, gain_a, gain_f = call(
        functools.partial(qkv_kernel, geo),
        (
            shape((n * T, D), BF),
            shape((2 * G, TG, 128), BF),
            shape((G, TG, 128), BF),
            shape((G, TG, 128), BF),
            shape((G, 64, TG), BF),
            shape((G, 64, TG), BF),
            shape((D, W), BF),
            shape((1, D), F32),
            shape((1, D), F32),
        ),
        2 * TG * D * W,
        12e6,
        in_specs=[SM] + [VM] * (np_ + n + 2),
        out_specs=(VM,) * 9,
        scratch_shapes=[pltpu.VMEM((TG, W), F32)],
        name="qkv",
    )(me1, *tok, *got_w, cos4, sin4)

    atts, lses, own_att = [], [], []
    near_o = None
    for g in range(G):
        o, lse = call(
            functools.partial(att_kernel, geo),
            (shape((n * T, 128), BF), shape((2, 1, TG), F32)),
            1e9,
            3e6,
            2 * TG * TG * 0.6,
            grid=(1,),
            in_specs=[
                SM,
                pl.BlockSpec((2, TG, 128), lambda i, g=g: (g, 0, 0)),
                pl.BlockSpec((1, TG, 128), lambda i, g=g: (g, 0, 0)),
                pl.BlockSpec((1, 64, TG), lambda i, g=g: (g, 0, 0)),
                VM,
                VM,
            ],
            out_specs=(VM, VM),
            name=f"attend{g}",
        )(me1, q, kd, vt, segc, segr)
        own_att.append(o)
        lses.append(lse)
        if g == 0:
            k = len(near_d)
            o, q, *rest = tie((o, q, *near_d, *wo_half), ())
            near_d, wo_half = rest[:k], rest[k:]
            wo_mine = jnp.concatenate(wo_half, axis=0)
            wo_sib = sib(wo_mine)
            near_o = near(o)
        else:
            o, *near_o = tie((o, *near_o), ())
            atts += far(near_o)
            near_o = near(o)
    near_d, near_o = list(near_d), list(near_o)
    wo_mine, wo_sib, *rest = tie((wo_mine, wo_sib, *near_d, *near_o, *atts), ())
    k = len(near_d)
    near_d, near_o, atts = rest[:k], rest[k : k + len(near_o)], rest[k + len(near_o) :]
    atts += far(near_o)
    douts = far(near_d)
    lse = jnp.concatenate(lses, axis=0)

    hidden, x = call(
        functools.partial(hidden_kernel, geo, len(atts)),
        (shape((T, D), F32), shape((n * T, D), BF)),
        2 * TG * D * D,
        16e6,
        in_specs=[SM] + [VM] * (len(atts) + np_ + 3),
        out_specs=(VM,) * 2,
        scratch_shapes=[pltpu.VMEM((D, D), BF)],
        name="hidden",
    )(scal, *atts, *tok, wo_mine, wo_sib, gain_f)
    x, *douts = tie((x, *douts), ())
    dout = jnp.concatenate(douts, axis=0)

    w_gate, w_up, w_down = hbm(w_gate, w_up, w_down)
    early = E // 2
    kept = None
    for e in range(early):
        kept, send, keeps = expert(n, T, E, e, scal, x, dout, w_gate, w_up, w_down, kept)
        kept = hbm(*kept)
        sums.add(e, keeps, send)
        if e == 0:
            x, *kept = sums.advance((x, *kept))
    kept = hbm(*forwards(n, T, E, early, scal, x, dout, w_gate, w_up, w_down, kept))
    (last,) = input_grad(T, E, (n - 1) * T, [T], *kept[1:], w_gate, w_up)
    x, act, gg, ug, last = sums.advance((x, *kept, last))

    def weights(e, x, act, gg, ug):
        send, keeps = weight_grad(M, e, scal, x, dout, act, gg, ug)
        sums.add(e, keeps, send)
        return tie((x, act, gg, ug), (send,))

    far_part = px(last, n - 1)
    x, act, gg, ug = weights(early, x, act, gg, ug)
    if n == 4:
        first = input_grad(T, E, 0, [T] * (n - 1), gg, ug, w_gate, w_up)
    else:
        first = [
            v
            for m in range(n - 1)
            for v in input_grad(T, E, m * T, [T], gg, ug, w_gate, w_up)
        ]
    *first, x, act, gg, ug, far_part = sums.advance((*first, x, act, gg, ug), (far_part,))
    came = [first[0], far_part] + [px(first[m], m) for m in range(n - 2, 0, -1)]
    rest = []
    for e in range(early + 1, E):
        send, keeps = weight_grad(M, e, scal, x, dout, act, gg, ug)
        rest += [send, *keeps]
    k = len(came)
    came = tie((*came, act, *rest), ())
    came, act, rest = came[:k], came[k], came[k + 1 :]
    for e in range(early + 1, E):
        sums.add(e, rest[1 : 1 + CH], rest[0])
        rest = rest[1 + CH :]

    hidden_grad, branch, gain_f_part = norm_back(came, d_out, hidden, gain_f, True)
    (act,) = tie((act,), (branch,))
    branches = near(branch)
    mix = sums.advance(mix_parts(n, T, [T] * n, act, w_down), branches)
    mix, branches = mix[:n], far(mix[n:])

    prev = None
    finished = 0

    def finishing(most):
        nonlocal prev, finished
        while finished < most and finished in sums.done:
            prev = finish(finished, E, scal, *sums.whole(finished), prev)
            finished += 1

    def tie_finished(vals):
        nonlocal prev
        if prev is None:
            return tuple(vals)
        got = lax.optimization_barrier(tuple(vals) + tuple(prev))
        prev = got[-3:]
        return got[:-3]

    finishing(1)
    w_out_ = w_out
    nb = len(branches)
    *branches, q, kd = tie_finished((*branches, q, kd))
    mix = list(tie(mix, branches))
    mix_far = px(mix[n - 1], n - 1)

    def attend_back(g, q, kd):
        return call(
            functools.partial(att_back_kernel, geo, g),
            shape((n * T, 256), BF),
            4e9 / G,
            8e6,
            4 * TG * TG * 0.6 / G,
            grid=(1,),
            in_specs=[SM]
            + [VM] * nb
            + [
                pl.BlockSpec((128, D), lambda i: (g, 0)),
                pl.BlockSpec((2, TG, 128), lambda i: (g, 0, 0)),
                pl.BlockSpec((1, TG, 128), lambda i: (g, 0, 0)),
                pl.BlockSpec((1, 64, TG), lambda i: (g, 0, 0)),
                pl.BlockSpec((1, TG, 128), lambda i: (g, 0, 0)),
                pl.BlockSpec((2, 1, TG), lambda i: (g, 0, 0)),
            ]
            + [VM] * 4,
            out_specs=VM,
            scratch_shapes=[
                pltpu.VMEM((2, TG, 128), BF),
                pltpu.VMEM((1, TG, 128), F32),
                pltpu.VMEM((1, TG, 128), F32),
                pltpu.VMEM((2, 64, TG), F32),
            ],
            name=f"attend_back{g}",
        )(me1, *branches, *hbm(w_out_, q, kd, kt, vd, lse, segc, segr, cos4, sin4))

    def head_grad(g, y):
        return call(
            functools.partial(head_grad_kernel, geo, g == 0),
            (shape((r + 16, 256), BF),) * n,
            1e9,
            4e6,
            grid=(1,),
            in_specs=[
                SM,
                VM,
                VM,
                pl.BlockSpec((D, 256), lambda i: (0, g)),
                VM,
            ],
            out_specs=(VM,) * n,
            name=f"head_grad{g}",
        )(scal, normed, y, w_cols, gain_f_part)

    lead = n // 2
    orows = r // 2 * (D // 256) // lead

    def add_small(g, arrived, out=None):
        got = jnp.stack(arrived).reshape(2, lead, r + 16, 256)
        keep, send = at(got, core), at(got, 1 - core)
        if out is not None:
            keep = jnp.concatenate([keep, out[1]], axis=1)
            send = jnp.concatenate([send, out[0]], axis=1)
        sums.add(("small", g), [keep], send)

    out = call(
        functools.partial(out_grad_kernel, nb, G),
        (shape((lead, orows, 256), BF),) * 2,
        1e9,
        4e6,
        in_specs=[SM] + [VM] * (nb + G),
        out_specs=(VM, VM),
        name="out_grad",
    )(scal, *branches, *own_att)
    ys = [attend_back(0, q, kd)]
    msgs = head_grad(0, ys[0])
    q, kd, *got, mix_far = sums.advance((q, kd, *msgs, *out), (mix_far,))
    msgs, out = got[:n], got[n:]
    arrived = [msgs[0]] + [px(msgs[m], m) for m in range(1, n)]
    if G == 2:
        ys.append(attend_back(1, q, kd))
    got = tie((*ys, *arrived), ())
    ys, arrived = got[:G], got[G:]
    add_small(0, arrived, out)
    arrived = []
    if G == 2:
        msgs = head_grad(1, ys[1])
        ys = tie(ys, msgs[:1])
        arrived = [msgs[0]] + [px(msgs[m], m) for m in range(1, n)]
    back = call(
        functools.partial(back_kernel, T, G),
        (shape((T, D), BF),) * n,
        1e9,
        8e6,
        in_specs=[VM] * (1 + G),
        out_specs=(VM,) * n,
        name="back",
    )(w_cols, *ys)
    came = scatter(back)
    came[0], *arrived = sums.advance(came[:1], arrived)
    if G == 2:
        add_small(1, arrived)
    k = len(came)
    got = sums.advance((), (*came, *mix))
    came, mix = got[:k], got[k:]
    mix = [mix[0], mix_far] + [px(mix[m], m) for m in range(n - 2, 0, -1)]
    (d_tokens,) = norm_back(came, hidden_grad, tokens, gain_a, False)
    finishing(E // 2)
    (d_tokens,) = tie_finished((d_tokens,))
    (d_tokens,) = sums.advance((d_tokens,))
    finishing(E)
    (d_tokens,) = tie_finished((d_tokens,))
    d_tokens, *mix = sums.advance((d_tokens,), mix)
    mixed = mixed_sum(hidden, mix)
    while sums.live:
        (d_tokens,) = sums.advance((d_tokens,))
    finishing(E)
    g_gate, g_up, g_down = prev

    if G == 2:
        one, two = sums.whole(("small", 0)), sums.whole(("small", 1))
        g_ga, g_q, g_k, g_v, g_out_all, g_gf = call(
            functools.partial(last_kernel, n, r),
            (
                shape((1, r), F32),
                shape((r, QUERY_HEADS * HEAD), F32),
                shape((r, KEY_VALUE_HEADS * HEAD), F32),
                shape((r, KEY_VALUE_HEADS * HEAD), F32),
                shape((r, D), F32),
                shape((1, r), F32),
            ),
            1e6,
            5e6,
            in_specs=[SM] + [VM] * 5,
            out_specs=(VM,) * 6,
            name="last",
        )(scal, one[0], two[0], one[1], two[1], gain_attn.reshape(1, r))
        g_ga, g_gf = g_ga.reshape(r), g_gf.reshape(r)
    else:
        v, other = sums.whole(("small", 0))
        v = jnp.where(core == 0, jnp.stack([v, other]), jnp.stack([other, v])).astype(F32)
        g_out_all = v[:, :, r + 16 :, :].reshape(2, D // 256, r // 2, 256)
        g_out_all = g_out_all.transpose(0, 2, 1, 3).reshape(r, D)
        v = v[:, :, : r + 16].reshape(n, r + 16, 256)
        in_order = [at(v, me ^ j)[:r] for j in range(n)]
        g_q, g_k, g_v = [
            jnp.concatenate([b[:, lo:hi] for b in in_order], axis=1)
            for lo, hi in ((0, 128), (128, 192), (192, 256))
        ]
        g_ga = jnp.sum(v[:, r, :r], axis=0) / gain_attn.astype(F32)
        g_gf = jnp.sum(v[:, r + 1, :r], axis=0)
    return (mixed, d_tokens, g_ga, g_q, g_k, g_v, g_out_all, g_gf, g_gate, g_up, g_down)


def solution(mesh):
    rows = P(("rep", "shard"), None)
    own = P("shard", None)
    own3 = P("shard", None, None)
    vec = P("shard")
    return jax.shard_map(
        per_device,
        mesh=mesh,
        in_specs=(
            rows,
            rows,
            rows,
            rows,
            P("rep", None),
            vec,
            own,
            own,
            own,
            own,
            vec,
            own3,
            own3,
            own3,
        ),
        out_specs=(rows, rows, vec, own, own, own, own, vec, own3, own3, own3),
        check_vma=False,
    )
```

```python
import functools
import math

import jax
import jax.numpy as jnp
from jax import lax
from jax.experimental import pallas as pl
from jax.experimental.pallas import tpu as pltpu
from jax.sharding import PartitionSpec as P

QUERY_HEADS = 16
KEY_VALUE_HEADS = 8
HEAD = 64
EXPERTS = 16
PROMPT = 1024
EPS = 1e-06
F32 = jnp.float32
BF = jnp.bfloat16
TILE = 256
VMEM_LIMIT = 30 * 1024 * 1024


def nn(a, b):
    return lax.dot_general(a, b, (((1,), (0,)), ((), ())), preferred_element_type=F32)


def nt(a, b):
    return lax.dot_general(a, b, (((1,), (1,)), ((), ())), preferred_element_type=F32)


def tn(a, b):
    return lax.dot_general(a, b, (((0,), (0,)), ((), ())), preferred_element_type=F32)


COST = 0.25


def call(kernel, out_shape, flops, nbytes, trans=0, **kw):
    return pl.pallas_call(
        kernel,
        out_shape=out_shape,
        compiler_params=pltpu.CompilerParams(vmem_limit_bytes=VMEM_LIMIT),
        cost_estimate=pl.CostEstimate(
            flops=int(COST * flops), bytes_accessed=int(COST * nbytes), transcendentals=int(COST * trans)
        ),
        **kw,
    )


VM = pl.BlockSpec(memory_space=pltpu.VMEM)
SM = pl.BlockSpec(memory_space=pltpu.SMEM)


def shape(dims, dtype):
    return jax.ShapeDtypeStruct(dims, dtype)


class Geo:
    def __init__(self, n, rows, conts):
        self.n = n
        self.T = rows
        self.PS = PROMPT // n
        self.CT = conts
        self.CS = conts // n
        self.TG = PROMPT + conts
        self.G = KEY_VALUE_HEADS // n
        self.relay = n == 4

    def pieces(self):
        out = [(m, 0, self.T) for m in range(self.n)]
        if self.relay:
            half = self.T // 2
            out = out[:-1] + [(3, 0, half), (3, half, half)]
        return out

    def places(self, me, m, off, rows):
        j = me ^ m
        out = []
        lead = max(0, min(self.PS, off + rows) - off)
        if lead:
            out.append((0, lead, pl.multiple_of(j * self.PS + off, 32)))
        if rows > lead:
            start = off + lead - self.PS
            out.append((lead, rows - lead, pl.multiple_of(PROMPT + j * self.CS + start, 32)))
        return out

    def tiles(self):
        out = []
        for i in range(PROMPT // TILE):
            ks = [(0, i * TILE, 0)] if i else []
            out.append((i * TILE, ks + [(i * TILE, TILE, 1)]))
        for c in range(self.CT // TILE):
            ks = [(0, PROMPT, 0)]
            if c:
                ks.append((PROMPT + (c - 1) * TILE, TILE, 2))
            ks.append((PROMPT + c * TILE, TILE, 3))
            out.append((PROMPT + c * TILE, ks))
        return out

    def spread(self, me, start):
        out = []
        if start < PROMPT:
            step = min(self.PS, TILE)
            for a in range(0, TILE, step):
                j = (start + a) // self.PS
                off = (start + a) % self.PS
                out.append((a, step, pl.multiple_of((me ^ j) * self.T + off, 32)))
        else:
            step = min(self.CS, TILE)
            for a in range(0, TILE, step):
                j = (start - PROMPT + a) // self.CS
                off = (start - PROMPT + a) % self.CS
                out.append((a, step, pl.multiple_of((me ^ j) * self.T + self.PS + off, 32)))
        return out


def iota(dims, axis):
    return lax.broadcasted_iota(jnp.int32, dims, axis)


def swap_halves(v):
    lane = iota(v.shape, 1)
    first = (lane & 32) == 0
    return jnp.where(first, pltpu.roll(v, 96, 1), pltpu.roll(v, 32, 1))


def masked(s, kind, q0, k0, segc_ref, segr_ref):
    if kind == 0:
        return s
    ok = None
    if kind != 2:
        ok = iota(s.shape, 0) <= iota(s.shape, 1)
    if kind != 1:
        same = segc_ref[k0 - PROMPT : k0 - PROMPT + TILE, :] == segr_ref[:, q0 - PROMPT : q0 - PROMPT + TILE]
        ok = same if ok is None else ok & same
    return jnp.where(ok, s, -1e30)


def qkv_kernel(geo, me_ref, *refs):
    np_ = len(geo.pieces())
    toks = refs[:np_]
    n = geo.n
    msgs = refs[np_ : np_ + n]
    c_ref, s_ref = refs[np_ + n : np_ + n + 2]
    (normed_ref, q_ref, kd_ref, vd_ref, kt_ref, vt_ref, w_ref, ga_ref, gf_ref, raw) = refs[
        np_ + n + 2 :
    ]
    me = me_ref[0]
    G = geo.G
    r = msgs[0].shape[0] - 16
    for m, msg in enumerate(msgs):
        w_ref[pl.ds(pl.multiple_of((me ^ m) * r, 128), r), :] = msg[:r, :]
        gains = msg[r : r + 16, :].astype(F32)[:1, :]
        for j in range(n):

            @pl.when((me ^ m) == j)
            def _():
                ga_ref[:, j * r : (j + 1) * r] = gains[:, :r]
                gf_ref[:, j * r : (j + 1) * r] = gains[:, r : 2 * r]

    gain = ga_ref[...]
    for (m, off, rows), tok in zip(geo.pieces(), toks):
        v = tok[...].astype(F32)
        r = lax.rsqrt(jnp.mean(v * v, axis=-1, keepdims=True) + EPS)
        x = (v * r * gain).astype(BF)
        normed_ref[m * geo.T + off : m * geo.T + off + rows, :] = x
        y = nn(x, w_ref[...])
        for a, cnt, dst in geo.places(me, m, off, rows):
            raw[pl.ds(dst, cnt), :] = y[a : a + cnt, :]
    for t in range(0, geo.TG, TILE):
        rows = slice(t, t + TILE)
        cos, sin = c_ref[rows, :], s_ref[rows, :]
        low = iota((TILE, 128), 1) < 64
        for g in range(G):
            v = raw[rows, g * 256 : g * 256 + 128]
            q = (v * cos + swap_halves(v) * sin).astype(BF).astype(F32) * 0.125
            q_ref[2 * g, rows, :] = jnp.where(low, q, 0.0).astype(BF)
            q_ref[2 * g + 1, rows, :] = jnp.where(low, 0.0, q).astype(BF)
            kv = raw[rows, g * 256 + 128 : g * 256 + 256]
            vk = pltpu.roll(kv, 64, 1)
            k = jnp.where(low, kv, vk)
            k = (k * cos + swap_halves(k) * sin).astype(BF)
            v = jnp.where(low, vk, kv)
            kd_ref[g, rows, :] = k
            vd_ref[g, rows, :] = v.astype(BF)
            kt_ref[g, :, rows] = k.astype(F32).T[:64, :].astype(BF)
            vt_ref[g, :, rows] = v.T[:64, :].astype(BF)


def columns_kernel(geo, me_ref, wq_ref, wk_ref, wv_ref, ga_ref, gf_ref, *outs):
    me = me_ref[0]
    r = wq_ref.shape[0]
    low = iota((r, 128), 1) < 64
    gains = jnp.concatenate([ga_ref[...], gf_ref[...]], axis=1)
    gains = jnp.broadcast_to(gains, (16, gains.shape[1]))
    for j in range(geo.n):
        cols = []
        for g in range(geo.G):
            h = j * geo.G + g
            pair = slice(h // 2 * 128, h // 2 * 128 + 128)
            k = wk_ref[:, pair].astype(F32)
            v = wv_ref[:, pair].astype(F32)
            if h % 2 == 0:
                kv = jnp.where(low, k, pltpu.roll(v, 64, 1))
            else:
                kv = jnp.where(low, pltpu.roll(k, 64, 1), v)
            cols += [wq_ref[:, h * 128 : h * 128 + 128], kv.astype(BF)]
        block = jnp.concatenate(cols, axis=1)
        for m, out in enumerate(outs):

            @pl.when((me ^ m) == j)
            def _():
                out[:r, :] = block
                out[r:, :] = gains


def pack_kernel(d_ref, r_ref, g_ref, segc_ref, segr_ref, out_ref, c_ref, s_ref):
    D = d_ref.shape[1]
    out_ref[:, :D] = d_ref[...]
    lane = iota((d_ref.shape[0], 128), 1)
    gate = jnp.zeros(lane.shape, F32)
    for k in range(r_ref.shape[1]):
        hit = (lane & (EXPERTS - 1)) == r_ref[:, k : k + 1]
        gate = gate + jnp.where(hit, g_ref[:, k : k + 1], 0.0)
    top = gate.astype(BF).astype(F32)
    mid = (gate - top).astype(BF).astype(F32)
    low = gate - top - mid
    term = jnp.where(lane < EXPERTS, top, jnp.where(lane < 2 * EXPERTS, mid, low))
    out_ref[:, D:] = jnp.where(lane < 3 * EXPERTS, term, 0.0).astype(BF)

    lane = iota((1, 128), 1)
    freq = jnp.exp((lane & 31).astype(F32) * (-2.0 * math.log(10000.0) / HEAD))
    sign = jnp.where((lane & 32) == 0, -1.0, 1.0)
    for t in range(0, c_ref.shape[0], TILE):
        row = iota((TILE, 1), 0).astype(F32) + float(t)
        if t >= PROMPT:
            own = segc_ref[t - PROMPT : t - PROMPT + TILE, :]
            start = jnp.sum(jnp.where(segr_ref[...] < own, 1.0, 0.0), axis=1, keepdims=True)
            row = row - start
        ang = row * freq
        c_ref[t : t + TILE, :] = jnp.cos(ang)
        s_ref[t : t + TILE, :] = jnp.sin(ang) * sign


def att_kernel(geo, me_ref, q_ref, kd_ref, vt_ref, segc_ref, segr_ref, o_ref, lse_ref):
    me = me_ref[0]
    for q0, keys in geo.tiles():
        outs = []
        for h in range(2):
            q = q_ref[h, q0 : q0 + TILE, :]
            ss = [
                masked(nt(kd_ref[0, k0 : k0 + kn, :], q), kind, q0, k0, segc_ref, segr_ref)
                for k0, kn, kind in keys
            ]
            top = functools.reduce(
                jnp.maximum, [jnp.max(s, axis=0, keepdims=True) for s in ss]
            )
            ps = [jnp.exp(s - top) for s in ss]
            total = functools.reduce(
                jnp.add, [jnp.sum(p, axis=0, keepdims=True) for p in ps]
            )
            lse_ref[h, :, q0 : q0 + TILE] = top + jnp.log(total)
            inv = 1.0 / total
            acc = None
            for p, (k0, kn, kind) in zip(ps, keys):
                part = nn(vt_ref[0, :, k0 : k0 + kn], (p * inv).astype(BF))
                acc = part if acc is None else acc + part
            outs.append(acc)
        o = jnp.concatenate(outs, axis=0).T.astype(BF)
        for a, cnt, dst in geo.spread(me, q0):
            o_ref[pl.ds(dst, cnt), :] = o[a : a + cnt, :]


def hidden_kernel(geo, natt, s_ref, *refs):
    pieces = geo.pieces()
    np_ = len(pieces)
    atts = refs[:natt]
    toks = refs[natt : natt + np_]
    mine_ref, other_ref, gain_ref = refs[natt + np_ : natt + np_ + 3]
    hid_ref, x_ref, w_ref = refs[natt + np_ + 3 :]
    half = mine_ref.shape[0] // geo.n
    for m in range(geo.n):
        own = pl.multiple_of((2 * m + s_ref[0]) * half, 64)
        sib = pl.multiple_of((2 * m + 1 - s_ref[0]) * half, 64)
        w_ref[pl.ds(own, half), :] = mine_ref[m * half : (m + 1) * half, :]
        w_ref[pl.ds(sib, half), :] = other_ref[m * half : (m + 1) * half, :]
    gain = gain_ref[...].astype(F32)
    index = {}
    k = 0
    for g in range(geo.G):
        for m, off, rows in att_pieces(geo):
            index[(m, g, off)] = (atts[k], off, rows)
            k += 1

    def att_rows(m, g, row, cnt):
        for (mm, gg, _), (ref, off, rows) in index.items():
            if mm == m and gg == g and off <= row and row + cnt <= off + rows:
                return ref[row - off : row - off + cnt, :]
        raise ValueError("piece")

    for (j, off, rows), tok in zip(pieces, toks):
        lhs = jnp.concatenate(
            [
                att_rows(m, g, (m ^ j) * geo.T + off, rows)
                for m in range(geo.n)
                for g in range(geo.G)
            ],
            axis=1,
        )
        h = tok[...].astype(F32) + nn(lhs, w_ref[...])
        if j == 0:
            hid_ref[...] = h
        r = lax.rsqrt(jnp.mean(h * h, axis=-1, keepdims=True) + EPS)
        x_ref[j * geo.T + off : j * geo.T + off + rows, :] = (h * r * gain).astype(BF)


def att_pieces(geo):
    rows = geo.n * geo.T
    out = [(m, 0, rows) for m in range(geo.n)]
    if geo.relay:
        out = out[:-1] + [(3, 0, rows // 2), (3, rows // 2, rows // 2)]
    return out


CH = 1


def expert_rows(x, dout, wg, wu, wd, gate):
    g = nn(x, wg)
    u = nn(x, wu)
    back = nt(dout, wd) * gate
    s = 1.0 / (1.0 + jnp.exp(-g))
    sil = g * s
    act = (sil * u * gate).astype(BF)
    gg = (back * u * (s + sil * (1.0 - s))).astype(BF)
    ug = (back * sil).astype(BF)
    return act, gg, ug


def gate_column(gm_ref, expert):
    lane = iota(gm_ref.shape, 1)
    mine = (lane == expert) | (lane == EXPERTS + expert) | (lane == 2 * EXPERTS + expert)
    return jnp.sum(jnp.where(mine, gm_ref[...].astype(F32), 0.0), axis=1, keepdims=True)


def put_grads(outs, x_ref, do_ref, gg_ref, ug_ref, ac_ref):
    cols = x_ref.shape[1] // len(outs)
    for k, out in enumerate(outs):
        x = x_ref[:, k * cols : (k + 1) * cols]
        out[0] = tn(x, gg_ref[...]).astype(BF)
        out[1] = tn(x, ug_ref[...]).astype(BF)
        out[2] = tn(do_ref[:, k * cols : (k + 1) * cols], ac_ref[...]).astype(BF)


def expert_kernel(n, T, E, e, s_ref, *refs):
    x_ref, do_ref, gm_ref, wg_ref, wu_ref, wd_ref, xc_ref, dc_ref = refs[:8]
    act_ref, gg_ref, ug_ref, send = refs[-7 - CH : -3 - CH]
    keeps = refs[-3 - CH : -3]
    gg_s, ug_s, ac_s = refs[-3:]
    r = pl.program_id(0)

    @pl.when(r < n)
    def _():
        act, gg, ug = expert_rows(
            x_ref[...],
            do_ref[...],
            wg_ref[0],
            wu_ref[0],
            wd_ref[0],
            gate_column(gm_ref, s_ref[1] * E + e),
        )
        rows = pl.ds(pl.multiple_of(r * T, 128), T)
        gg_s[rows, :] = gg
        ug_s[rows, :] = ug
        ac_s[rows, :] = act
        act_ref[...] = act
        gg_ref[...] = gg
        ug_ref[...] = ug

    @pl.when(r == n)
    def _():
        put_grads([send], xc_ref, dc_ref, gg_s, ug_s, ac_s)

    @pl.when(r == n + 1)
    def _():
        put_grads(keeps, xc_ref, dc_ref, gg_s, ug_s, ac_s)


def expert(n, T, E, e, scal, x, dout, wg, wu, wd, kept):
    D, M = wg.shape[1:]
    row = lambda r, c: (jnp.minimum(r, n - 1), 0)
    gate = lambda r, c: (jnp.minimum(r, n - 1), D // 128)
    half = lambda r, c: (0, jnp.where(r == n + 1, c[0], 1 - c[0]))
    fix = lambda r, c: (e, 0, 0)
    whole = lambda r, c: (0, 0, 0)
    block = pl.BlockSpec((T, M), lambda r, c: (jnp.minimum(r, n - 1), e))
    in_specs = [
        pl.BlockSpec((T, D), row),
        pl.BlockSpec((T, D), row),
        pl.BlockSpec((T, 128), gate),
        pl.BlockSpec((1, D, M), fix),
        pl.BlockSpec((1, D, M), fix),
        pl.BlockSpec((1, M, D), fix),
        pl.BlockSpec((n * T, D // 2), half),
        pl.BlockSpec((n * T, D // 2), half),
    ]
    args = [x, dout, dout, wg, wu, wd, x, dout]
    alias = {}
    if kept is not None:
        in_specs += [pl.BlockSpec(memory_space=pl.ANY)] * 3
        args += list(kept)
        alias = {9: 0, 10: 1, 11: 2}
    out = call(
        functools.partial(expert_kernel, n, T, E, e),
        (pltpu.HBM((n * T, E * M), BF),) * 3
        + (shape((3, D // 2, M), BF),)
        + (shape((3, D // 2 // CH, M), BF),) * CH,
        12 * n * T * D * M,
        20e6,
        grid_spec=pltpu.PrefetchScalarGridSpec(
            num_scalar_prefetch=1,
            grid=(n + 2,),
            in_specs=in_specs,
            out_specs=(block,) * 3
            + (pl.BlockSpec((3, D // 2, M), whole),)
            + (pl.BlockSpec((3, D // 2 // CH, M), whole),) * CH,
            scratch_shapes=[pltpu.VMEM((n * T, M), BF)] * 3,
        ),
        input_output_aliases=alias,
        name=f"expert{e}",
    )(scal, *args)
    return out[:3], out[3], out[4:]


def forward_kernel(E, e0, s_ref, x_ref, do_ref, gm_ref, wg_ref, wu_ref, wd_ref, *refs):
    act_ref, gg_ref, ug_ref = refs[-3:]
    act, gg, ug = expert_rows(
        x_ref[...],
        do_ref[...],
        wg_ref[0],
        wu_ref[0],
        wd_ref[0],
        gate_column(gm_ref, s_ref[1] * E + e0 + pl.program_id(0)),
    )
    act_ref[...] = act
    gg_ref[...] = gg
    ug_ref[...] = ug


def forwards(n, T, E, e0, scal, x, dout, wg, wu, wd, kept):
    D, M = wg.shape[1:]
    R = n * T // 2
    any_ = pl.BlockSpec(memory_space=pl.ANY)
    row = pl.BlockSpec((R, D), lambda i, r, c: (r, 0))
    fix = lambda i, r, c: (e0 + i, 0, 0)
    block = pl.BlockSpec((R, M), lambda i, r, c: (r, e0 + i))
    return call(
        functools.partial(forward_kernel, E, e0),
        (pltpu.HBM((n * T, E * M), BF),) * 3,
        6 * (E - e0) * n * T * D * M,
        (E - e0) * 12e6,
        grid_spec=pltpu.PrefetchScalarGridSpec(
            num_scalar_prefetch=1,
            grid=(E - e0, 2),
            in_specs=[
                row,
                row,
                pl.BlockSpec((R, 128), lambda i, r, c: (r, D // 128)),
                pl.BlockSpec((1, D, M), fix),
                pl.BlockSpec((1, D, M), fix),
                pl.BlockSpec((1, M, D), fix),
                any_,
                any_,
                any_,
            ],
            out_specs=(block,) * 3,
        ),
        input_output_aliases={7: 0, 8: 1, 9: 2},
        name="forwards",
    )(scal, x, dout, dout, wg, wu, wd, *kept)


def input_grad_kernel(E, T, gg_ref, ug_ref, wg_ref, wu_ref, *refs):
    outs, acc = refs[:-1], refs[-1]
    i = pl.program_id(0)
    v = nt(gg_ref[...], wg_ref[0]) + nt(ug_ref[...], wu_ref[0])

    @pl.when(i == 0)
    def _():
        acc[...] = v

    @pl.when(i > 0)
    def _():
        acc[...] += v

    @pl.when(i == E - 1)
    def _():
        put_blocks(T, acc, outs)


def input_grad(T, E, first, rows, gg, ug, wg, wu):
    D, M = wg.shape[1:]
    R = sum(rows)
    block = pl.BlockSpec((R, M), lambda i: (first // R, i))
    weight = pl.BlockSpec((1, D, M), lambda i: (i, 0, 0))
    return call(
        functools.partial(input_grad_kernel, E, T),
        tuple(shape((v, D), BF) for v in rows),
        4 * E * R * D * M,
        16e6,
        grid=(E,),
        in_specs=[block, block, weight, weight],
        out_specs=tuple(pl.BlockSpec((v, D), lambda i: (0, 0)) for v in rows),
        scratch_shapes=[pltpu.VMEM((R, D), F32)],
        name=f"input_grad{first}",
    )(gg, ug, wg, wu)


def weight_grad_kernel(s_ref, x_ref, do_ref, gg_ref, ug_ref, ac_ref, send, *keeps):
    @pl.when(pl.program_id(0) == 0)
    def _():
        put_grads([send], x_ref, do_ref, gg_ref, ug_ref, ac_ref)

    @pl.when(pl.program_id(0) == 1)
    def _():
        put_grads(keeps, x_ref, do_ref, gg_ref, ug_ref, ac_ref)


def weight_grad(M, e, scal, x, dout, act, gg, ug):
    R, D = x.shape
    half = lambda s, c: (0, jnp.where(s == 1, c[0], 1 - c[0]))
    whole = lambda s, c: (0, 0, 0)
    block = pl.BlockSpec((R, M), lambda s, c: (0, e))
    out = call(
        weight_grad_kernel,
        (shape((3, D // 2, M), BF),) + (shape((3, D // 2 // CH, M), BF),) * CH,
        6 * R * D * M,
        14e6,
        grid_spec=pltpu.PrefetchScalarGridSpec(
            num_scalar_prefetch=1,
            grid=(2,),
            in_specs=[
                pl.BlockSpec((R, D // 2), half),
                pl.BlockSpec((R, D // 2), half),
                block,
                block,
                block,
            ],
            out_specs=(pl.BlockSpec((3, D // 2, M), whole),)
            + (pl.BlockSpec((3, D // 2 // CH, M), whole),) * CH,
        ),
        name=f"weight_grad{e}",
    )(scal, x, dout, gg, ug, act)
    return out[0], out[1:]


def norm_back_kernel(count, low, *refs):
    parts = refs[:count]
    base_ref, v_ref, gain_ref = refs[count : count + 3]
    outs = refs[count + 3 :]
    grad = parts[0][...].astype(F32)
    for p in parts[1:]:
        grad = grad + p[...].astype(F32)
    v = v_ref[...].astype(F32)
    r = lax.rsqrt(jnp.mean(v * v, axis=-1, keepdims=True) + EPS)
    gv = gain_ref[...].astype(F32) * grad
    res = (
        base_ref[...].astype(F32)
        + r * gv
        - v * (r * r * r * jnp.mean(gv * v, axis=-1, keepdims=True))
    )
    outs[0][...] = res
    if low:
        outs[1][...] = res.astype(BF)
        part = jnp.sum(grad * v * r, axis=0, keepdims=True)

        @pl.when(pl.program_id(0) == 0)
        def _():
            outs[2][...] = part

        @pl.when(pl.program_id(0) > 0)
        def _():
            outs[2][...] += part


def norm_back(parts, base, v, gain, low):
    T, D = v.shape
    B = 128
    row = pl.BlockSpec((B, D), lambda i: (i, 0))
    one = pl.BlockSpec((1, D), lambda i: (0, 0))
    out = [shape((T, D), F32)]
    specs = [row]
    if low:
        out += [shape((T, D), BF), shape((1, D), F32)]
        specs += [row, one]
    return call(
        functools.partial(norm_back_kernel, len(parts), low),
        tuple(out),
        20 * T * D,
        T * D * 16,
        grid=(T // B,),
        in_specs=[row] * len(parts) + [row, row, one],
        out_specs=tuple(specs),
        name="norm_back",
    )(*parts, base, v, gain)


def att_back_kernel(geo, gi, me_ref, *refs):
    pieces = geo.pieces()
    np_ = len(pieces)
    brs = refs[:np_]
    (w_ref, q_ref, kd_ref, kt_ref, vd_ref, lse_ref, segc_ref, segr_ref, c_ref, s_ref) = refs[
        np_ : np_ + 10
    ]
    out_ref, do_s, dk_s, dv_s, dq_s = refs[np_ + 10 :]
    me = me_ref[0]
    for (m, off, rows), br in zip(pieces, brs):
        y = nt(br[...], w_ref[...])
        low = iota((rows, 128), 1) < 64
        lo = jnp.where(low, y, 0.0).astype(BF)
        hi = jnp.where(low, 0.0, y).astype(BF)
        for a, cnt, dst in geo.places(me, m, off, rows):
            do_s[0, pl.ds(dst, cnt), :] = lo[a : a + cnt, :]
            do_s[1, pl.ds(dst, cnt), :] = hi[a : a + cnt, :]
    dk_s[...] = jnp.zeros_like(dk_s)
    dv_s[...] = jnp.zeros_like(dv_s)

    def head(i, carry):
        g = 0
        for q0, keys in geo.tiles():
            q = q_ref[i, q0 : q0 + TILE, :]
            do = do_s[i, q0 : q0 + TILE, :]
            lse = lse_ref[i, :, q0 : q0 + TILE]
            ps, dps = [], []
            delta = None
            for k0, kn, kind in keys:
                s = masked(nt(kd_ref[g, k0 : k0 + kn, :], q), kind, q0, k0, segc_ref, segr_ref)
                p = jnp.exp(s - lse)
                dp = nt(vd_ref[g, k0 : k0 + kn, :], do)
                dv_s[g, k0 : k0 + kn, :] += nn(p.astype(BF), do)
                d = jnp.sum(p * dp, axis=0, keepdims=True)
                delta = d if delta is None else delta + d
                ps.append(p)
                dps.append(dp)
            acc = None
            for p, dp, (k0, kn, kind) in zip(ps, dps, keys):
                ds = (p * (dp - delta)).astype(BF)
                dk_s[g, k0 : k0 + kn, :] += nn(ds, q)
                part = nn(kt_ref[g, :, k0 : k0 + kn], ds)
                acc = part if acc is None else acc + part
            dq_s[i, :, q0 : q0 + TILE] = acc
        return carry

    lax.fori_loop(0, 2, head, 0)
    low = iota((TILE, 128), 1) < 64
    for t in range(0, geo.TG, TILE):
        rows = slice(t, t + TILE)
        cos, sin = c_ref[rows, :], s_ref[rows, :]
        v = jnp.concatenate([dq_s[0, :, rows], dq_s[1, :, rows]], axis=0).T * 0.125
        dq = v * cos - swap_halves(v) * sin
        k = dk_s[0, rows, :]
        k = k + pltpu.roll(k, 64, 1)
        k = k * cos - swap_halves(k) * sin
        v = dv_s[0, rows, :]
        for x, col in enumerate((dq, jnp.where(low, k, v + pltpu.roll(v, 64, 1)))):
            y = col.astype(BF)
            for a, cnt, dst in geo.spread(me, t):
                out_ref[pl.ds(dst, cnt), x * 128 : x * 128 + 128] = y[a : a + cnt, :]


def mix_kernel(T, act_ref, w_ref, *refs):
    outs, acc = refs[:-1], refs[-1]
    i = pl.program_id(0)
    v = nn(act_ref[...], w_ref[0])

    @pl.when(i == 0)
    def _():
        acc[...] = v

    @pl.when(i > 0)
    def _():
        acc[...] += v

    @pl.when(i == pl.num_programs(0) - 1)
    def _():
        put_blocks(T, acc, outs)


def mix_parts(n, T, rows, act, wd):
    E, M, D = wd.shape
    return call(
        functools.partial(mix_kernel, T),
        (shape((T, D), F32),) + tuple(shape((v, D), BF) for v in rows[1:]),
        2 * n * T * E * M * D,
        10e6,
        grid=(E,),
        in_specs=[
            pl.BlockSpec((n * T, M), lambda i: (0, i)),
            pl.BlockSpec((1, M, D), lambda i: (i, 0, 0)),
        ],
        out_specs=tuple(pl.BlockSpec((v, D), lambda i: (0, 0)) for v in rows),
        scratch_shapes=[pltpu.VMEM((n * T, D), F32)],
        name="mix",
    )(act, wd)


def back_kernel(T, G, w_ref, *refs):
    ys, outs = refs[:G], refs[G:]
    at = 0
    for out in outs:
        rows = out.shape[0]
        v = None
        for g, y in enumerate(ys):
            p = nt(y[at : at + rows, :], w_ref[:, g * 256 : (g + 1) * 256])
            v = p if v is None else v + p
        out[...] = v.astype(BF)
        at += rows


def head_grad_kernel(geo, first, s_ref, x_ref, y_ref, w_ref, gf_ref, *outs):
    me = s_ref[1]
    r = w_ref.shape[0] // geo.n
    ones = jnp.ones((16, 256), BF)
    row = iota((16, 256), 0)
    for j in range(geo.n):
        dw = tn(x_ref[:, j * r : (j + 1) * r], y_ref[...])
        prod = dw * w_ref[j * r : (j + 1) * r, :].astype(F32)
        hi = prod.astype(BF)
        lo = (prod - hi.astype(F32)).astype(BF)
        gain = nt(ones, hi) + nt(ones, lo)
        below = gf_ref[:, j * r : (j + 1) * r] if first else jnp.zeros((1, r), F32)
        if r < 256:
            gain = jnp.concatenate([gain, jnp.zeros((16, 256 - r), F32)], axis=1)
            below = jnp.concatenate([below, jnp.zeros((1, 256 - r), F32)], axis=1)
        extra = jnp.where(row == 0, gain, jnp.where(row == 1, below, 0.0)).astype(BF)
        low = dw.astype(BF)
        for m, out in enumerate(outs):

            @pl.when((me ^ m) == j)
            def _():
                out[:r, :] = low
                out[r:, :] = extra


def out_grad_kernel(np_, G, s_ref, *refs):
    brs, atts = refs[:np_], refs[np_ : np_ + G]
    send, keep = refs[np_ + G], refs[np_ + G + 1]
    per = []
    for o in atts:
        v, at_ = None, 0
        for br in brs:
            rows = br.shape[0]
            p = tn(o[at_ : at_ + rows, :], br[...])
            v = p if v is None else v + p
            at_ += rows
        per.append(v)
    v = jnp.concatenate(per, axis=0).astype(BF)
    lead, rows = send.shape[0], send.shape[1]
    half = v.shape[0] // 2
    count = rows // half

    def put(out, top):
        for a in range(lead):
            for b in range(count):
                c = (a * count + b) * 256
                out[a, b * half : (b + 1) * half, :] = v[top : top + half, c : c + 256]

    @pl.when(s_ref[0] == 0)
    def _():
        put(keep, 0)
        put(send, half)

    @pl.when(s_ref[0] == 1)
    def _():
        put(keep, half)
        put(send, 0)


def combine_kernel(ops, wide, k, *refs):
    end = (refs[0][0] == 0) | (refs[0][0] == refs[0][1])
    ins, outs = refs[1 : 1 + k], refs[len(refs) - len(ops) :]

    def plus(a, b):
        return (ins[a][...].astype(F32) + ins[b][...].astype(F32)).astype(BF)

    for (kind, *at), w, out in zip(ops, wide, outs):

        def work():
            if kind == "add":
                out[...] = plus(*at)
                return

            @pl.when(end)
            def _():
                out[...] = plus(*at[:2]) if kind == "merge" else ins[at[0]][...]

            @pl.when(jnp.logical_not(end))
            def _():
                out[...] = plus(*at[2:]) if kind == "merge" else ins[at[1]][...]

        if w:
            work()
        else:
            pl.when((pl.program_id(0) == 0) & (pl.program_id(1) == 0))(work)


def combine(pos, ops):
    arrays, specs, keys, coded, outs, out_specs, wide = [], [], [], [], [], [], []

    def spec(w, block, part):
        if w:
            half = (1, block[0] // 2, block[1])
            return pl.BlockSpec(half, lambda i, h, p: (i, 2 * part + h, 0))
        return pl.BlockSpec(block, lambda i, h, p: (0,) * len(block))

    for kind, args, place in ops:
        a = args[0][0]
        w = a.shape[0] == 3
        block = a.shape[1:] if w else a.shape
        at = []
        for v, part in args:
            key = (id(v), part)
            if key not in keys:
                keys.append(key)
                arrays.append(v)
                specs.append(spec(w, block, part))
            at.append(keys.index(key))
        coded.append((kind, *at))
        wide.append(w)
        if place is None:
            outs.append(shape(a.shape, BF))
            out_specs.append(spec(w, block, 0))
        else:
            outs.append(shape((3, CH * block[0], block[1]), BF))
            out_specs.append(spec(w, block, place[1]))
    k = len(arrays)
    alias = {}
    for i, (_, _, place) in enumerate(ops):
        if place is not None and place[0] is not None:
            alias[1 + len(arrays)] = i
            arrays.append(place[0])
            specs.append(pl.BlockSpec(memory_space=pl.ANY))
    out = call(
        functools.partial(combine_kernel, coded, wide, k),
        tuple(outs),
        1e6,
        1e6,
        grid_spec=pltpu.PrefetchScalarGridSpec(
            num_scalar_prefetch=1,
            grid=(3, 2),
            in_specs=specs,
            out_specs=tuple(out_specs),
        ),
        input_output_aliases=alias,
        name="combine",
    )(pos, *arrays)
    return list(out)


def put_blocks(T, acc, outs, first=0):
    at = first
    for out in outs:
        rows = out.shape[0]
        out[...] = acc[at : at + rows, :].astype(out.dtype)
        at += rows


def finish_kernel(e, first, c_ref, own_ref, sib_ref, *refs):
    g_ref, u_ref, d_ref = refs if first else refs[3:]

    def put(src):
        g_ref[0] = src[0].astype(F32)
        u_ref[0] = src[1].astype(F32)
        d_ref[0] = src[2].astype(F32).T

    @pl.when(pl.program_id(0) < 2)
    def _():
        put(own_ref)

    @pl.when(pl.program_id(0) >= 2)
    def _():
        put(sib_ref)


def finish(e, E, core, own, sib, prev):
    _, Dh, M = own.shape
    rows = Dh // 2
    first = prev is None
    half = lambda s, c: jnp.where(s < 2, 2 * c[0] + s, 2 * (1 - c[0]) + s - 2)
    any_ = pl.BlockSpec(memory_space=pl.ANY)
    return call(
        functools.partial(finish_kernel, e, first),
        (
            shape((E, 2 * Dh, M), F32),
            shape((E, 2 * Dh, M), F32),
            shape((E, M, 2 * Dh), F32),
        ),
        1e6,
        10e6,
        grid_spec=pltpu.PrefetchScalarGridSpec(
            num_scalar_prefetch=1,
            grid=(4,),
            in_specs=[
                pl.BlockSpec((3, rows, M), lambda s, c: (0, jnp.minimum(s, 1), 0)),
                pl.BlockSpec((3, rows, M), lambda s, c: (0, jnp.maximum(s - 2, 0), 0)),
            ]
            + ([] if first else [any_] * 3),
            out_specs=(
                pl.BlockSpec((1, rows, M), lambda s, c: (e, half(s, c), 0)),
                pl.BlockSpec((1, rows, M), lambda s, c: (e, half(s, c), 0)),
                pl.BlockSpec((1, M, rows), lambda s, c: (e, 0, half(s, c))),
            ),
        ),
        input_output_aliases={} if first else {3: 0, 4: 1, 5: 2},
        name=f"finish{e}",
    )(core, own, sib, *([] if first else prev))


def last_kernel(n, r, s_ref, *refs):
    halves = (refs[0:2], refs[2:4])
    gain_ref, ga_ref, q_ref, k_ref, v_ref, o_ref, gf_ref = refs[4:]
    core, me = s_ref[0], s_ref[1]
    lead = n // 2
    low = iota((r, 128), 1) < 64
    ga = jnp.zeros((1, 256), F32)
    gf = jnp.zeros((1, 256), F32)
    for side, pair in enumerate(halves):
        hh = core if side == 0 else 1 - core
        for l in range(lead):
            one, two = pair[0][l, :r, :].astype(F32), pair[1][l, :r, :].astype(F32)
            kv0, kv1 = one[:, 128:], two[:, 128:]
            k = jnp.where(low, kv0, pltpu.roll(kv1, 64, 1))
            v = jnp.where(low, pltpu.roll(kv0, 64, 1), kv1)
            for j in range(n):

                @pl.when((me ^ (hh * lead + l)) == j)
                def _():
                    q_ref[:, j * 256 : j * 256 + 128] = one[:, :128]
                    q_ref[:, j * 256 + 128 : j * 256 + 256] = two[:, :128]
                    k_ref[:, j * 128 : j * 128 + 128] = k
                    v_ref[:, j * 128 : j * 128 + 128] = v

            below = pair[0][l, r : r + 16, :].astype(F32)
            ga = ga + below[:1, :] + pair[1][l, r : r + 16, :].astype(F32)[:1, :]
            gf = gf + below[1:2, :]
            count = (pair[0].shape[1] - r - 16) // (r // 2)
            for b in range(count):
                c = (l * count + b) * 256
                at = r + 16 + b * (r // 2)
                o_ref[pl.ds(pl.multiple_of(hh * (r // 2), 128), r // 2), c : c + 256] = pair[0][
                    l, at : at + r // 2, :
                ].astype(F32)
    ga_ref[...] = ga[:, :r] / gain_ref[...].astype(F32)
    gf_ref[...] = gf[:, :r]


def mixed_kernel(*refs):
    v = refs[0][...]
    for p in refs[1:-1]:
        v = v + p[...].astype(F32)
    refs[-1][...] = v.astype(BF)


def mixed_sum(hidden, parts):
    T, D = hidden.shape
    row = pl.BlockSpec((T // 2, D), lambda i: (i, 0))
    return call(
        mixed_kernel,
        shape((T, D), BF),
        1e6,
        6e6,
        grid=(2,),
        in_specs=[row] * (1 + len(parts)),
        out_specs=row,
        name="mixed",
    )(hidden, *parts)


def per_device(
    tokens,
    d_out,
    routes,
    gates,
    segment,
    gain_attn,
    w_query,
    key_weight,
    value_weight,
    w_out,
    gain_ffn,
    w_gate,
    w_up,
    w_down,
):
    n = lax.axis_size("shard")
    me = lax.axis_index("shard")
    R = lax.axis_size("rep")
    rp = lax.axis_index("rep")
    core, pos = rp % 2, rp // 2
    T, D = tokens.shape
    geo = Geo(n, T, segment.shape[1])
    G, TG = geo.G, geo.TG
    E, _, M = w_gate.shape
    me1 = me.reshape(1).astype(jnp.int32)
    scal = jnp.stack([core, me]).astype(jnp.int32)

    def px(v, m):
        return lax.ppermute(v, "shard", [(i, i ^ m) for i in range(n)])

    def at(v, i):
        return lax.dynamic_index_in_dim(v, i, 0, keepdims=False)

    def near(v):
        return [v] + [px(v, m) for m in ((1, 2) if geo.relay else range(1, n))]

    def far(got):
        if not geo.relay:
            return list(got)
        v, a, b = got
        h = v.shape[0] // 2
        return [v, a, b, px(a[:h], 2), px(b[h:], 1)]

    def hbm(*vals):
        return [pltpu.with_memory_space_constraint(v, pltpu.HBM) for v in vals]

    def tie(vals, deps):
        vals, deps = tuple(vals), tuple(deps)
        return lax.optimization_barrier(vals + deps)[: len(vals)]

    L = R // 2

    def pz(v, pairs):
        return lax.ppermute(v, "rep", [(2 * a + k, 2 * b + k) for a, b in pairs for k in (0, 1)])

    def sib(v):
        return lax.ppermute(v, "rep", [(i, i ^ 1) for i in range(R)])

    pos1 = jnp.stack([pos, jnp.full((), L - 1)]).astype(jnp.int32)
    near_pairs = [(0, 1), (1, 0), (2, 3), (3, 2)]

    class Sums:
        def __init__(self):
            self.live, self.done, self.final = [], {}, {}

        def add(self, tag, keeps, send):
            if L != 4:
                both_ = jnp.stack([jnp.concatenate(keeps, axis=1), send])
                both_ = jnp.where(core == 0, both_, both_[::-1])
                both_ = lax.psum(both_, "rep")
                self.done[tag] = at(both_, core), at(both_, 1 - core)
                return
            new = sib(send)
            for k, keep in enumerate(keeps):
                self.live.append(
                    dict(tag=tag, part=k, parts=len(keeps), step=0, acc=keep, new=new)
                )

        def meet(self, chunks, vals):
            names = [(c, f) for c in chunks for f in ("acc", "new")]
            flat = []
            for c, f in names:
                if not any(c[f] is v for v in flat):
                    flat.append(c[f])
            got = lax.optimization_barrier(tuple(vals) + tuple(flat))
            fresh = got[len(vals) :]
            for c, f in names:
                c[f] = next(b for a, b in zip(flat, fresh) if a is c[f])
            return got[: len(vals)]

        def advance(self, vals, more=(), hold=(), starts=1):
            live = []
            for c in self.live:
                if c["tag"] in hold:
                    continue
                if c["step"] == 0:
                    if not starts:
                        continue
                    starts -= 1
                live.append(c)
            vals = self.meet([c for c in live if c["step"] > 0], vals)
            vals = self.meet(live, (*vals, *more))
            if not live:
                return vals
            ops, then = [], []
            into = [c for c in live if c["step"] == 0]
            out = [c for c in live if c["step"] == 2]

            def arrived(c):
                return [(c["acc"], 0), (c["new"], c["part"] if c["step"] == 0 else 0)]

            pairs = []
            for c in out:
                mate = next((d for d in into if d["acc"].shape == c["acc"].shape), None)
                if mate is not None:
                    into.remove(mate)
                pairs.append((mate, c))
            pairs += [(d, None) for d in into]
            for c in live:
                if c["step"] == 3:
                    whole = self.final.get(c["tag"])
                    place = None if c["parts"] == 1 else (whole, c["part"])
                    ops.append(("take", [(c["new"], 0), (c["acc"], 0)], place))
                    then.append(("done", c))
                elif c["step"] == 1:
                    ops.append(("add", arrived(c), None))
                    then.append(("mid", c))
            for d, c in pairs:
                if c is None:
                    ops.append(("add", arrived(d), None))
                    then.append(("in", d))
                elif d is None:
                    ops.append(("add", arrived(c), None))
                    then.append(("out", c))
                else:
                    ops.append(("add", arrived(d), None))
                    then.append(("acc", d))
                    ops.append(("merge", arrived(d) + arrived(c), None))
                    then.append(("both", d, c))
            res = combine(pos1, ops)
            waiting = [t for t, v in self.done.items() if len(v) == 1]
            got = lax.optimization_barrier(
                vals + tuple(res) + tuple(self.done[t][0] for t in waiting)
            )
            vals, res, old = (
                got[: len(vals)],
                got[len(vals) : len(vals) + len(res)],
                got[len(vals) + len(res) :],
            )
            for t, v in zip(waiting, old):
                self.done[t] = (v,)
            for (what, *cs), v in zip(then, res):
                c = cs[-1]
                if what == "done":
                    self.final[c["tag"]] = v
                    c["step"] = 4
                    if all(o["step"] == 4 or o["tag"] != c["tag"] for o in self.live):
                        self.done[c["tag"]] = (v,)
                elif what == "mid":
                    c.update(step=2, acc=v, new=pz(v, [(1, 2), (2, 1)]))
                elif what == "acc":
                    c.update(acc=v)
                elif what == "in":
                    c.update(step=1, acc=v, new=pz(v, [(0, 1), (3, 2)]))
                elif what == "out":
                    c.update(step=3, acc=v, new=pz(v, [(1, 0), (2, 3)]))
                else:
                    new = pz(v, near_pairs)
                    cs[0].update(step=1, new=new)
                    c.update(step=3, acc=v, new=new)
            self.live = [c for c in self.live if c["step"] < 4]
            return vals

        def with_done(self, vals):
            waiting = [t for t, v in self.done.items() if len(v) == 1]
            got = lax.optimization_barrier(
                tuple(vals) + tuple(self.done[t][0] for t in waiting)
            )
            for t, v in zip(waiting, got[len(vals) :]):
                self.done[t] = (v,)
            return got[: len(vals)]

        def whole(self, tag):
            if len(self.done[tag]) == 1:
                self.done[tag] = (*self.done[tag], sib(*self.done[tag]))
            return self.done[tag]

    sums = Sums()

    def scatter(parts):
        return [parts[0]] + [px(parts[m], m) for m in range(n - 1, 0, -1)]

    r = w_query.shape[0]
    W = G * 256
    segc, segr = segment.reshape(-1, 1), segment
    near_tok = near(tokens)
    wmsg = call(
        functools.partial(columns_kernel, geo),
        (shape((r + 16, W), BF),) * n,
        1e6,
        2e6,
        in_specs=[SM] + [VM] * 5,
        out_specs=(VM,) * n,
        name="columns",
    )(me1, w_query, key_weight, value_weight, gain_attn.reshape(1, r), gain_ffn.reshape(1, r))
    got_w = [wmsg[0]] + [px(wmsg[m], m) for m in range(1, n)]
    dmsg, cos4, sin4 = call(
        pack_kernel,
        (shape((T, D + 128), BF), shape((TG, 128), F32), shape((TG, 128), F32)),
        1e6,
        2e6,
        in_specs=[VM] * 5,
        out_specs=(VM,) * 3,
        name="pack",
    )(d_out, routes, gates, segc, segr)
    wo_own = at(w_out.reshape(2, r // 2, D), core)
    dmsg, cos4, wo_own, *near_tok = tie((dmsg, cos4, wo_own, *near_tok), ())
    tok = far(near_tok)
    near_wo = near(wo_own)
    dmsg, *rest = tie((dmsg, *tok, *near_wo, *got_w), ())
    np_ = len(tok)
    tok, near_wo, got_w = rest[:np_], rest[np_ : -n], rest[-n:]
    near_d = near(dmsg)
    wo_half = far(near_wo)

    normed, q, kd, vd, kt, vt, w_cols, gain_a, gain_f = call(
        functools.partial(qkv_kernel, geo),
        (
            shape((n * T, D), BF),
            shape((2 * G, TG, 128), BF),
            shape((G, TG, 128), BF),
            shape((G, TG, 128), BF),
            shape((G, 64, TG), BF),
            shape((G, 64, TG), BF),
            shape((D, W), BF),
            shape((1, D), F32),
            shape((1, D), F32),
        ),
        2 * TG * D * W,
        12e6,
        in_specs=[SM] + [VM] * (np_ + n + 2),
        out_specs=(VM,) * 9,
        scratch_shapes=[pltpu.VMEM((TG, W), F32)],
        name="qkv",
    )(me1, *tok, *got_w, cos4, sin4)

    atts, lses, own_att = [], [], []
    near_o = None
    for g in range(G):
        o, lse = call(
            functools.partial(att_kernel, geo),
            (shape((n * T, 128), BF), shape((2, 1, TG), F32)),
            1e9,
            3e6,
            2 * TG * TG * 0.6,
            grid=(1,),
            in_specs=[
                SM,
                pl.BlockSpec((2, TG, 128), lambda i, g=g: (g, 0, 0)),
                pl.BlockSpec((1, TG, 128), lambda i, g=g: (g, 0, 0)),
                pl.BlockSpec((1, 64, TG), lambda i, g=g: (g, 0, 0)),
                VM,
                VM,
            ],
            out_specs=(VM, VM),
            name=f"attend{g}",
        )(me1, q, kd, vt, segc, segr)
        own_att.append(o)
        lses.append(lse)
        if g == 0:
            k = len(near_d)
            o, q, *rest = tie((o, q, *near_d, *wo_half), ())
            near_d, wo_half = rest[:k], rest[k:]
            wo_mine = jnp.concatenate(wo_half, axis=0)
            wo_sib = sib(wo_mine)
            near_o = near(o)
        else:
            o, *near_o = tie((o, *near_o), ())
            atts += far(near_o)
            near_o = near(o)
    near_d, near_o = list(near_d), list(near_o)
    wo_mine, wo_sib, *rest = tie((wo_mine, wo_sib, *near_d, *near_o, *atts), ())
    k = len(near_d)
    near_d, near_o, atts = rest[:k], rest[k : k + len(near_o)], rest[k + len(near_o) :]
    atts += far(near_o)
    douts = far(near_d)
    lse = jnp.concatenate(lses, axis=0)

    hidden, x = call(
        functools.partial(hidden_kernel, geo, len(atts)),
        (shape((T, D), F32), shape((n * T, D), BF)),
        2 * TG * D * D,
        16e6,
        in_specs=[SM] + [VM] * (len(atts) + np_ + 3),
        out_specs=(VM,) * 2,
        scratch_shapes=[pltpu.VMEM((D, D), BF)],
        name="hidden",
    )(scal, *atts, *tok, wo_mine, wo_sib, gain_f)
    x, *douts = tie((x, *douts), ())
    dout = jnp.concatenate(douts, axis=0)

    w_gate, w_up, w_down = hbm(w_gate, w_up, w_down)
    early = E // 2
    kept = None
    for e in range(early):
        kept, send, keeps = expert(n, T, E, e, scal, x, dout, w_gate, w_up, w_down, kept)
        kept = hbm(*kept)
        sums.add(e, keeps, send)
        if e == 0:
            x, *kept = sums.advance((x, *kept))
    kept = hbm(*forwards(n, T, E, early, scal, x, dout, w_gate, w_up, w_down, kept))
    (last,) = input_grad(T, E, (n - 1) * T, [T], *kept[1:], w_gate, w_up)
    x, act, gg, ug, last = sums.advance((x, *kept, last))

    def weights(e, x, act, gg, ug):
        send, keeps = weight_grad(M, e, scal, x, dout, act, gg, ug)
        sums.add(e, keeps, send)
        return tie((x, act, gg, ug), (send,))

    far_part = px(last, n - 1)
    x, act, gg, ug = weights(early, x, act, gg, ug)
    if n == 4:
        first = input_grad(T, E, 0, [T] * (n - 1), gg, ug, w_gate, w_up)
    else:
        first = [
            v
            for m in range(n - 1)
            for v in input_grad(T, E, m * T, [T], gg, ug, w_gate, w_up)
        ]
    *first, x, act, gg, ug, far_part = sums.advance((*first, x, act, gg, ug), (far_part,))
    came = [first[0], far_part] + [px(first[m], m) for m in range(n - 2, 0, -1)]
    rest = []
    for e in range(early + 1, E):
        send, keeps = weight_grad(M, e, scal, x, dout, act, gg, ug)
        rest += [send, *keeps]
    k = len(came)
    came = tie((*came, act, *rest), ())
    came, act, rest = came[:k], came[k], came[k + 1 :]
    for e in range(early + 1, E):
        sums.add(e, rest[1 : 1 + CH], rest[0])
        rest = rest[1 + CH :]

    hidden_grad, branch, gain_f_part = norm_back(came, d_out, hidden, gain_f, True)
    (act,) = tie((act,), (branch,))
    branches = near(branch)
    mix = sums.advance(mix_parts(n, T, [T] * n, act, w_down), branches)
    mix, branches = mix[:n], far(mix[n:])

    prev = None
    finished = 0

    def finishing(most):
        nonlocal prev, finished
        while finished < most and finished in sums.done:
            prev = finish(finished, E, scal, *sums.whole(finished), prev)
            finished += 1

    def tie_finished(vals):
        nonlocal prev
        if prev is None:
            return tuple(vals)
        got = lax.optimization_barrier(tuple(vals) + tuple(prev))
        prev = got[-3:]
        return got[:-3]

    finishing(1)
    w_out_ = w_out
    nb = len(branches)
    *branches, q, kd = tie_finished((*branches, q, kd))
    mix = list(tie(mix, branches))
    mix_far = px(mix[n - 1], n - 1)

    def attend_back(g, q, kd):
        return call(
            functools.partial(att_back_kernel, geo, g),
            shape((n * T, 256), BF),
            4e9 / G,
            8e6,
            4 * TG * TG * 0.6 / G,
            grid=(1,),
            in_specs=[SM]
            + [VM] * nb
            + [
                pl.BlockSpec((128, D), lambda i: (g, 0)),
                pl.BlockSpec((2, TG, 128), lambda i: (g, 0, 0)),
                pl.BlockSpec((1, TG, 128), lambda i: (g, 0, 0)),
                pl.BlockSpec((1, 64, TG), lambda i: (g, 0, 0)),
                pl.BlockSpec((1, TG, 128), lambda i: (g, 0, 0)),
                pl.BlockSpec((2, 1, TG), lambda i: (g, 0, 0)),
            ]
            + [VM] * 4,
            out_specs=VM,
            scratch_shapes=[
                pltpu.VMEM((2, TG, 128), BF),
                pltpu.VMEM((1, TG, 128), F32),
                pltpu.VMEM((1, TG, 128), F32),
                pltpu.VMEM((2, 64, TG), F32),
            ],
            name=f"attend_back{g}",
        )(me1, *branches, *hbm(w_out_, q, kd, kt, vd, lse, segc, segr, cos4, sin4))

    def head_grad(g, y):
        return call(
            functools.partial(head_grad_kernel, geo, g == 0),
            (shape((r + 16, 256), BF),) * n,
            1e9,
            4e6,
            grid=(1,),
            in_specs=[
                SM,
                VM,
                VM,
                pl.BlockSpec((D, 256), lambda i: (0, g)),
                VM,
            ],
            out_specs=(VM,) * n,
            name=f"head_grad{g}",
        )(scal, normed, y, w_cols, gain_f_part)

    lead = n // 2
    orows = r // 2 * (D // 256) // lead

    def add_small(g, arrived, out=None):
        got = jnp.stack(arrived).reshape(2, lead, r + 16, 256)
        keep, send = at(got, core), at(got, 1 - core)
        if out is not None:
            keep = jnp.concatenate([keep, out[1]], axis=1)
            send = jnp.concatenate([send, out[0]], axis=1)
        sums.add(("small", g), [keep], send)

    out = call(
        functools.partial(out_grad_kernel, nb, G),
        (shape((lead, orows, 256), BF),) * 2,
        1e9,
        4e6,
        in_specs=[SM] + [VM] * (nb + G),
        out_specs=(VM, VM),
        name="out_grad",
    )(scal, *branches, *own_att)
    ys = [attend_back(0, q, kd)]
    msgs = head_grad(0, ys[0])
    q, kd, *got, mix_far = sums.advance((q, kd, *msgs, *out), (mix_far,))
    msgs, out = got[:n], got[n:]
    arrived = [msgs[0]] + [px(msgs[m], m) for m in range(1, n)]
    if G == 2:
        ys.append(attend_back(1, q, kd))
    got = tie((*ys, *arrived), ())
    ys, arrived = got[:G], got[G:]
    add_small(0, arrived, out)
    arrived = []
    if G == 2:
        msgs = head_grad(1, ys[1])
        ys = tie(ys, msgs[:1])
        arrived = [msgs[0]] + [px(msgs[m], m) for m in range(1, n)]
    back = call(
        functools.partial(back_kernel, T, G),
        (shape((T, D), BF),) * n,
        1e9,
        8e6,
        in_specs=[VM] * (1 + G),
        out_specs=(VM,) * n,
        name="back",
    )(w_cols, *ys)
    came = scatter(back)
    came[0], *arrived = sums.advance(came[:1], arrived)
    if G == 2:
        add_small(1, arrived)
    k = len(came)
    got = sums.advance((), (*came, *mix))
    came, mix = got[:k], got[k:]
    mix = [mix[0], mix_far] + [px(mix[m], m) for m in range(n - 2, 0, -1)]
    (d_tokens,) = norm_back(came, hidden_grad, tokens, gain_a, False)
    finishing(E // 2)
    (d_tokens,) = tie_finished((d_tokens,))
    (d_tokens,) = sums.advance((d_tokens,))
    finishing(E)
    (d_tokens,) = tie_finished((d_tokens,))
    d_tokens, *mix = sums.advance((d_tokens,), mix)
    mixed = mixed_sum(hidden, mix)
    while sums.live:
        (d_tokens,) = sums.advance((d_tokens,))
    finishing(E)
    g_gate, g_up, g_down = prev

    if G == 2:
        one, two = sums.whole(("small", 0)), sums.whole(("small", 1))
        g_ga, g_q, g_k, g_v, g_out_all, g_gf = call(
            functools.partial(last_kernel, n, r),
            (
                shape((1, r), F32),
                shape((r, QUERY_HEADS * HEAD), F32),
                shape((r, KEY_VALUE_HEADS * HEAD), F32),
                shape((r, KEY_VALUE_HEADS * HEAD), F32),
                shape((r, D), F32),
                shape((1, r), F32),
            ),
            1e6,
            5e6,
            in_specs=[SM] + [VM] * 5,
            out_specs=(VM,) * 6,
            name="last",
        )(scal, one[0], two[0], one[1], two[1], gain_attn.reshape(1, r))
        g_ga, g_gf = g_ga.reshape(r), g_gf.reshape(r)
    else:
        v, other = sums.whole(("small", 0))
        v = jnp.where(core == 0, jnp.stack([v, other]), jnp.stack([other, v])).astype(F32)
        g_out_all = v[:, :, r + 16 :, :].reshape(2, D // 256, r // 2, 256)
        g_out_all = g_out_all.transpose(0, 2, 1, 3).reshape(r, D)
        v = v[:, :, : r + 16].reshape(n, r + 16, 256)
        in_order = [at(v, me ^ j)[:r] for j in range(n)]
        g_q, g_k, g_v = [
            jnp.concatenate([b[:, lo:hi] for b in in_order], axis=1)
            for lo, hi in ((0, 128), (128, 192), (192, 256))
        ]
        g_ga = jnp.sum(v[:, r, :r], axis=0) / gain_attn.astype(F32)
        g_gf = jnp.sum(v[:, r + 1, :r], axis=0)
    return (mixed, d_tokens, g_ga, g_q, g_k, g_v, g_out_all, g_gf, g_gate, g_up, g_down)


def solution(mesh):
    rows = P(("rep", "shard"), None)
    own = P("shard", None)
    own3 = P("shard", None, None)
    vec = P("shard")
    return jax.shard_map(
        per_device,
        mesh=mesh,
        in_specs=(
            rows,
            rows,
            rows,
            rows,
            P("rep", None),
            vec,
            own,
            own,
            own,
            own,
            vec,
            own3,
            own3,
            own3,
        ),
        out_specs=(rows, rows, vec, own, own, own, own, vec, own3, own3, own3),
        check_vma=False,
    )
```
